32 devices in a mesh: fsdp: 16 (over z, x, core), seq: 2 (over y).
Axes of the slice: x: 2, y: 2, z: 4, core: 2. Of those that a mesh axis runs over, the one named last changes fastest.
Arguments:
- queries: bfloat16 [4096, 3072], P(('fsdp', 'seq')), may hold values from -1000 to 1000
- keys: bfloat16 [4096, 3072], P(('fsdp', 'seq')), may hold values from -1000 to 1000
- values: bfloat16 [4096, 3072], P(('fsdp', 'seq')), may hold values from -6 to 6
- image_ids: int32 [16, 256], P('fsdp'), may hold values from 0 to 15, never falling along the last dimension, each value on 1 to 128 neighbouring positions
- q_gain: float32 [128], replicated, may hold values from 0.6 to 6
- k_gain: float32 [128], replicated, may hold values from 0.6 to 6
- w_out: bfloat16 [3072, 6144], P('fsdp', 'seq'), may hold values from -0.109375 to 0.109375
- grad_y: bfloat16 [4096, 6144], P('fsdp', 'seq'), may hold values from -6 to 6
Outputs:
- grad_queries: bfloat16 [4096, 24, 128], P('fsdp', 'seq')
- grad_keys: bfloat16 [4096, 24, 128], P('fsdp', 'seq')
- grad_values: bfloat16 [4096, 24, 128], P('fsdp', 'seq')
- grad_w: float32 [3072, 6144], P('fsdp', 'seq')
The draws below stay inside these ranges and needn't reach their ends.
All inputs are finite; a program needn't handle non-finite values.
Results may differ from the reference program's by a relative error of at most 0.02.
The reference program's roundings to bfloat16 on the way count: a program that leaves them out, or rounds other values in their place, can miss the bound.
Values may be sent and summed in bfloat16 or wider, within the bound.
No kernel may reach another device: no remote copies, remote signals or barrier semaphores. Data moves between devices by JAX's collectives and lax.ppermute only.
A program may use at most 128 MiB of HBM per device.

```python
import math
import jax
import jax.numpy as jnp
import numpy as np
from jax import lax

D = 6144
HEADS = 24
HEAD_DIM = 128
IMAGES = 16
SEQ_LEN = 256
GROUPS = 16
TOKENS = 4096
N_SEQ = 2


def pair_fields(key):
    base = jax.random.fold_in(key, 101)
    parts = jax.random.split(base, 6)
    width = HEADS * HEAD_DIM
    span = math.log(10.0)
    col_q = jnp.exp(jax.random.uniform(parts[0], (1, width), minval=0.0, maxval=span))
    col_k = jnp.exp(jax.random.uniform(parts[1], (1, width), minval=0.0, maxval=span))
    row_q = jnp.exp(jax.random.uniform(parts[2], (TOKENS, 1), minval=0.0, maxval=span))
    row_k = jnp.exp(jax.random.uniform(parts[3], (TOKENS, 1), minval=0.0, maxval=span))
    raw_q = jnp.clip(jax.random.normal(parts[4], (TOKENS, width)), -6.0, 6.0)
    raw_k = jnp.clip(jax.random.normal(parts[5], (TOKENS, width)), -6.0, 6.0)
    keys_out = raw_k * col_k * row_k
    queries_out = raw_q * col_q * row_q
    return (queries_out, keys_out)


def draw_queries(key, part):
    return pair_fields(key)[0].astype(jnp.bfloat16)


def draw_keys(key, part):
    return pair_fields(key)[1].astype(jnp.bfloat16)


def draw_q_gain(key, part):
    inner = jax.random.fold_in(key, 202)
    return jax.random.uniform(inner, (HEAD_DIM,), minval=0.6, maxval=1.8)


def draw_k_gain(key, part):
    inner = jax.random.fold_in(key, 303)
    return jax.random.uniform(inner, (HEAD_DIM,), minval=0.6, maxval=1.8)


def steps_of(rng, shape, cuts, least, high):
    def one(dim, blocks):
        draws = jax.random.uniform(jax.random.fold_in(jax.random.fold_in(rng, 6), dim), (blocks,), jnp.float32, least / len(cuts), high / len(cuts))
        return jnp.repeat(jnp.exp(draws), shape[dim] // blocks).reshape((-1,) + (1,) * (len(shape) - dim - 1))

    level = one(*cuts[0])
    for cut in cuts[1:]:
        level = level * one(*cut)
    return level


def length_profile(amount, total, reach, lean):
    weights = [(1 << 20) // math.isqrt(grade ** lean) + 1 for grade in range(2, amount + 1)]
    surplus, counts = total - reach - (amount - 1), [1] * (amount - 1)
    while surplus > 0:
        movable = [i for i in range(amount - 1) if counts[i] < reach]
        whole, remaining = sum([weights[i] for i in movable]), surplus
        for i in movable:
            addition = min(reach - counts[i], max(1, remaining * weights[i] // whole), surplus)
            counts[i] = counts[i] + addition
            surplus = surplus - addition
    return np.array([reach] + counts)


def ragged(stream_key, count, total, most, lean):
    if count == 2:
        one = jax.random.randint(stream_key, (), max(1, total - most), min(most, total - 1) + 1)
        return jnp.stack([one, total - one])
    sizes = jnp.asarray(length_profile(count, total, most, lean), jnp.int32)
    twos = (count - 1) // 2
    donor, taker = sizes[1:1 + 2 * twos:2], sizes[2:2 + 2 * twos:2]
    slack = jnp.minimum(donor - 1, most - taker)
    shifted = jax.random.randint(jax.random.fold_in(stream_key, 1), (twos,), 0, 1 << 20) % (slack + 1)
    sizes = sizes.at[1:1 + 2 * twos:2].set(donor - shifted).at[2:2 + 2 * twos:2].set(taker + shifted)
    return sizes[jax.random.permutation(jax.random.fold_in(stream_key, 2), count)]


def normal_values(rng, dims, scale, most, cuts=(), dtype=jnp.bfloat16):
    array = jax.random.normal(rng, dims, jnp.float32) * scale
    if len(cuts) > 0:
        array = steps_of(rng, dims, cuts, -0.22, 0.18) * array
    return jnp.clip(array, min=-most, max=most).astype(dtype)


def setup_inputs(seed: int = 0) -> dict:
    streams_of = jax.random.split(jax.random.key(seed), 9)
    queries = draw_queries(jax.random.fold_in(streams_of[8], 71), 0)
    keys = draw_keys(jax.random.fold_in(streams_of[8], 71), 0)
    values = normal_values(streams_of[2], (TOKENS, HEADS * HEAD_DIM), 1.0, 6.0, ((0, 32),))
    image_ids = jax.vmap(lambda own: jnp.searchsorted(jnp.cumsum(ragged(own, IMAGES, SEQ_LEN, SEQ_LEN // 2, 2)), jnp.arange(SEQ_LEN), side="right"))(jax.random.split(streams_of[3], GROUPS)).reshape((GROUPS, SEQ_LEN)).astype(jnp.int32)
    q_gain = draw_q_gain(jax.random.fold_in(streams_of[8], 71), 0)
    k_gain = draw_k_gain(jax.random.fold_in(streams_of[8], 71), 0)
    w_out = normal_values(streams_of[6], (HEADS * HEAD_DIM, D), (HEADS * HEAD_DIM) ** -0.5, 0.109375, ((0, 16), (1, 2)))
    grad_y = normal_values(streams_of[7], (TOKENS, D), 1.0, 6.0, ((0, 16), (1, 2)))
    return {"queries": queries, "keys": keys, "values": values, "image_ids": image_ids, "q_gain": q_gain, "k_gain": k_gain, "w_out": w_out, "grad_y": grad_y}


def norm_parts(source, gain):
    wide = source.astype(jnp.float32)
    centred = wide - lax.optimization_barrier(jnp.mean(wide, axis=-1, keepdims=True))
    scale_inv = lax.rsqrt(lax.optimization_barrier(jnp.mean(centred * centred, axis=-1, keepdims=True)) + 1e-06)
    x_hat = centred * scale_inv
    return (x_hat, scale_inv, (x_hat * gain).astype(jnp.bfloat16))

def norm_back(grad_n, x_hat, scale_inv, gain):
    scaled = grad_n * gain
    return scale_inv * (scaled - lax.optimization_barrier(jnp.mean(scaled, axis=-1, keepdims=True)) - x_hat * lax.optimization_barrier(jnp.mean(scaled * x_hat, axis=-1, keepdims=True)))

def reference(queries, keys, values, image_ids, q_gain, k_gain, w_out, grad_y):
    scale_factor = HEAD_DIM ** (-0.5)
    width = D // N_SEQ
    grad_sum = jnp.zeros((TOKENS, HEADS * HEAD_DIM), jnp.float32)
    for column in range(N_SEQ):
        block = jnp.dot(grad_y[:, column * width:(column + 1) * width], w_out[:, column * width:(column + 1) * width].T, preferred_element_type=jnp.float32)
        block = lax.optimization_barrier(block.astype(jnp.bfloat16))
        grad_sum = grad_sum + block.astype(jnp.float32)
    attention_gradient = grad_sum.astype(jnp.bfloat16)

    def shaped(source):
        return source.reshape(GROUPS, SEQ_LEN, HEADS, HEAD_DIM).transpose(0, 2, 1, 3)

    def group_pass(packed):
        q_group, k_group, v_group, d_group, image_row = packed
        same_image = image_row[:, None] == image_row[None, :]

        def head_pass(inner):
            q_head, k_head, v_head, d_head = inner
            q_hat, q_inv, normalized_queries = norm_parts(q_head, q_gain)
            k_hat, k_inv, normalized_keys = norm_parts(k_head, k_gain)
            scores = jnp.dot(normalized_queries, normalized_keys.T, preferred_element_type=jnp.float32) * scale_factor
            scores = jnp.where(same_image, scores, -1e+30)
            row_top = lax.optimization_barrier(jnp.max(scores, axis=-1, keepdims=True))
            exp_terms = jnp.exp(scores - row_top)
            prob_rows = exp_terms / lax.optimization_barrier(jnp.sum(exp_terms, axis=-1, keepdims=True))
            probs_reduced_precision = prob_rows.astype(jnp.bfloat16)
            attended = jnp.dot(probs_reduced_precision, v_head, preferred_element_type=jnp.float32).astype(jnp.bfloat16)
            grad_v = jnp.dot(probs_reduced_precision.T, d_head, preferred_element_type=jnp.float32).astype(jnp.bfloat16)
            probability_gradient = jnp.dot(d_head, v_head.T, preferred_element_type=jnp.float32)
            row_delta = lax.optimization_barrier(jnp.sum(prob_rows * probability_gradient, axis=-1, keepdims=True))
            score_gradient = (prob_rows * (probability_gradient - row_delta) * scale_factor).astype(jnp.bfloat16)
            normed_query_gradient = jnp.dot(score_gradient, normalized_keys, preferred_element_type=jnp.float32)
            normed_key_gradient = jnp.dot(score_gradient.T, normalized_queries, preferred_element_type=jnp.float32)
            grad_q = norm_back(normed_query_gradient, q_hat, q_inv, q_gain).astype(jnp.bfloat16)
            grad_k = norm_back(normed_key_gradient, k_hat, k_inv, k_gain).astype(jnp.bfloat16)
            return (attended, grad_q, grad_k, grad_v)
        return lax.map(head_pass, (q_group, k_group, v_group, d_group))
    attended, grad_q, grad_k, grad_v = lax.map(group_pass, (shaped(queries), shaped(keys), shaped(values), shaped(attention_gradient), image_ids))

    def unshaped(source):
        return source.transpose(0, 2, 1, 3).reshape(TOKENS, HEADS, HEAD_DIM)
    attended_flat = unshaped(attended).reshape(TOKENS, HEADS * HEAD_DIM)
    grad_w = jnp.dot(attended_flat.T, grad_y, preferred_element_type=jnp.float32) * SEQ_LEN ** (-0.5)
    return (unshaped(grad_q), unshaped(grad_k), unshaped(grad_v), grad_w)
```

```python
import functools

import jax
import jax.numpy as jnp
from jax import lax
from jax.experimental import pallas as pl
from jax.experimental.pallas import tpu as pltpu
from jax.sharding import PartitionSpec as P

F32 = jnp.float32
BF16 = jnp.bfloat16


def norm_parts(source, gain):
    wide = source.astype(jnp.float32)
    centred = wide - jnp.mean(wide, axis=-1, keepdims=True)
    scale_inv = lax.rsqrt(jnp.mean(centred * centred, axis=-1, keepdims=True) + 1e-06)
    x_hat = centred * scale_inv
    return (x_hat, scale_inv, (x_hat * gain).astype(jnp.bfloat16))


def norm_back(grad_n, x_hat, scale_inv, gain):
    scaled = grad_n * gain
    return scale_inv * (
        scaled
        - jnp.mean(scaled, axis=-1, keepdims=True)
        - x_hat * jnp.mean(scaled * x_hat, axis=-1, keepdims=True)
    )


def probabilities(normalized_queries, normalized_keys, same_image, scale_factor):
    scores = (
        jnp.einsum(
            "krt,irt->rki", normalized_queries, normalized_keys, preferred_element_type=jnp.float32
        )
        * scale_factor
    )
    scores = jnp.where(same_image[None], scores, -1e30)
    row_top = jnp.max(scores, axis=-1, keepdims=True)
    exp_terms = jnp.exp(scores - row_top)
    return exp_terms / jnp.sum(exp_terms, axis=-1, keepdims=True)


def local_any(queries, keys, values, image_ids, q_gain, k_gain, w_out, grad_y):
    head_dim = q_gain.shape[0]
    tok_rows = queries.shape[0]
    heads_all = queries.shape[1] // head_dim
    scale_factor = head_dim ** (-0.5)
    q_patch = queries.reshape(tok_rows, heads_all, head_dim)
    k_patch = keys.reshape(tok_rows, heads_all, head_dim)
    v_patch = values.reshape(tok_rows, heads_all, head_dim)
    q_local, k_local, value_shard = (
        lax.all_to_all(q_patch, "seq", split_axis=1, concat_axis=0, tiled=True),
        lax.all_to_all(k_patch, "seq", split_axis=1, concat_axis=0, tiled=True),
        lax.all_to_all(v_patch, "seq", split_axis=1, concat_axis=0, tiled=True),
    )
    seq_length = q_local.shape[0]
    local_heads = q_local.shape[1]
    image_row = image_ids[0]
    same_image = image_row[:, None] == image_row[None, :]
    q_hat, q_inv, normalized_queries = norm_parts(q_local, q_gain)
    k_hat, k_inv, normalized_keys = norm_parts(k_local, k_gain)
    prob_rows = probabilities(normalized_queries, normalized_keys, same_image, scale_factor)
    probs_reduced_precision = prob_rows.astype(jnp.bfloat16)
    attended = jnp.einsum(
        "tgi,itp->gtp", probs_reduced_precision, value_shard, preferred_element_type=jnp.float32
    ).astype(jnp.bfloat16)
    attended_flat = attended.reshape(seq_length, local_heads * head_dim)
    partial_g = jnp.einsum(
        "ld,cd->lc",
        grad_y,
        lax.all_gather(w_out, "fsdp", axis=0, tiled=True),
        preferred_element_type=jnp.float32,
    )
    grad_sum = lax.psum_scatter(
        partial_g.astype(jnp.bfloat16), "seq", scatter_dimension=1, tiled=True
    )
    attention_gradient = grad_sum.reshape(seq_length, local_heads, head_dim)
    grad_values = jnp.einsum(
        "jpw,pjy->wjy",
        probs_reduced_precision,
        attention_gradient,
        preferred_element_type=jnp.float32,
    ).astype(jnp.bfloat16)
    probability_gradient = jnp.einsum(
        "krt,irt->rki", attention_gradient, value_shard, preferred_element_type=jnp.float32
    )
    row_delta = jnp.sum(prob_rows * probability_gradient, axis=-1, keepdims=True)
    score_gradient = (prob_rows * (probability_gradient - row_delta) * scale_factor).astype(
        jnp.bfloat16
    )
    normed_query_gradient = jnp.einsum(
        "tgi,itp->gtp", score_gradient, normalized_keys, preferred_element_type=jnp.float32
    )
    normed_key_gradient = jnp.einsum(
        "jpw,pjy->wjy", score_gradient, normalized_queries, preferred_element_type=jnp.float32
    )
    grad_queries = norm_back(normed_query_gradient, q_hat, q_inv, q_gain).astype(jnp.bfloat16)
    grad_keys = norm_back(normed_key_gradient, k_hat, k_inv, k_gain).astype(jnp.bfloat16)
    partial_w = jnp.einsum(
        "lc,ld->cd",
        lax.all_gather(attended_flat, "seq", axis=1, tiled=True),
        grad_y,
        preferred_element_type=jnp.float32,
    )
    summed = lax.psum_scatter(partial_w, "fsdp", scatter_dimension=0, tiled=True)
    grad_w = summed * seq_length ** (-0.5)
    return (grad_queries, grad_keys, grad_values, grad_w)


def dot_nt(a, b):
    return lax.dot_general(a, b, (((1,), (1,)), ((), ())), preferred_element_type=F32)


def dot_tn(a, b):
    return lax.dot_general(a, b, (((0,), (0,)), ((), ())), preferred_element_type=F32)


def dot_nn(a, b):
    return jnp.dot(a, b, preferred_element_type=F32)


def assemble(first, own, came):
    return jnp.concatenate([jnp.where(first, own, came), jnp.where(first, came, own)], axis=0)


def head_inputs(place, refs, h, dim):
    q_ref, k_ref, v_ref, came_ref = refs
    first = place[0] == 0
    cols = slice(h * dim, (h + 1) * dim)
    return [
        assemble(first, ref[:, cols], came_ref[n, :, cols])
        for n, ref in enumerate((q_ref, k_ref, v_ref))
    ]


def head_probs(q, k, qg, kg, same, scale):
    q_hat, q_inv, qn = norm_parts(q, qg)
    k_hat, k_inv, kn = norm_parts(k, kg)
    scores = jnp.where(same, dot_nt(qn, kn) * scale, -1e30)
    exp_terms = jnp.exp(scores - jnp.max(scores, axis=-1, keepdims=True))
    probs = exp_terms / jnp.sum(exp_terms, axis=-1, keepdims=True)
    return probs, q_hat, q_inv, qn, k_hat, k_inv, kn


def forward_kernel(per, dim, place, q_ref, k_ref, v_ref, came_ref, row_ref, col_ref, qg_ref, kg_ref, even_ref, odd_ref):
    same = col_ref[...] == row_ref[...]
    done = []
    for h in range(per):
        q, k, v = head_inputs(place, (q_ref, k_ref, v_ref, came_ref), h, dim)
        probs = head_probs(q, k, qg_ref[...], kg_ref[...], same, dim**-0.5)[0]
        done.append(dot_nn(probs.astype(BF16), v).T.astype(BF16))
    att = jnp.concatenate(done, axis=0)
    half = att.shape[0] // 2
    straight = (place[1] & 1) == 0
    low, high = att[:half], att[half:]
    even_ref[0] = jnp.where(straight, low, high)
    odd_ref[0] = jnp.where(straight, high, low)


def backward_kernel(per, dim, place, q_ref, k_ref, v_ref, came_ref, d_ref, row_ref, col_ref, qg_ref, kg_ref, gq_ref, gk_ref, gv_ref):
    same = col_ref[...] == row_ref[...]
    scale = dim**-0.5
    straight = (place[1] & 1) == 0
    one, two = d_ref[0, 0], d_ref[0, 1]
    grad = jnp.concatenate([jnp.where(straight, one, two), jnp.where(straight, two, one)], axis=0)
    qg, kg = qg_ref[...], kg_ref[...]
    for h in range(per):
        q, k, v = head_inputs(place, (q_ref, k_ref, v_ref, came_ref), h, dim)
        probs, q_hat, q_inv, qn, k_hat, k_inv, kn = head_probs(q, k, qg, kg, same, scale)
        d = grad[h * dim : (h + 1) * dim].T
        gv = dot_tn(probs.astype(BF16), d)
        gp = dot_nt(d, v)
        delta = jnp.sum(probs * gp, axis=-1, keepdims=True)
        gs = (probs * (gp - delta) * scale).astype(BF16)
        cols = slice(h * dim, (h + 1) * dim)
        gq_ref[:, cols] = norm_back(dot_nn(gs, kn), q_hat, q_inv, qg).astype(BF16)
        gk_ref[:, cols] = norm_back(dot_tn(gs, qn), k_hat, k_inv, kg).astype(BF16)
        gv_ref[:, cols] = gv.astype(BF16)


def attention_specs(per, dim, half_tokens, steps):
    width = per * dim
    own = pl.BlockSpec((half_tokens, width), lambda i, p: (0, p[0] * steps + i))
    came = pl.BlockSpec((3, half_tokens, width), lambda i, p: (0, 0, i))
    return [own, own, own, came]


def whole(shape):
    return pl.BlockSpec(shape, lambda *_: (0,) * len(shape))


def pair_index(i, p):
    return i ^ (p[1] >> 1) ^ (p[2] << 1)


def attention_forward(place, queries, keys, values, came, row, col, qg, kg):
    dim = qg.shape[1]
    half_tokens, heads = queries.shape[0], came.shape[2] // dim
    tokens, per = 2 * half_tokens, heads // 4
    rows = per * dim // 2
    out = pl.BlockSpec((1, rows, tokens), lambda i, p: (pair_index(i, p), 0, 0))
    return pl.pallas_call(
        functools.partial(forward_kernel, per, dim),
        grid_spec=pltpu.PrefetchScalarGridSpec(
            num_scalar_prefetch=1,
            grid=(4,),
            in_specs=attention_specs(per, dim, half_tokens, 4)
            + [whole((1, tokens)), whole((tokens, 1)), whole((1, dim)), whole((1, dim))],
            out_specs=[out, out],
        ),
        out_shape=[jax.ShapeDtypeStruct((4, rows, tokens), BF16)] * 2,
        compiler_params=pltpu.CompilerParams(vmem_limit_bytes=40 << 20),
        cost_estimate=pl.CostEstimate(flops=4 * tokens * tokens * dim * heads, bytes_accessed=6 * tokens * heads * dim, transcendentals=tokens * tokens * heads),
        name="attention_forward",
    )(place, queries, keys, values, came, row, col, qg, kg)


def attention_backward(place, queries, keys, values, came, grads, row, col, qg, kg):
    dim = qg.shape[1]
    half_tokens, heads = queries.shape[0], came.shape[2] // dim
    tokens, per = 2 * half_tokens, heads // 4
    rows = per * dim // 2
    out = pl.BlockSpec((tokens, per * dim), lambda i, p: (0, i))
    return pl.pallas_call(
        functools.partial(backward_kernel, per, dim),
        grid_spec=pltpu.PrefetchScalarGridSpec(
            num_scalar_prefetch=1,
            grid=(4,),
            in_specs=attention_specs(per, dim, half_tokens, 4)
            + [pl.BlockSpec((1, 2, rows, tokens), lambda i, p: (pair_index(i, p), 0, 0, 0))]
            + [whole((1, tokens)), whole((tokens, 1)), whole((1, dim)), whole((1, dim))],
            out_specs=[out, out, out],
        ),
        out_shape=[jax.ShapeDtypeStruct((tokens, heads * dim), BF16)] * 3,
        compiler_params=pltpu.CompilerParams(vmem_limit_bytes=40 << 20),
        cost_estimate=pl.CostEstimate(flops=12 * tokens * tokens * dim * heads, bytes_accessed=14 * tokens * heads * dim, transcendentals=tokens * tokens * heads),
        name="attention_backward",
    )(place, queries, keys, values, came, grads, row, col, qg, kg)


def products_kernel(place, w_ref, wr_ref, *rest):
    n = (len(rest) - 3) // 1
    g_refs, (keep_ref, send_ref, acc_ref) = rest[:n], rest[n:]
    step = pl.program_id(0)
    rows = w_ref.shape[0]

    @pl.when(step == 0)
    def _():
        acc_ref[...] = jnp.zeros_like(acc_ref)

    for j, g_ref in enumerate(g_refs):
        g = g_ref[...]
        acc_ref[j, :rows] += dot_nt(w_ref[...], g)
        acc_ref[j, rows:] += dot_nt(wr_ref[...], g)

    @pl.when(step == pl.num_programs(0) - 1)
    def _():
        flip = place[2] == 1
        for j in range(n):
            own, other = acc_ref[j, :rows].astype(BF16), acc_ref[j, rows:].astype(BF16)
            keep_ref[j] = jnp.where(flip, other, own)
            send_ref[j] = jnp.where(flip, own, other)


def gradient_products(place, w, wr, blocks, tile=1024):
    rows, depth = w.shape
    tokens = blocks[0].shape[0]
    n = len(blocks)
    out = whole((n, rows, tokens))
    return pl.pallas_call(
        products_kernel,
        grid_spec=pltpu.PrefetchScalarGridSpec(
            num_scalar_prefetch=1,
            grid=(depth // tile,),
            in_specs=[pl.BlockSpec((rows, tile), lambda i, p: (0, i))] * 2
            + [pl.BlockSpec((tokens, tile), lambda i, p: (0, i))] * n,
            out_specs=[out, out],
            scratch_shapes=[pltpu.VMEM((n, 2 * rows, tokens), F32)],
        ),
        out_shape=[jax.ShapeDtypeStruct((n, rows, tokens), BF16)] * 2,
        compiler_params=pltpu.CompilerParams(vmem_limit_bytes=40 << 20),
        cost_estimate=pl.CostEstimate(flops=4 * n * rows * tokens * depth, bytes_accessed=2 * (2 * rows + n * tokens) * depth, transcendentals=0),
        name="gradient_products",
    )(place, w, wr, *blocks)


def weight_kernel(pick, place, *refs):
    n = (len(refs) - 1) // 4
    own_refs, other_refs, g_refs, out_ref = refs[:n], refs[n : 2 * n], refs[2 * n : 4 * n], refs[4 * n]
    use_own = place[2] == pick
    total = None
    for j in range(n):
        for c in range(2):
            att = jnp.where(use_own, own_refs[j][c], other_refs[j][c])
            term = dot_nn(att, g_refs[2 * j + c][...])
            total = term if total is None else total + term
    out_ref[...] = total.astype(out_ref.dtype)


def weight_terms(pick, place, own, other, blocks, dtype, tile=512):
    rows, tokens = own[0].shape[1:]
    depth = blocks[0].shape[1]
    n = len(own)
    return pl.pallas_call(
        functools.partial(weight_kernel, pick),
        grid_spec=pltpu.PrefetchScalarGridSpec(
            num_scalar_prefetch=1,
            grid=(depth // tile,),
            in_specs=[whole((2, rows, tokens))] * (2 * n)
            + [pl.BlockSpec((tokens, tile), lambda i, p: (0, i))] * (2 * n),
            out_specs=pl.BlockSpec((rows, tile), lambda i, p: (0, i)),
        ),
        out_shape=jax.ShapeDtypeStruct((rows, depth), dtype),
        compiler_params=pltpu.CompilerParams(vmem_limit_bytes=40 << 20),
        cost_estimate=pl.CostEstimate(flops=4 * n * rows * tokens * depth, bytes_accessed=2 * (rows + 2 * n * tokens) * depth, transcendentals=0),
        name="weight_terms",
    )(place, *own, *other, *blocks)


def xor(k):
    return [(j, j ^ k) for j in range(16)]


CORE, CROSS, PLANE = xor(1), xor(2), xor(4)
FAR = [(j, 12 - (j & 12) + (j & 3)) for j in range(16)]


def move(a, perm):
    return lax.ppermute(a, "fsdp", perm)


def swap(a):
    return lax.ppermute(a, "seq", [(0, 1), (1, 0)])


def local_grid(queries, keys, values, image_ids, q_gain, k_gain, w_out, grad_y):
    y = lax.axis_index("seq")
    f = lax.axis_index("fsdp")
    place = jnp.stack([y, f & 7, (f >> 3) ^ y]).astype(jnp.int32)
    dim = q_gain.shape[0]
    tokens = image_ids.shape[1]
    half = queries.shape[1] // 2
    row, col = image_ids, image_ids.reshape(tokens, 1)
    qg, kg = q_gain.reshape(1, dim), k_gain.reshape(1, dim)

    came = swap(
        jnp.stack(
            [lax.dynamic_slice_in_dim(a, (1 - y) * half, half, axis=1) for a in (queries, keys, values)]
        )
    )
    g4 = move(grad_y, PLANE)
    g2 = move(grad_y, CROSS)
    wr = move(w_out, FAR)
    g6 = move(g4, CROSS)
    evens = [grad_y, g2, g4, g6]
    blocks = []
    for g in evens:
        blocks += [g, move(g, CORE)]

    even, odd = attention_forward(place, queries, keys, values, came, row, col, qg, kg)
    odd = move(odd, CORE)
    own = [jnp.stack([even[j], odd[j]]) for j in range(4)]
    own = [own[0]] + [move(own[j], xor(2 * j)) for j in (1, 2, 3)]
    other = [swap(a) for a in own]

    sent = weight_terms(1, place, own, other, blocks, BF16)
    far = move(sent, FAR)
    kept = weight_terms(0, place, own, other, blocks, F32)

    order = [blocks[k] for k in (0, 2, 4, 6, 1, 3, 5, 7)]
    keep, send = gradient_products(place, w_out, wr, order)
    summed = (keep.astype(F32) + swap(send).astype(F32)).astype(BF16)
    even, odd = summed[:4], move(summed[4:], CORE)
    pairs = [jnp.stack([even[j], odd[j]]) for j in range(4)]
    grads = jnp.stack([pairs[0]] + [move(pairs[j], xor(2 * j)) for j in (1, 2, 3)])
    gq, gk, gv = attention_backward(place, queries, keys, values, came, grads, row, col, qg, kg)

    grad_w = (kept + far.astype(F32)) * tokens ** (-0.5)
    shape = (tokens, half // dim, dim)
    return (gq.reshape(shape), gk.reshape(shape), gv.reshape(shape), grad_w)


def solution(mesh):
    in_specs = (
        P(("fsdp", "seq"), None),
        P(("fsdp", "seq"), None),
        P(("fsdp", "seq"), None),
        P("fsdp", None),
        P(),
        P(),
        P("fsdp", "seq"),
        P("fsdp", "seq"),
    )
    out_specs = (
        P("fsdp", "seq", None),
        P("fsdp", "seq", None),
        P("fsdp", "seq", None),
        P("fsdp", "seq"),
    )
    grid = mesh.shape["fsdp"] == 16 and mesh.shape["seq"] == 2
    local = local_grid if grid else local_any
    return jax.shard_map(local, mesh=mesh, in_specs=in_specs, out_specs=out_specs, check_vma=False)
```

```python
import functools

import jax
import jax.numpy as jnp
from jax import lax
from jax.experimental import pallas as pl
from jax.experimental.pallas import tpu as pltpu
from jax.sharding import PartitionSpec as P

F32 = jnp.float32
BF16 = jnp.bfloat16


def norm_parts(source, gain):
    wide = source.astype(jnp.float32)
    centred = wide - jnp.mean(wide, axis=-1, keepdims=True)
    scale_inv = lax.rsqrt(jnp.mean(centred * centred, axis=-1, keepdims=True) + 1e-06)
    x_hat = centred * scale_inv
    return (x_hat, scale_inv, (x_hat * gain).astype(jnp.bfloat16))


def norm_back(grad_n, x_hat, scale_inv, gain):
    scaled = grad_n * gain
    return scale_inv * (
        scaled
        - jnp.mean(scaled, axis=-1, keepdims=True)
        - x_hat * jnp.mean(scaled * x_hat, axis=-1, keepdims=True)
    )


def probabilities(normalized_queries, normalized_keys, same_image, scale_factor):
    scores = (
        jnp.einsum(
            "krt,irt->rki", normalized_queries, normalized_keys, preferred_element_type=jnp.float32
        )
        * scale_factor
    )
    scores = jnp.where(same_image[None], scores, -1e30)
    row_top = jnp.max(scores, axis=-1, keepdims=True)
    exp_terms = jnp.exp(scores - row_top)
    return exp_terms / jnp.sum(exp_terms, axis=-1, keepdims=True)


def local_any(queries, keys, values, image_ids, q_gain, k_gain, w_out, grad_y):
    head_dim = q_gain.shape[0]
    tok_rows = queries.shape[0]
    heads_all = queries.shape[1] // head_dim
    scale_factor = head_dim ** (-0.5)
    q_patch = queries.reshape(tok_rows, heads_all, head_dim)
    k_patch = keys.reshape(tok_rows, heads_all, head_dim)
    v_patch = values.reshape(tok_rows, heads_all, head_dim)
    q_local, k_local, value_shard = (
        lax.all_to_all(q_patch, "seq", split_axis=1, concat_axis=0, tiled=True),
        lax.all_to_all(k_patch, "seq", split_axis=1, concat_axis=0, tiled=True),
        lax.all_to_all(v_patch, "seq", split_axis=1, concat_axis=0, tiled=True),
    )
    seq_length = q_local.shape[0]
    local_heads = q_local.shape[1]
    image_row = image_ids[0]
    same_image = image_row[:, None] == image_row[None, :]
    q_hat, q_inv, normalized_queries = norm_parts(q_local, q_gain)
    k_hat, k_inv, normalized_keys = norm_parts(k_local, k_gain)
    prob_rows = probabilities(normalized_queries, normalized_keys, same_image, scale_factor)
    probs_reduced_precision = prob_rows.astype(jnp.bfloat16)
    attended = jnp.einsum(
        "tgi,itp->gtp", probs_reduced_precision, value_shard, preferred_element_type=jnp.float32
    ).astype(jnp.bfloat16)
    attended_flat = attended.reshape(seq_length, local_heads * head_dim)
    partial_g = jnp.einsum(
        "ld,cd->lc",
        grad_y,
        lax.all_gather(w_out, "fsdp", axis=0, tiled=True),
        preferred_element_type=jnp.float32,
    )
    grad_sum = lax.psum_scatter(
        partial_g.astype(jnp.bfloat16), "seq", scatter_dimension=1, tiled=True
    )
    attention_gradient = grad_sum.reshape(seq_length, local_heads, head_dim)
    grad_values = jnp.einsum(
        "jpw,pjy->wjy",
        probs_reduced_precision,
        attention_gradient,
        preferred_element_type=jnp.float32,
    ).astype(jnp.bfloat16)
    probability_gradient = jnp.einsum(
        "krt,irt->rki", attention_gradient, value_shard, preferred_element_type=jnp.float32
    )
    row_delta = jnp.sum(prob_rows * probability_gradient, axis=-1, keepdims=True)
    score_gradient = (prob_rows * (probability_gradient - row_delta) * scale_factor).astype(
        jnp.bfloat16
    )
    normed_query_gradient = jnp.einsum(
        "tgi,itp->gtp", score_gradient, normalized_keys, preferred_element_type=jnp.float32
    )
    normed_key_gradient = jnp.einsum(
        "jpw,pjy->wjy", score_gradient, normalized_queries, preferred_element_type=jnp.float32
    )
    grad_queries = norm_back(normed_query_gradient, q_hat, q_inv, q_gain).astype(jnp.bfloat16)
    grad_keys = norm_back(normed_key_gradient, k_hat, k_inv, k_gain).astype(jnp.bfloat16)
    partial_w = jnp.einsum(
        "lc,ld->cd",
        lax.all_gather(attended_flat, "seq", axis=1, tiled=True),
        grad_y,
        preferred_element_type=jnp.float32,
    )
    summed = lax.psum_scatter(partial_w, "fsdp", scatter_dimension=0, tiled=True)
    grad_w = summed * seq_length ** (-0.5)
    return (grad_queries, grad_keys, grad_values, grad_w)


def dot_nt(a, b):
    return lax.dot_general(a, b, (((1,), (1,)), ((), ())), preferred_element_type=F32)


def dot_tn(a, b):
    return lax.dot_general(a, b, (((0,), (0,)), ((), ())), preferred_element_type=F32)


def dot_nn(a, b):
    return jnp.dot(a, b, preferred_element_type=F32)


def assemble(first, own, came):
    return jnp.concatenate([jnp.where(first, own, came), jnp.where(first, came, own)], axis=0)


def head_inputs(place, own_ref, came_ref, h, dim):
    first = place[0] == 0
    cols = slice(h * dim, (h + 1) * dim)
    return [assemble(first, own_ref[n, :, cols], came_ref[n, :, cols]) for n in range(3)]


def pack_kernel(place, *refs):
    mine, theirs, own_ref, send_ref = refs[:3], refs[3:6], refs[6], refs[7]
    for n in range(3):
        own_ref[n] = mine[n][...]
        send_ref[n] = theirs[n][...]


def pack(place, arrays, steps=2):
    rows, width = arrays[0].shape[0], arrays[0].shape[1] // 2
    wide = width // steps
    mine = pl.BlockSpec((rows, wide), lambda i, p: (0, p[0] * steps + i))
    theirs = pl.BlockSpec((rows, wide), lambda i, p: (0, (1 - p[0]) * steps + i))
    out = pl.BlockSpec((3, rows, wide), lambda i, p: (0, 0, i))
    return pl.pallas_call(
        pack_kernel,
        grid_spec=pltpu.PrefetchScalarGridSpec(
            num_scalar_prefetch=1, grid=(steps,), in_specs=[mine] * 3 + [theirs] * 3, out_specs=[out, out]
        ),
        out_shape=[jax.ShapeDtypeStruct((3, rows, width), BF16)] * 2,
        cost_estimate=pl.CostEstimate(flops=1000, bytes_accessed=1000, transcendentals=0),
        name="pack",
    )(place, *arrays, *arrays)


def head_probs(q, k, qg, kg, same, scale):
    q_hat, q_inv, qn = norm_parts(q, qg)
    k_hat, k_inv, kn = norm_parts(k, kg)
    scores = jnp.where(same, dot_nt(qn, kn) * scale, -1e30)
    exp_terms = jnp.exp(scores - jnp.max(scores, axis=-1, keepdims=True))
    probs = exp_terms / jnp.sum(exp_terms, axis=-1, keepdims=True)
    return probs, q_hat, q_inv, qn, k_hat, k_inv, kn


def forward_kernel(per, dim, place, own_ref, came_ref, row_ref, col_ref, qg_ref, kg_ref, even_ref, odd_ref):
    same = col_ref[...] == row_ref[...]
    done = []
    for h in range(per):
        q, k, v = head_inputs(place, own_ref, came_ref, h, dim)
        probs = head_probs(q, k, qg_ref[...], kg_ref[...], same, dim**-0.5)[0]
        done.append(dot_nn(probs.astype(BF16), v).T.astype(BF16))
    att = jnp.concatenate(done, axis=0)
    half = att.shape[0] // 2
    straight = (place[1] & 1) == 0
    low, high = att[:half], att[half:]
    even_ref[0] = jnp.where(straight, low, high)
    odd_ref[0] = jnp.where(straight, high, low)


def backward_kernel(per, dim, n_into, place, own_ref, came_ref, d_ref, row_ref, col_ref, qg_ref, kg_ref, *rest):
    into, outs = rest[:n_into], rest[n_into:]
    wide = per * dim
    if n_into:
        start = pl.multiple_of(wide * (2 * ((place[1] >> 2) ^ place[2] ^ 1) + pair_index(pl.program_id(0), place) % 2), wide)

        @pl.when(pl.program_id(0) == 0)
        def _():
            first = pl.multiple_of(2 * wide * ((place[1] >> 2) ^ place[2]), 2 * wide)
            for ref, out in zip(into, outs):
                out[:, pl.ds(first, 2 * wide)] = ref[...]

    else:
        start = pl.multiple_of(wide * (pair_index(pl.program_id(0), place) % 2), wide)
    gq_ref, gk_ref, gv_ref = (out.at[:, pl.ds(start, wide)] for out in outs)
    same = col_ref[...] == row_ref[...]
    scale = dim**-0.5
    straight = (place[1] & 1) == 0
    one, two = d_ref[0, 0], d_ref[0, 1]
    grad = jnp.concatenate([jnp.where(straight, one, two), jnp.where(straight, two, one)], axis=0)
    qg, kg = qg_ref[...], kg_ref[...]
    for h in range(per):
        q, k, v = head_inputs(place, own_ref, came_ref, h, dim)
        probs, q_hat, q_inv, qn, k_hat, k_inv, kn = head_probs(q, k, qg, kg, same, scale)
        d = grad[h * dim : (h + 1) * dim].T
        gv = dot_tn(probs.astype(BF16), d)
        gp = dot_nt(d, v)
        delta = jnp.sum(probs * gp, axis=-1, keepdims=True)
        gs = (probs * (gp - delta) * scale).astype(BF16)
        cols = slice(h * dim, (h + 1) * dim)
        gq_ref[:, cols] = norm_back(dot_nn(gs, kn), q_hat, q_inv, qg).astype(BF16)
        gk_ref[:, cols] = norm_back(dot_tn(gs, qn), k_hat, k_inv, kg).astype(BF16)
        gv_ref[:, cols] = gv.astype(BF16)


def whole(shape):
    return pl.BlockSpec(shape, lambda *_: (0,) * len(shape))


def pair_index(i, p):
    return i ^ (p[1] >> 1) ^ (p[2] << 1)


def attention_forward(place, mine, came, row, col, qg, kg):
    dim = qg.shape[1]
    half_tokens, heads = mine.shape[1], mine.shape[2] // dim
    tokens, per = 2 * half_tokens, heads // 4
    rows = per * dim // 2
    out = pl.BlockSpec((1, rows, tokens), lambda i, p: (pair_index(i, p), 0, 0))
    return pl.pallas_call(
        functools.partial(forward_kernel, per, dim),
        grid_spec=pltpu.PrefetchScalarGridSpec(
            num_scalar_prefetch=1,
            grid=(4,),
            in_specs=[pl.BlockSpec((3, half_tokens, per * dim), lambda i, p: (0, 0, i))] * 2
            + [whole((1, tokens)), whole((tokens, 1)), whole((1, dim)), whole((1, dim))],
            out_specs=[out, out],
        ),
        out_shape=[jax.ShapeDtypeStruct((4, rows, tokens), BF16)] * 2,
        compiler_params=pltpu.CompilerParams(vmem_limit_bytes=40 << 20),
        cost_estimate=pl.CostEstimate(flops=1000, bytes_accessed=1000, transcendentals=0),
        name="attention_forward",
    )(place, mine, came, row, col, qg, kg)


def attention_backward(place, pairs, mine, came, grads, row, col, qg, kg, into=()):
    dim = qg.shape[1]
    half_tokens, heads = mine.shape[1], mine.shape[2] // dim
    tokens, per = 2 * half_tokens, heads // 4
    rows, half = per * dim // 2, 2 * per * dim
    width = 2 * half if into else half
    return pl.pallas_call(
        functools.partial(backward_kernel, per, dim, len(into)),
        grid_spec=pltpu.PrefetchScalarGridSpec(
            num_scalar_prefetch=1,
            grid=(2,),
            in_specs=[pl.BlockSpec((3, half_tokens, per * dim), lambda i, p: (0, 0, pair_index(i + pairs, p)))] * 2
            + [pl.BlockSpec((1, 2, rows, tokens), lambda i, p: (i, 0, 0, 0))]
            + [whole((1, tokens)), whole((tokens, 1)), whole((1, dim)), whole((1, dim))]
            + [whole((tokens, half))] * len(into),
            out_specs=[whole((tokens, width))] * 3,
        ),
        out_shape=[jax.ShapeDtypeStruct((tokens, width), BF16)] * 3,
        compiler_params=pltpu.CompilerParams(vmem_limit_bytes=(60 if into else 40) << 20),
        cost_estimate=pl.CostEstimate(flops=1000, bytes_accessed=1000, transcendentals=0),
        name="attention_backward",
    )(place, mine, came, grads, row, col, qg, kg, *into)


def products_kernel(n, place, *refs):
    w_refs, mid_refs, end_refs, rest = refs[:2], refs[2:4], refs[4:7], refs[7:]
    g_refs, (keep_ref, send_ref, acc_ref) = rest[: 2 * n], rest[2 * n :]
    step = pl.program_id(0)
    rows = w_refs[0].shape[0]

    @pl.when(step == 0)
    def _():
        acc_ref[...] = jnp.zeros_like(acc_ref)

    ends = (jnp.where(step < 2, end_refs[0][...], end_refs[1][...]), end_refs[2][...])
    both = [
        jnp.concatenate([w_refs[c][...], jnp.where(place[3] == 1, mid_refs[c][...], ends[c])], axis=0)
        for c in range(2)
    ]
    both = jnp.concatenate(both, axis=1)
    for j in range(n):
        acc_ref[j] += dot_nt(both, jnp.concatenate([g_refs[j][...], g_refs[n + j][...]], axis=1))

    @pl.when(step == pl.num_programs(0) - 1)
    def _():
        flip = place[2] == 1
        for j in range(n):
            own, other = acc_ref[j, :rows].astype(BF16), acc_ref[j, rows:].astype(BF16)
            keep_ref[j] = jnp.where(flip, other, own)
            send_ref[j] = jnp.where(flip, own, other)


def columns(rows, tile, start=0):
    skip = start // tile
    return pl.BlockSpec((rows, tile), lambda i, p: (0, i + skip))


def gradient_products(place, w, mid, end, halves):
    rows, depth = w.shape
    cut, tile = depth // 2, depth // 6
    n, tokens = len(halves[0]), halves[0][0][0].shape[0]
    out = whole((n, rows, tokens))
    ends = (lambda i, p: (0, jnp.minimum(i, 1)), lambda i, p: (0, 0), lambda i, p: (0, i + 1))
    return pl.pallas_call(
        functools.partial(products_kernel, n),
        grid_spec=pltpu.PrefetchScalarGridSpec(
            num_scalar_prefetch=1,
            grid=(3,),
            in_specs=[columns(rows, tile), columns(rows, tile, cut)] * 2
            + [pl.BlockSpec((rows, tile), index) for index in ends]
            + [columns(tokens, tile, start) for half in halves for _, start in half],
            out_specs=[out, out],
            scratch_shapes=[pltpu.VMEM((n, 2 * rows, tokens), F32)],
        ),
        out_shape=[jax.ShapeDtypeStruct((n, rows, tokens), BF16)] * 2,
        compiler_params=pltpu.CompilerParams(vmem_limit_bytes=40 << 20),
        cost_estimate=pl.CostEstimate(flops=1000, bytes_accessed=1000, transcendentals=0),
        name="gradient_products",
    )(place, w, w, mid, mid, end[0], end[1], end[1], *[a for half in halves for a, _ in half])


def weight_kernel(n, parts, place, own_ref, other_ref, *refs):
    g_refs, far_refs, kept_ref, both_ref = refs[:n], refs[n:-2], refs[-2], refs[-1]
    rows, tokens = own_ref.shape[1:]
    step = pl.program_id(0)

    @pl.when(step == 0)
    def _():
        flip = place[2] == 1
        for j in range(n):
            cols = slice(j * tokens, (j + 1) * tokens)
            both_ref[:rows, cols] = jnp.where(flip, own_ref[j], other_ref[j])
            both_ref[rows:, cols] = jnp.where(flip, other_ref[j], own_ref[j])

    total = dot_nn(both_ref[...], jnp.concatenate([g_ref[...] for g_ref in g_refs], axis=0))
    kept_ref[...] = total[rows:]
    sent = total[:rows].astype(BF16)
    first = 0
    for part, far_ref in zip(parts, far_refs):
        for c in range(part):

            @pl.when(step == first + c)
            def _(c=c, far_ref=far_ref):
                tile = sent.shape[1]
                far_ref[:, c * tile : (c + 1) * tile] = sent

        first += part


def weight_terms(place, own, other, half, parts, tile=512):
    n, rows, tokens = own.shape
    depth = sum(parts) * tile
    return pl.pallas_call(
        functools.partial(weight_kernel, n, parts),
        grid_spec=pltpu.PrefetchScalarGridSpec(
            num_scalar_prefetch=1,
            grid=(sum(parts),),
            in_specs=[whole((n, rows, tokens))] * 2 + [columns(tokens, tile, start) for start in half[1]],
            out_specs=[whole((rows, part * tile)) for part in parts] + [columns(rows, tile)],
            scratch_shapes=[pltpu.VMEM((2 * rows, n * tokens), BF16)],
        ),
        out_shape=[jax.ShapeDtypeStruct((rows, part * tile), BF16) for part in parts]
        + [jax.ShapeDtypeStruct((rows, depth), F32)],
        compiler_params=pltpu.CompilerParams(vmem_limit_bytes=40 << 20),
        cost_estimate=pl.CostEstimate(flops=1000, bytes_accessed=1000, transcendentals=0),
        name="weight_terms",
    )(place, own, other, *half[0])


def finish_kernel(parts, scale, *refs):
    kept_refs, far_refs, out_ref = refs[:2], refs[2:-1], refs[-1]
    kept = [kept_ref[...] for kept_ref in kept_refs]
    first, cut = 0, kept[0].shape[1]
    for far_ref in far_refs:
        last = first + far_ref.shape[1]
        own = kept[first // cut][:, first % cut : (last - 1) % cut + 1]
        out_ref[:, first:last] = (own + far_ref[...].astype(F32)) * scale
        first = last


def finish(kept, far, scale):
    rows, depth = kept[0].shape[0], 2 * kept[0].shape[1]
    tile = rows // 4

    def block(a):
        return pl.BlockSpec((tile, a.shape[1]), lambda i: (i, 0))

    return pl.pallas_call(
        functools.partial(finish_kernel, len(far), scale),
        grid=(rows // tile,),
        in_specs=[block(a) for a in (*kept, *far)],
        out_specs=pl.BlockSpec((tile, depth), lambda i: (i, 0)),
        out_shape=jax.ShapeDtypeStruct((rows, depth), F32),
        compiler_params=pltpu.CompilerParams(vmem_limit_bytes=40 << 20),
        cost_estimate=pl.CostEstimate(flops=1000, bytes_accessed=1000, transcendentals=0),
        name="finish",
    )(*kept, *far)


def xor(k):
    return [(j, j ^ k) for j in range(16)]


CORE, CROSS, PLANE = xor(1), xor(2), xor(4)
FAR = xor(12)
MIDDLE = [pair for pair in FAR if 4 <= pair[0] < 12]
ENDS = [pair for pair in FAR if not 4 <= pair[0] < 12]


def move(a, perm, name):
    with jax.named_scope(name):
        return lax.ppermute(a, "fsdp", perm)


def swap(a, name):
    with jax.named_scope(name):
        return lax.ppermute(a, "seq", [(0, 1), (1, 0)])


def local_grid(queries, keys, values, image_ids, q_gain, k_gain, w_out, grad_y):
    y = lax.axis_index("seq")
    f = lax.axis_index("fsdp")
    middle = (f >> 3) ^ ((f >> 2) & 1)
    place = jnp.stack([y, f & 7, (f >> 3) ^ y, middle]).astype(jnp.int32)
    dim = q_gain.shape[0]
    tokens = image_ids.shape[1]
    half = queries.shape[1] // 2
    row, col = image_ids, image_ids.reshape(tokens, 1)
    qg, kg = q_gain.reshape(1, dim), k_gain.reshape(1, dim)
    barrier = lax.optimization_barrier
    cut = grad_y.shape[1] // 2

    cut = grad_y.shape[1] // 2
    barrier = lax.optimization_barrier

    mine, send = pack(place, (queries, keys, values))
    third = 2 * cut // 3
    g4 = move(grad_y, PLANE, "gy_plane")
    w_a, w_b = w_out[:, :third], w_out[:, third:]
    send, gy, w_own, w_a = barrier((send, grad_y, w_out, w_a))
    came = swap(send, "qkv_seq")
    g2 = move(gy, CROSS, "gy_cross")
    w_end_a = move(w_a, ENDS, "w_ends_a")
    w_mid = move(w_own, MIDDLE, "w_middle")
    even, odd = attention_forward(place, mine, came, row, col, qg, kg)
    odd = move(odd, CORE, "att_core")
    even, odd, g2, g4, gy, w_mid, w_end_a, w_b = barrier((even, odd, g2, g4, gy, w_mid, w_end_a, w_b))
    own = [jnp.stack([even[j], odd[j]]) for j in range(4)]
    other = [swap(own[0], "att_seq")]
    own = [own[0]] + [move(own[j], xor(2 * j), "att_group") for j in (1, 2, 3)]
    g1 = move(gy, CORE, "gy_core")
    g4a, g4b = g4[:, :cut], g4[:, cut:]
    own, other, g4, g4a, g4b, w_b, g2, g1 = barrier((own, other, g4, g4a, g4b, w_b, g2, g1))
    other.append(swap(jnp.concatenate(own[1:]), "att_seq"))
    g6a = move(g4a, CROSS, "gy_plane_cross_a")
    w_end_b = move(w_b, ENDS, "w_ends_b")
    g3, g5 = (move(g, CORE, "gy_core") for g in (g2, g4))
    own, other = jnp.concatenate(own), jnp.concatenate(other)
    own, other, g6a, w_end_b, g3, g5, g4b = barrier((own, other, g6a, w_end_b, g3, g5, g4b))
    weights = (w_out, w_mid, (w_end_a, w_end_b))
    g6b = move(g4b, CROSS, "gy_plane_cross_b")
    g7a = move(g6a, CORE, "gy_core")
    half_a = ([gy, g1, g2, g3, g4, g5, g6a, g7a], (0,) * 8)
    *sent, kept_a = weight_terms(place, own, other, half_a, (1, 2))
    far = [move(sent[0], FAR, "grad_w_far")]
    tied = barrier((gy, g2, g1, g3, sent[0]))[:4]
    keep0, send0 = gradient_products(place, *weights, [[(a, start) for a in tied] for start in (0, cut)])
    g6b, keep0, send0, far, sent, kept_a = barrier((g6b, keep0, send0, far, sent, kept_a))
    came0 = swap(send0, "products_seq")
    far.append(move(sent[1], FAR, "grad_w_far"))
    summed0 = (keep0.astype(F32) + came0.astype(F32)).astype(BF16)
    odd = move(summed0[2:], CORE, "products_core")
    near = [jnp.stack([summed0[j], odd[j]]) for j in range(2)]
    near[1] = move(near[1], xor(2), "products_group")
    g7b = move(g6b, CORE, "gy_core")
    keep1, send1 = gradient_products(
        place, *weights, [[(g4, 0), (g6a, 0), (g5, 0), (g7a, 0)], [(g4, cut), (g6b, 0), (g5, cut), (g7b, 0)]]
    )
    came1 = swap(send1, "products_seq")
    half_b, keep1 = barrier(([gy, g1, g2, g3, g4, g5, g6b, g7b], keep1))
    *sent, kept_b = weight_terms(place, own, other, (half_b, (cut,) * 6 + (0,) * 2), (1, 2))
    far, near, keep1, came1, sent, kept_b = barrier((far, near, keep1, came1, sent, kept_b))
    far.append(move(sent[0], FAR, "grad_w_far"))
    summed1 = (keep1.astype(F32) + came1.astype(F32)).astype(BF16)
    odd = move(summed1[2:], CORE, "products_core")
    next_plane = [jnp.stack([summed1[j], odd[j]]) for j in range(2)]
    next_plane = [move(next_plane[j], xor(4 + 2 * j), "products_group") for j in range(2)]
    grads = attention_backward(place, 0, mine, came, jnp.stack(near), row, col, qg, kg)
    far, next_plane, grads, sent = barrier((far, next_plane, grads, sent))
    far.append(move(sent[1], FAR, "grad_w_far"))
    gq, gk, gv = attention_backward(
        place, 2, mine, came, jnp.stack(next_plane), row, col, qg, kg, tuple(grads)
    )

    grad_w = finish((kept_a, kept_b), far, tokens ** (-0.5))
    shape = (tokens, half // dim, dim)
    return (gq.reshape(shape), gk.reshape(shape), gv.reshape(shape), grad_w)


def solution(mesh):
    in_specs = (
        P(("fsdp", "seq"), None),
        P(("fsdp", "seq"), None),
        P(("fsdp", "seq"), None),
        P("fsdp", None),
        P(),
        P(),
        P("fsdp", "seq"),
        P("fsdp", "seq"),
    )
    out_specs = (
        P("fsdp", "seq", None),
        P("fsdp", "seq", None),
        P("fsdp", "seq", None),
        P("fsdp", "seq"),
    )
    grid = mesh.shape["fsdp"] == 16 and mesh.shape["seq"] == 2
    local = local_grid if grid else local_any
    return jax.shard_map(local, mesh=mesh, in_specs=in_specs, out_specs=out_specs, check_vma=False)
```

```python
import functools

import jax
import jax.numpy as jnp
from jax import lax
from jax.experimental import pallas as pl
from jax.experimental.pallas import tpu as pltpu
from jax.sharding import PartitionSpec as P

F32 = jnp.float32
BF16 = jnp.bfloat16


def norm_parts(source, gain):
    wide = source.astype(jnp.float32)
    centred = wide - jnp.mean(wide, axis=-1, keepdims=True)
    scale_inv = lax.rsqrt(jnp.mean(centred * centred, axis=-1, keepdims=True) + 1e-06)
    x_hat = centred * scale_inv
    return (x_hat, scale_inv, (x_hat * gain).astype(jnp.bfloat16))


def norm_back(grad_n, x_hat, scale_inv, gain):
    scaled = grad_n * gain
    return scale_inv * (
        scaled
        - jnp.mean(scaled, axis=-1, keepdims=True)
        - x_hat * jnp.mean(scaled * x_hat, axis=-1, keepdims=True)
    )


def probabilities(normalized_queries, normalized_keys, same_image, scale_factor):
    scores = (
        jnp.einsum(
            "krt,irt->rki", normalized_queries, normalized_keys, preferred_element_type=jnp.float32
        )
        * scale_factor
    )
    scores = jnp.where(same_image[None], scores, -1e30)
    row_top = jnp.max(scores, axis=-1, keepdims=True)
    exp_terms = jnp.exp(scores - row_top)
    return exp_terms / jnp.sum(exp_terms, axis=-1, keepdims=True)


def local_any(queries, keys, values, image_ids, q_gain, k_gain, w_out, grad_y):
    head_dim = q_gain.shape[0]
    tok_rows = queries.shape[0]
    heads_all = queries.shape[1] // head_dim
    scale_factor = head_dim ** (-0.5)
    q_patch = queries.reshape(tok_rows, heads_all, head_dim)
    k_patch = keys.reshape(tok_rows, heads_all, head_dim)
    v_patch = values.reshape(tok_rows, heads_all, head_dim)
    q_local, k_local, value_shard = (
        lax.all_to_all(q_patch, "seq", split_axis=1, concat_axis=0, tiled=True),
        lax.all_to_all(k_patch, "seq", split_axis=1, concat_axis=0, tiled=True),
        lax.all_to_all(v_patch, "seq", split_axis=1, concat_axis=0, tiled=True),
    )
    seq_length = q_local.shape[0]
    local_heads = q_local.shape[1]
    image_row = image_ids[0]
    same_image = image_row[:, None] == image_row[None, :]
    q_hat, q_inv, normalized_queries = norm_parts(q_local, q_gain)
    k_hat, k_inv, normalized_keys = norm_parts(k_local, k_gain)
    prob_rows = probabilities(normalized_queries, normalized_keys, same_image, scale_factor)
    probs_reduced_precision = prob_rows.astype(jnp.bfloat16)
    attended = jnp.einsum(
        "tgi,itp->gtp", probs_reduced_precision, value_shard, preferred_element_type=jnp.float32
    ).astype(jnp.bfloat16)
    attended_flat = attended.reshape(seq_length, local_heads * head_dim)
    partial_g = jnp.einsum(
        "ld,cd->lc",
        grad_y,
        lax.all_gather(w_out, "fsdp", axis=0, tiled=True),
        preferred_element_type=jnp.float32,
    )
    grad_sum = lax.psum_scatter(
        partial_g.astype(jnp.bfloat16), "seq", scatter_dimension=1, tiled=True
    )
    attention_gradient = grad_sum.reshape(seq_length, local_heads, head_dim)
    grad_values = jnp.einsum(
        "jpw,pjy->wjy",
        probs_reduced_precision,
        attention_gradient,
        preferred_element_type=jnp.float32,
    ).astype(jnp.bfloat16)
    probability_gradient = jnp.einsum(
        "krt,irt->rki", attention_gradient, value_shard, preferred_element_type=jnp.float32
    )
    row_delta = jnp.sum(prob_rows * probability_gradient, axis=-1, keepdims=True)
    score_gradient = (prob_rows * (probability_gradient - row_delta) * scale_factor).astype(
        jnp.bfloat16
    )
    normed_query_gradient = jnp.einsum(
        "tgi,itp->gtp", score_gradient, normalized_keys, preferred_element_type=jnp.float32
    )
    normed_key_gradient = jnp.einsum(
        "jpw,pjy->wjy", score_gradient, normalized_queries, preferred_element_type=jnp.float32
    )
    grad_queries = norm_back(normed_query_gradient, q_hat, q_inv, q_gain).astype(jnp.bfloat16)
    grad_keys = norm_back(normed_key_gradient, k_hat, k_inv, k_gain).astype(jnp.bfloat16)
    partial_w = jnp.einsum(
        "lc,ld->cd",
        lax.all_gather(attended_flat, "seq", axis=1, tiled=True),
        grad_y,
        preferred_element_type=jnp.float32,
    )
    summed = lax.psum_scatter(partial_w, "fsdp", scatter_dimension=0, tiled=True)
    grad_w = summed * seq_length ** (-0.5)
    return (grad_queries, grad_keys, grad_values, grad_w)


def dot_nt(a, b):
    return lax.dot_general(a, b, (((1,), (1,)), ((), ())), preferred_element_type=F32)


def dot_tn(a, b):
    return lax.dot_general(a, b, (((0,), (0,)), ((), ())), preferred_element_type=F32)


def dot_nn(a, b):
    return jnp.dot(a, b, preferred_element_type=F32)


def assemble(first, own, came):
    return jnp.concatenate([jnp.where(first, own, came), jnp.where(first, came, own)], axis=0)


def head_inputs(place, own_ref, came_ref, h, dim):
    first = place[0] == 0
    cols = slice(h * dim, (h + 1) * dim)
    return [assemble(first, own_ref[n, :, cols], came_ref[n, :, cols]) for n in range(3)]


def pack_kernel(place, *refs):
    mine, theirs, own_ref, send_ref = refs[:3], refs[3:6], refs[6], refs[7]
    for n in range(3):
        own_ref[n] = mine[n][...]
        send_ref[n] = theirs[n][...]


def pack(place, arrays, steps=1):
    rows, width = arrays[0].shape[0], arrays[0].shape[1] // 2
    wide = width // steps
    mine = pl.BlockSpec((rows, wide), lambda i, p: (0, p[0] * steps + i))
    theirs = pl.BlockSpec((rows, wide), lambda i, p: (0, (1 - p[0]) * steps + i))
    out = pl.BlockSpec((3, rows, wide), lambda i, p: (0, 0, i))
    return pl.pallas_call(
        pack_kernel,
        grid_spec=pltpu.PrefetchScalarGridSpec(
            num_scalar_prefetch=1, grid=(steps,), in_specs=[mine] * 3 + [theirs] * 3, out_specs=[out, out]
        ),
        out_shape=[pltpu.HBM((3, rows, width), BF16), jax.ShapeDtypeStruct((3, rows, width), BF16)],
        cost_estimate=pl.CostEstimate(flops=1000, bytes_accessed=1000, transcendentals=0),
        name="pack",
    )(place, *arrays, *arrays)


def head_probs(q, k, qg, kg, same, scale):
    q_hat, q_inv, qn = norm_parts(q, qg)
    k_hat, k_inv, kn = norm_parts(k, kg)
    scores = jnp.where(same, dot_nt(qn, kn) * scale, -1e30)
    exp_terms = jnp.exp(scores - jnp.max(scores, axis=-1, keepdims=True))
    probs = exp_terms / jnp.sum(exp_terms, axis=-1, keepdims=True)
    return probs, q_hat, q_inv, qn, k_hat, k_inv, kn


def forward_kernel(per, dim, place, own_ref, came_ref, row_ref, col_ref, qg_ref, kg_ref, even_ref, odd_ref):
    same = col_ref[...] == row_ref[...]
    done = []
    for h in range(per):
        q, k, v = head_inputs(place, own_ref, came_ref, h, dim)
        probs = head_probs(q, k, qg_ref[...], kg_ref[...], same, dim**-0.5)[0]
        done.append(dot_nn(probs.astype(BF16), v).T.astype(BF16))
    att = jnp.concatenate(done, axis=0)
    half = att.shape[0] // 2
    straight = (place[1] & 1) == 0
    low, high = att[:half], att[half:]
    even_ref[0] = jnp.where(straight, low, high)
    odd_ref[0] = jnp.where(straight, high, low)


def prepare_kernel(per, dim, place, own_ref, came_ref, row_ref, col_ref, qg_ref, kg_ref, p_ref, hat_ref, inv_ref, low_ref):
    same = col_ref[...] == row_ref[...]
    for h in range(per):
        q, k, v = head_inputs(place, own_ref, came_ref, h, dim)
        probs, *parts = head_probs(q, k, qg_ref[...], kg_ref[...], same, dim**-0.5)
        p_ref[h] = probs
        for n, (hat, inv, normed) in enumerate((parts[:3], parts[3:])):
            hat_ref[n, h] = hat
            inv_ref[n, h] = jnp.broadcast_to(inv, hat.shape)
            low_ref[n, h] = normed
        low_ref[2, h] = v


def backward_kernel(per, dim, n_into, place, p_ref, hat_ref, inv_ref, low_ref, d_ref, qg_ref, kg_ref, *rest):
    gq_ref, gk_ref, gv_ref = rest[n_into:]
    scale = dim**-0.5
    straight = (place[1] & 1) == 0
    one, two = d_ref[0, 0], d_ref[0, 1]
    grad = jnp.concatenate([jnp.where(straight, one, two), jnp.where(straight, two, one)], axis=0)
    qg, kg = qg_ref[...], kg_ref[...]
    for h in range(per):
        probs, qn, kn, v = p_ref[h], low_ref[0, h], low_ref[1, h], low_ref[2, h]
        d = grad[h * dim : (h + 1) * dim].T
        gp = dot_nt(d, v)
        gv_ref[h] = dot_tn(probs.astype(BF16), d).astype(BF16)
        delta = jnp.sum(probs * gp, axis=-1, keepdims=True)
        gs = (probs * (gp - delta) * scale).astype(BF16)
        gq_ref[h] = norm_back(dot_nn(gs, kn), hat_ref[0, h], inv_ref[0, h], qg).astype(BF16)
        gk_ref[h] = norm_back(dot_tn(gs, qn), hat_ref[1, h], inv_ref[1, h], kg).astype(BF16)


def whole(shape):
    return pl.BlockSpec(shape, lambda *_: (0,) * len(shape))


def pair_index(i, p):
    return i ^ (p[1] >> 1) ^ (p[2] << 1)


def attention_forward(place, mine, came, row, col, qg, kg):
    dim = qg.shape[1]
    half_tokens, heads = mine.shape[1], mine.shape[2] // dim
    tokens, per = 2 * half_tokens, heads // 4
    rows = per * dim // 2
    out = pl.BlockSpec((1, rows, tokens), lambda i, p: (pair_index(i, p), 0, 0))
    return pl.pallas_call(
        functools.partial(forward_kernel, per, dim),
        grid_spec=pltpu.PrefetchScalarGridSpec(
            num_scalar_prefetch=1,
            grid=(4,),
            in_specs=[pl.BlockSpec((3, half_tokens, per * dim), lambda i, p: (0, 0, i))] * 2
            + [whole((1, tokens)), whole((tokens, 1)), whole((1, dim)), whole((1, dim))],
            out_specs=[out, out],
        ),
        out_shape=[jax.ShapeDtypeStruct((4, rows, tokens), BF16)] * 2,
        compiler_params=pltpu.CompilerParams(vmem_limit_bytes=16 << 20),
        cost_estimate=pl.CostEstimate(flops=1000, bytes_accessed=1000, transcendentals=0),
        name="attention_forward",
    )(place, pltpu.with_memory_space_constraint(mine, pltpu.HBM), came, row, col, qg, kg)


def attention_prepare(place, mine, came, row, col, qg, kg):
    dim = qg.shape[1]
    half_tokens, heads = mine.shape[1], mine.shape[2] // dim
    tokens, per = 2 * half_tokens, heads // 4

    def saved(n, dtype):
        spec = pl.BlockSpec((n, per, tokens, dim), lambda i, p: (0, i, 0, 0))
        return spec, pltpu.HBM((n, heads, tokens, dim), dtype)

    probs = pl.BlockSpec((per, tokens, tokens), lambda i, p: (i, 0, 0)), pltpu.HBM((heads, tokens, tokens), F32)
    specs, shapes = zip(probs, saved(2, F32), saved(2, F32), saved(3, BF16))
    return pl.pallas_call(
        functools.partial(prepare_kernel, per, dim),
        grid_spec=pltpu.PrefetchScalarGridSpec(
            num_scalar_prefetch=1,
            grid=(4,),
            in_specs=[pl.BlockSpec((3, half_tokens, per * dim), lambda i, p: (0, 0, i))] * 2
            + [whole((1, tokens)), whole((tokens, 1)), whole((1, dim)), whole((1, dim))],
            out_specs=specs,
        ),
        out_shape=shapes,
        compiler_params=pltpu.CompilerParams(vmem_limit_bytes=16 << 20),
        cost_estimate=pl.CostEstimate(flops=1000, bytes_accessed=1000, transcendentals=0),
        name="attention_prepare",
    )(place, pltpu.with_memory_space_constraint(mine, pltpu.HBM), came, row, col, qg, kg)


def attention_backward(place, first, pairs, saved, grads, qg, kg, into=()):
    heads, tokens = saved[0].shape[:2]
    dim, per, rows = qg.shape[1], heads // 4, grads.shape[2]

    def index(i, p):
        return pair_index(i + first, p)

    def block(n):
        return pl.BlockSpec((n, per, tokens, dim), lambda i, p: (0, index(i, p), 0, 0))

    return pl.pallas_call(
        functools.partial(backward_kernel, per, dim, len(into)),
        grid_spec=pltpu.PrefetchScalarGridSpec(
            num_scalar_prefetch=1,
            grid=(pairs,),
            in_specs=[pl.BlockSpec((per, tokens, tokens), lambda i, p: (index(i, p), 0, 0)), block(2), block(2), block(3)]
            + [pl.BlockSpec((1, 2, rows, tokens), lambda i, p: (i, 0, 0, 0))]
            + [whole((1, dim)), whole((1, dim))]
            + [pl.BlockSpec(memory_space=pl.ANY)] * len(into),
            out_specs=[pl.BlockSpec((per, tokens, dim), lambda i, p: (index(i, p), 0, 0))] * 3,
        ),
        out_shape=[pltpu.HBM((heads, tokens, dim), BF16)] * 3,
        input_output_aliases={8 + n: n for n in range(len(into))},
        compiler_params=pltpu.CompilerParams(vmem_limit_bytes=16 << 20),
        cost_estimate=pl.CostEstimate(flops=1000, bytes_accessed=1000, transcendentals=0),
        name="attention_backward",
    )(place, *saved, grads, qg, kg, *into)


VECTOR = pl.BlockSpec(memory_space=pltpu.VMEM)
SCALAR = pl.BlockSpec(memory_space=pltpu.SMEM)


def hold_kernel(*refs):
    n = len(refs) // 2
    for source, held in zip(refs[:n], refs[n:]):
        held[...] = source[...]


def hold(*arrays, steps=4):
    specs = [pl.BlockSpec((a.shape[0] // steps, a.shape[1]), lambda i: (i, 0)) for a in arrays]
    return pl.pallas_call(
        hold_kernel,
        grid=(steps,),
        in_specs=specs,
        out_specs=specs,
        out_shape=[pltpu.VMEM(a.shape, a.dtype) for a in arrays],
        compiler_params=pltpu.CompilerParams(vmem_limit_bytes=16 << 20),
        cost_estimate=pl.CostEstimate(flops=1000, bytes_accessed=1000, transcendentals=0),
        name="hold",
    )(*arrays)


def products_kernel(n, parts, place, w_ref, mid_ref, end_ref, *refs):
    g_refs, (keep_ref, send_ref, both_ref) = refs[:-3], refs[-3:]
    rows = w_ref.shape[0]
    middle, flip = place[3] == 1, place[2] == 1
    for first, depth, _ in parts:
        cols = slice(first, first + depth)
        own, far = w_ref[:, cols], jnp.where(middle, mid_ref[:, cols], end_ref[:, cols])
        both_ref[:rows, cols] = jnp.where(flip, far, own)
        both_ref[rows:, cols] = jnp.where(flip, own, far)
    for j in range(n):
        total = None
        for c, (first, depth, starts) in enumerate(parts):
            start = starts[j]
            term = dot_nt(both_ref[:, first : first + depth], g_refs[c * n + j][:, start : start + depth])
            total = term if total is None else total + term
        keep_ref[j] = total[:rows].astype(BF16)
        send_ref[j] = total[rows:].astype(BF16)


def gradient_products(place, w, mid, end, parts):
    rows, depth = w.shape
    n, tokens = len(parts[0][0]), parts[0][0][0].shape[0]
    blocks = [a for part in parts for a in part[0]]
    return pl.pallas_call(
        functools.partial(products_kernel, n, [(first, wide, starts) for _, starts, first, wide in parts]),
        in_specs=[SCALAR] + [VECTOR] * (3 + len(blocks)),
        out_specs=[VECTOR] * 2,
        out_shape=[jax.ShapeDtypeStruct((n, rows, tokens), BF16)] * 2,
        scratch_shapes=[pltpu.VMEM((2 * rows, depth), BF16)],
        compiler_params=pltpu.CompilerParams(vmem_limit_bytes=16 << 20),
        cost_estimate=pl.CostEstimate(flops=1000, bytes_accessed=1000, transcendentals=0),
        name="gradient_products",
    )(place, w, mid, end, *blocks)


def weight_kernel(n, starts, parts, place, own_ref, other_ref, *refs):
    g_refs, far_refs, kept_ref, both_ref = refs[:n], refs[n:-2], refs[-2], refs[-1]
    rows, tokens = own_ref.shape[1:]
    flip = place[2] == 1
    for j in range(n):
        cols = slice(j * tokens, (j + 1) * tokens)
        both_ref[:rows, cols] = jnp.where(flip, own_ref[j], other_ref[j])
        both_ref[rows:, cols] = jnp.where(flip, other_ref[j], own_ref[j])
    first = 0
    for part, far_ref in zip(parts, far_refs):
        blocks = [g_ref[:, start + first : start + first + part] for g_ref, start in zip(g_refs, starts)]
        total = dot_nn(both_ref[...], jnp.concatenate(blocks, axis=0))
        far_ref[...] = total[:rows].astype(BF16)
        kept_ref[:, first : first + part] = total[rows:]
        first += part


def weight_terms(place, own, other, half, parts):
    n, rows, tokens = own.shape
    depth = sum(parts)
    return pl.pallas_call(
        functools.partial(weight_kernel, n, half[1], parts),
        in_specs=[SCALAR] + [VECTOR] * (2 + n),
        out_specs=[VECTOR] * (len(parts) + 1),
        out_shape=[jax.ShapeDtypeStruct((rows, part), BF16) for part in parts]
        + [jax.ShapeDtypeStruct((rows, depth), F32)],
        scratch_shapes=[pltpu.VMEM((2 * rows, n * tokens), BF16)],
        compiler_params=pltpu.CompilerParams(vmem_limit_bytes=16 << 20),
        cost_estimate=pl.CostEstimate(flops=1000, bytes_accessed=1000, transcendentals=0),
        name="weight_terms",
    )(place, own, other, *half[0])


def finish_kernel(n, scale, *refs):
    kept_refs, far_refs, out_ref = refs[:n], refs[n:-1], refs[-1]
    for group, cast in ((kept_refs, False), (far_refs, True)):
        first = 0
        for ref in group:
            last = first + ref.shape[1]
            if cast:
                out_ref[:, first:last] = (out_ref[:, first:last] + ref[...].astype(F32)) * scale
            else:
                out_ref[:, first:last] = ref[...]
            first = last


def finish(kept, far, scale):
    rows, depth = kept[0].shape[0], sum(a.shape[1] for a in kept)
    tile = rows // 4

    def block(a):
        return pl.BlockSpec((tile, a.shape[1]), lambda i: (i, 0))

    return pl.pallas_call(
        functools.partial(finish_kernel, len(kept), scale),
        grid=(rows // tile,),
        in_specs=[block(a) for a in (*kept, *far)],
        out_specs=pl.BlockSpec((tile, depth), lambda i: (i, 0)),
        out_shape=jax.ShapeDtypeStruct((rows, depth), F32),
        compiler_params=pltpu.CompilerParams(vmem_limit_bytes=16 << 20),
        cost_estimate=pl.CostEstimate(flops=1000, bytes_accessed=1000, transcendentals=0),
        name="finish",
    )(*kept, *far)


def xor(k):
    return [(j, j ^ k) for j in range(16)]


CORE, CROSS, PLANE = xor(1), xor(2), xor(4)
FAR = xor(12)
MIDDLE = [pair for pair in FAR if 4 <= pair[0] < 12]
ENDS = [pair for pair in FAR if not 4 <= pair[0] < 12]


def move(a, perm, name):
    with jax.named_scope(name):
        return lax.ppermute(a, "fsdp", perm)


def swap(a, name):
    with jax.named_scope(name):
        return lax.ppermute(a, "seq", [(0, 1), (1, 0)])


def local_grid(queries, keys, values, image_ids, q_gain, k_gain, w_out, grad_y):
    y = lax.axis_index("seq")
    f = lax.axis_index("fsdp")
    middle = (f >> 3) ^ ((f >> 2) & 1)
    place = jnp.stack([y, f & 7, (f >> 3) ^ y, middle]).astype(jnp.int32)
    dim = q_gain.shape[0]
    tokens = image_ids.shape[1]
    half = queries.shape[1] // 2
    row, col = image_ids, image_ids.reshape(tokens, 1)
    qg, kg = q_gain.reshape(1, dim), k_gain.reshape(1, dim)
    barrier = lax.optimization_barrier
    width = grad_y.shape[1]
    cut = 2 * width // 3

    width = grad_y.shape[1]
    cut = 2 * width // 3
    barrier = lax.optimization_barrier

    mine, send = pack(place, (queries, keys, values))
    send, gy, w_own = barrier((send, grad_y, w_out))
    came = swap(send, "qkv_seq")
    g4 = move(gy, PLANE, "gy_plane")
    g2 = move(gy, CROSS, "gy_cross")
    w_mid = move(w_own, MIDDLE, "w_middle")
    g1 = move(gy, CORE, "gy_core")
    even, odd = attention_forward(place, mine, came, row, col, qg, kg)
    odd = move(odd, CORE, "att_core")
    even, odd, g2, g4, gy, w_own, w_mid, g1 = barrier((even, odd, g2, g4, gy, w_own, w_mid, g1))
    own = [jnp.stack([even[j], odd[j]]) for j in range(4)]
    other = [swap(own[0], "att_seq")]
    own = [own[0]] + [move(own[j], xor(2 * j), "att_group") for j in (1, 2, 3)]
    g4a, g4b = g4[:, :cut], g4[:, cut:]
    held, w_held = hold(gy, w_own)
    own, other, g4, g4a, g4b, w_own, g2, gy, w_held = barrier((own, other, g4, g4a, g4b, w_own, g2, held, w_held))
    other.append(swap(jnp.concatenate(own[1:]), "att_seq"))
    g6a = move(g4a, CROSS, "gy_plane_cross_a")
    w_end = move(w_own, ENDS, "w_ends")
    g3, g5 = (move(g, CORE, "gy_core") for g in (g2, g4))
    saved = attention_prepare(place, mine, came, row, col, qg, kg)
    own, other = jnp.concatenate(own), jnp.concatenate(other)
    own, other, g6a, g3, g5, g4b, w_end, saved = barrier((own, other, g6a, g3, g5, g4b, w_end, saved))
    g6b = move(g4b, CROSS, "gy_plane_cross_b")
    g7a = move(g6a, CORE, "gy_core")
    blocks_a = [gy, g1, g2, g3, g4, g5, g6a, g7a]
    *sent, kept_a = weight_terms(place, own, other, (blocks_a, (0,) * 8), (cut // 4, cut // 2, cut // 4))
    far = [move(sent[0], FAR, "grad_w_far")]
    weights = (w_held, w_mid, w_end)
    tied = barrier((gy, g2, g1, g3, sent))[:4]
    keep0, send0 = gradient_products(place, *weights, [(tied, (start,) * 4, start, depth) for start, depth in ((0, cut), (cut, width - cut))])
    g6b, far, sent, kept_a, keep0, send0 = barrier((g6b, far, sent, kept_a, keep0, send0))
    came0 = swap(send0, "products_seq")
    far.append(move(sent[1], FAR, "grad_w_far"))
    g7b = move(g6b, CORE, "gy_core")
    keep1, send1 = gradient_products(
        place,
        *weights,
        [([g4, g6a, g5, g7a], (0,) * 4, 0, cut), ([g4, g6b, g5, g7b], (cut, 0, cut, 0), cut, width - cut)],
    )
    came1 = swap(send1, "products_seq")
    came0, keep1, blocks_b = barrier((came0, keep1, [gy, g1, g2, g3, g4, g5, g6b, g7b]))
    summed0 = (keep0.astype(F32) + came0.astype(F32)).astype(BF16)
    odd = move(summed0[2:], CORE, "products_core")
    near = [jnp.stack([summed0[j], odd[j]]) for j in range(2)]
    near[1] = move(near[1], xor(2), "products_group")
    starts_b = (cut,) * 6 + (0,) * 2
    *sent_b, kept_b = weight_terms(place, own, other, (blocks_b, starts_b), (width - cut,))
    far, near, keep1, came1, sent, sent_b, kept_b = barrier((far, near, keep1, came1, sent, sent_b, kept_b))
    summed1 = (keep1.astype(F32) + came1.astype(F32)).astype(BF16)
    odd = move(summed1[2:], CORE, "products_core")
    next_plane = [jnp.stack([summed1[j], odd[j]]) for j in range(2)]
    next_plane = [move(next_plane[j], xor(4 + 2 * j), "products_group") for j in range(2)]
    far += [move(part, FAR, "grad_w_far") for part in (sent[2], *sent_b)]
    grads = attention_backward(place, 0, 2, saved, jnp.stack(near), qg, kg)
    grads = attention_backward(place, 2, 2, saved, jnp.stack(next_plane), qg, kg, tuple(grads))

    grad_w = finish((kept_a, kept_b), far, tokens ** (-0.5))
    return (*(g.transpose(1, 0, 2) for g in grads), grad_w)


def solution(mesh):
    in_specs = (
        P(("fsdp", "seq"), None),
        P(("fsdp", "seq"), None),
        P(("fsdp", "seq"), None),
        P("fsdp", None),
        P(),
        P(),
        P("fsdp", "seq"),
        P("fsdp", "seq"),
    )
    out_specs = (
        P("fsdp", "seq", None),
        P("fsdp", "seq", None),
        P("fsdp", "seq", None),
        P("fsdp", "seq"),
    )
    grid = mesh.shape["fsdp"] == 16 and mesh.shape["seq"] == 2
    local = local_grid if grid else local_any
    return jax.shard_map(local, mesh=mesh, in_specs=in_specs, out_specs=out_specs, check_vma=False)
```

```python
import functools

import jax
import jax.numpy as jnp
from jax import lax
from jax.experimental import pallas as pl
from jax.experimental.pallas import tpu as pltpu
from jax.sharding import PartitionSpec as P

F32 = jnp.float32
BF16 = jnp.bfloat16


def norm_parts(source, gain):
    wide = source.astype(jnp.float32)
    centred = wide - jnp.mean(wide, axis=-1, keepdims=True)
    scale_inv = lax.rsqrt(jnp.mean(centred * centred, axis=-1, keepdims=True) + 1e-06)
    x_hat = centred * scale_inv
    return (x_hat, scale_inv, (x_hat * gain).astype(jnp.bfloat16))


def norm_back(grad_n, x_hat, scale_inv, gain):
    scaled = grad_n * gain
    return scale_inv * (
        scaled
        - jnp.mean(scaled, axis=-1, keepdims=True)
        - x_hat * jnp.mean(scaled * x_hat, axis=-1, keepdims=True)
    )


def probabilities(normalized_queries, normalized_keys, same_image, scale_factor):
    scores = (
        jnp.einsum(
            "krt,irt->rki", normalized_queries, normalized_keys, preferred_element_type=jnp.float32
        )
        * scale_factor
    )
    scores = jnp.where(same_image[None], scores, -1e30)
    row_top = jnp.max(scores, axis=-1, keepdims=True)
    exp_terms = jnp.exp(scores - row_top)
    return exp_terms / jnp.sum(exp_terms, axis=-1, keepdims=True)


def local_any(queries, keys, values, image_ids, q_gain, k_gain, w_out, grad_y):
    head_dim = q_gain.shape[0]
    tok_rows = queries.shape[0]
    heads_all = queries.shape[1] // head_dim
    scale_factor = head_dim ** (-0.5)
    q_patch = queries.reshape(tok_rows, heads_all, head_dim)
    k_patch = keys.reshape(tok_rows, heads_all, head_dim)
    v_patch = values.reshape(tok_rows, heads_all, head_dim)
    q_local, k_local, value_shard = (
        lax.all_to_all(q_patch, "seq", split_axis=1, concat_axis=0, tiled=True),
        lax.all_to_all(k_patch, "seq", split_axis=1, concat_axis=0, tiled=True),
        lax.all_to_all(v_patch, "seq", split_axis=1, concat_axis=0, tiled=True),
    )
    seq_length = q_local.shape[0]
    local_heads = q_local.shape[1]
    image_row = image_ids[0]
    same_image = image_row[:, None] == image_row[None, :]
    q_hat, q_inv, normalized_queries = norm_parts(q_local, q_gain)
    k_hat, k_inv, normalized_keys = norm_parts(k_local, k_gain)
    prob_rows = probabilities(normalized_queries, normalized_keys, same_image, scale_factor)
    probs_reduced_precision = prob_rows.astype(jnp.bfloat16)
    attended = jnp.einsum(
        "tgi,itp->gtp", probs_reduced_precision, value_shard, preferred_element_type=jnp.float32
    ).astype(jnp.bfloat16)
    attended_flat = attended.reshape(seq_length, local_heads * head_dim)
    partial_g = jnp.einsum(
        "ld,cd->lc",
        grad_y,
        lax.all_gather(w_out, "fsdp", axis=0, tiled=True),
        preferred_element_type=jnp.float32,
    )
    grad_sum = lax.psum_scatter(
        partial_g.astype(jnp.bfloat16), "seq", scatter_dimension=1, tiled=True
    )
    attention_gradient = grad_sum.reshape(seq_length, local_heads, head_dim)
    grad_values = jnp.einsum(
        "jpw,pjy->wjy",
        probs_reduced_precision,
        attention_gradient,
        preferred_element_type=jnp.float32,
    ).astype(jnp.bfloat16)
    probability_gradient = jnp.einsum(
        "krt,irt->rki", attention_gradient, value_shard, preferred_element_type=jnp.float32
    )
    row_delta = jnp.sum(prob_rows * probability_gradient, axis=-1, keepdims=True)
    score_gradient = (prob_rows * (probability_gradient - row_delta) * scale_factor).astype(
        jnp.bfloat16
    )
    normed_query_gradient = jnp.einsum(
        "tgi,itp->gtp", score_gradient, normalized_keys, preferred_element_type=jnp.float32
    )
    normed_key_gradient = jnp.einsum(
        "jpw,pjy->wjy", score_gradient, normalized_queries, preferred_element_type=jnp.float32
    )
    grad_queries = norm_back(normed_query_gradient, q_hat, q_inv, q_gain).astype(jnp.bfloat16)
    grad_keys = norm_back(normed_key_gradient, k_hat, k_inv, k_gain).astype(jnp.bfloat16)
    partial_w = jnp.einsum(
        "lc,ld->cd",
        lax.all_gather(attended_flat, "seq", axis=1, tiled=True),
        grad_y,
        preferred_element_type=jnp.float32,
    )
    summed = lax.psum_scatter(partial_w, "fsdp", scatter_dimension=0, tiled=True)
    grad_w = summed * seq_length ** (-0.5)
    return (grad_queries, grad_keys, grad_values, grad_w)


def dot_nt(a, b):
    return lax.dot_general(a, b, (((1,), (1,)), ((), ())), preferred_element_type=F32)


def dot_tn(a, b):
    return lax.dot_general(a, b, (((0,), (0,)), ((), ())), preferred_element_type=F32)


def dot_nn(a, b):
    return jnp.dot(a, b, preferred_element_type=F32)


def assemble(first, own, came):
    return jnp.concatenate([jnp.where(first, own, came), jnp.where(first, came, own)], axis=0)


def head_probs(q, k, qg, kg, same, scale):
    q_hat, q_inv, qn = norm_parts(q, qg)
    k_hat, k_inv, kn = norm_parts(k, kg)
    scores = jnp.where(same, dot_nt(qn, kn) * scale, -1e30)
    exp_terms = jnp.exp(scores - jnp.max(scores, axis=-1, keepdims=True))
    probs = exp_terms / jnp.sum(exp_terms, axis=-1, keepdims=True)
    return probs, q_hat, q_inv, qn, k_hat, k_inv, kn


def probabilities_kernel(per, dim, place, q_ref, k_ref, came_ref, row_ref, col_ref, qg_ref, kg_ref, p_ref, hat_ref, inv_ref, low_ref, p_low_ref):
    same = col_ref[...] == row_ref[...]
    first = place[0] == 0
    for h in range(per):
        cols = slice(h * dim, (h + 1) * dim)
        q, k = (assemble(first, ref[:, cols], came_ref[n, :, cols]) for n, ref in enumerate((q_ref, k_ref)))
        probs, *parts = head_probs(q, k, qg_ref[...], kg_ref[...], same, dim**-0.5)
        p_ref[h] = probs
        p_low_ref[h] = probs.astype(BF16)
        for n, (hat, inv, normed) in enumerate((parts[:3], parts[3:])):
            hat_ref[n, h] = hat
            inv_ref[n, h] = jnp.broadcast_to(inv, hat.shape)
            low_ref[n, h] = normed


def attended_kernel(per, dim, place, p_low_ref, v_ref, came_ref, even_ref, odd_ref, whole_ref):
    first = place[0] == 0
    done = []
    for h in range(per):
        cols = slice(h * dim, (h + 1) * dim)
        v = assemble(first, v_ref[:, cols], came_ref[:, cols])
        whole_ref[h] = v
        done.append(dot_nn(p_low_ref[h], v).T.astype(BF16))
    att = jnp.concatenate(done, axis=0)
    half = att.shape[0] // 2
    straight = (place[1] & 1) == 0
    low, high = att[:half], att[half:]
    even_ref[0] = jnp.where(straight, low, high)
    odd_ref[0] = jnp.where(straight, high, low)


def backward_kernel(per, dim, n_into, place, p_ref, hat_ref, inv_ref, low_ref, v_ref, d_ref, qg_ref, kg_ref, *rest):
    gq_ref, gk_ref, gv_ref = rest[n_into:]
    scale = dim**-0.5
    straight = (place[1] & 1) == 0
    one, two = d_ref[0, 0], d_ref[0, 1]
    grad = jnp.concatenate([jnp.where(straight, one, two), jnp.where(straight, two, one)], axis=0)
    qg, kg = qg_ref[...], kg_ref[...]
    for h in range(per):
        probs, qn, kn, v = p_ref[h], low_ref[0, h], low_ref[1, h], v_ref[h]
        d = grad[h * dim : (h + 1) * dim].T
        gp = dot_nt(d, v)
        gv_ref[h] = dot_tn(probs.astype(BF16), d).astype(BF16)
        delta = jnp.sum(probs * gp, axis=-1, keepdims=True)
        gs = (probs * (gp - delta) * scale).astype(BF16)
        gq_ref[h] = norm_back(dot_nn(gs, kn), hat_ref[0, h], inv_ref[0, h], qg).astype(BF16)
        gk_ref[h] = norm_back(dot_tn(gs, qn), hat_ref[1, h], inv_ref[1, h], kg).astype(BF16)


def whole(shape):
    return pl.BlockSpec(shape, lambda *_: (0,) * len(shape))


def pair_index(i, p):
    return i ^ (p[1] >> 1) ^ (p[2] << 1)


def own_heads(rows, wide):
    return pl.BlockSpec((rows, wide), lambda i, p: (0, p[0] * 4 + i))


def in_hbm(a):
    return pltpu.with_memory_space_constraint(a, pltpu.HBM)


def attention_probabilities(place, queries, keys, came, row, col, qg, kg):
    dim = qg.shape[1]
    half_tokens, heads = came.shape[1], came.shape[2] // dim
    tokens, per = 2 * half_tokens, heads // 4
    wide = per * dim

    def saved(n, dtype):
        spec = pl.BlockSpec((n, per, tokens, dim), lambda i, p: (0, i, 0, 0))
        return spec, pltpu.HBM((n, heads, tokens, dim), dtype)

    square, probs = pl.BlockSpec((per, tokens, tokens), lambda i, p: (i, 0, 0)), (heads, tokens, tokens)
    specs, shapes = zip(
        (square, pltpu.HBM(probs, F32)),
        saved(2, F32),
        saved(2, F32),
        saved(2, BF16),
        (square, jax.ShapeDtypeStruct(probs, BF16)),
    )
    *saved, low = pl.pallas_call(
        functools.partial(probabilities_kernel, per, dim),
        grid_spec=pltpu.PrefetchScalarGridSpec(
            num_scalar_prefetch=1,
            grid=(4,),
            in_specs=[own_heads(half_tokens, wide)] * 2
            + [pl.BlockSpec((2, half_tokens, wide), lambda i, p: (0, 0, i))]
            + [whole((1, tokens)), whole((tokens, 1)), whole((1, dim)), whole((1, dim))],
            out_specs=specs,
        ),
        out_shape=shapes,
        compiler_params=pltpu.CompilerParams(vmem_limit_bytes=16 << 20),
        cost_estimate=pl.CostEstimate(flops=1000, bytes_accessed=1000, transcendentals=0),
        name="attention_probabilities",
    )(place, in_hbm(queries), in_hbm(keys), came, row, col, qg, kg)
    return saved, low


def attention_attended(place, low, values, came, dim):
    half_tokens, heads = came.shape[0], low.shape[0]
    tokens, per = 2 * half_tokens, heads // 4
    rows, wide = per * dim // 2, per * dim
    out = pl.BlockSpec((1, rows, tokens), lambda i, p: (pair_index(i, p), 0, 0))
    return pl.pallas_call(
        functools.partial(attended_kernel, per, dim),
        grid_spec=pltpu.PrefetchScalarGridSpec(
            num_scalar_prefetch=1,
            grid=(4,),
            in_specs=[pl.BlockSpec((per, tokens, tokens), lambda i, p: (i, 0, 0))]
            + [own_heads(half_tokens, wide), pl.BlockSpec((half_tokens, wide), lambda i, p: (0, i))],
            out_specs=[out, out, pl.BlockSpec((per, tokens, dim), lambda i, p: (i, 0, 0))],
        ),
        out_shape=[jax.ShapeDtypeStruct((4, rows, tokens), BF16)] * 2 + [pltpu.HBM((heads, tokens, dim), BF16)],
        compiler_params=pltpu.CompilerParams(vmem_limit_bytes=16 << 20),
        cost_estimate=pl.CostEstimate(flops=1000, bytes_accessed=1000, transcendentals=0),
        name="attention_attended",
    )(place, low, in_hbm(values), came)


def attention_backward(place, first, pairs, saved, grads, qg, kg, into=()):
    heads, tokens = saved[0].shape[:2]
    dim, per, rows = qg.shape[1], heads // 4, grads.shape[2]

    def index(i, p):
        return pair_index(i + first, p)

    def block(n):
        return pl.BlockSpec((n, per, tokens, dim), lambda i, p: (0, index(i, p), 0, 0))

    return pl.pallas_call(
        functools.partial(backward_kernel, per, dim, len(into)),
        grid_spec=pltpu.PrefetchScalarGridSpec(
            num_scalar_prefetch=1,
            grid=(pairs,),
            in_specs=[pl.BlockSpec((per, tokens, tokens), lambda i, p: (index(i, p), 0, 0)), block(2), block(2), block(2)]
            + [pl.BlockSpec((per, tokens, dim), lambda i, p: (index(i, p), 0, 0))]
            + [pl.BlockSpec((1, 2, rows, tokens), lambda i, p: (i, 0, 0, 0))]
            + [whole((1, dim)), whole((1, dim))]
            + [pl.BlockSpec(memory_space=pl.ANY)] * len(into),
            out_specs=[pl.BlockSpec((per, tokens, dim), lambda i, p: (index(i, p), 0, 0))] * 3,
        ),
        out_shape=[pltpu.HBM((heads, tokens, dim), BF16)] * 3,
        input_output_aliases={9 + n: n for n in range(len(into))},
        compiler_params=pltpu.CompilerParams(vmem_limit_bytes=16 << 20),
        cost_estimate=pl.CostEstimate(flops=1000, bytes_accessed=1000, transcendentals=0),
        name="attention_backward",
    )(place, *saved, grads, qg, kg, *into)


VECTOR = pl.BlockSpec(memory_space=pltpu.VMEM)
SCALAR = pl.BlockSpec(memory_space=pltpu.SMEM)


def hold_kernel(*refs):
    n = len(refs) // 2
    for source, held in zip(refs[:n], refs[n:]):
        held[...] = source[...]


def hold(*arrays, steps=4):
    specs = [pl.BlockSpec((a.shape[0] // steps, a.shape[1]), lambda i: (i, 0)) for a in arrays]
    return pl.pallas_call(
        hold_kernel,
        grid=(steps,),
        in_specs=specs,
        out_specs=specs,
        out_shape=[pltpu.VMEM(a.shape, a.dtype) for a in arrays],
        compiler_params=pltpu.CompilerParams(vmem_limit_bytes=16 << 20),
        cost_estimate=pl.CostEstimate(flops=1000, bytes_accessed=1000, transcendentals=0),
        name="hold",
    )(*arrays)


def choose_kernel(place, mid_ref, end_ref, far_ref):
    far_ref[...] = jnp.where(place[3] == 1, mid_ref[...], end_ref[...])


def choose(place, mid, end):
    return pl.pallas_call(
        choose_kernel,
        in_specs=[SCALAR, VECTOR, VECTOR],
        out_specs=VECTOR,
        out_shape=pltpu.VMEM(mid.shape, mid.dtype),
        compiler_params=pltpu.CompilerParams(vmem_limit_bytes=4 << 20),
        cost_estimate=pl.CostEstimate(flops=10**10, bytes_accessed=1000, transcendentals=0),
        name="choose",
    )(place, mid, end)


def products_kernel(n, parts, place, w_ref, far_ref, *refs):
    g_refs, (keep_ref, send_ref, both_ref) = refs[:-3], refs[-3:]
    rows = w_ref.shape[0]
    flip = place[2] == 1
    for first, depth, _ in parts:
        cols = slice(first, first + depth)
        own, far = w_ref[:, cols], far_ref[:, cols]
        both_ref[:rows, cols] = jnp.where(flip, far, own)
        both_ref[rows:, cols] = jnp.where(flip, own, far)
    for j in range(n):
        total = None
        for c, (first, depth, starts) in enumerate(parts):
            start = starts[j]
            term = dot_nt(both_ref[:, first : first + depth], g_refs[c * n + j][:, start : start + depth])
            total = term if total is None else total + term
        keep_ref[j] = total[:rows].astype(BF16)
        send_ref[j] = total[rows:].astype(BF16)


def gradient_products(place, w, far, parts):
    rows, depth = w.shape
    n, tokens = len(parts[0][0]), parts[0][0][0].shape[0]
    blocks = [a for part in parts for a in part[0]]
    return pl.pallas_call(
        functools.partial(products_kernel, n, [(first, wide, starts) for _, starts, first, wide in parts]),
        in_specs=[SCALAR] + [VECTOR] * (2 + len(blocks)),
        out_specs=[VECTOR] * 2,
        out_shape=[jax.ShapeDtypeStruct((n, rows, tokens), BF16)] * 2,
        scratch_shapes=[pltpu.VMEM((2 * rows, depth), BF16)],
        compiler_params=pltpu.CompilerParams(vmem_limit_bytes=16 << 20),
        cost_estimate=pl.CostEstimate(flops=1000, bytes_accessed=1000, transcendentals=0),
        name="gradient_products",
    )(place, w, far, *blocks)


def weight_kernel(n, starts, parts, place, own_ref, other_ref, *refs):
    g_refs, far_refs, kept_ref, both_ref = refs[:n], refs[n:-2], refs[-2], refs[-1]
    rows, tokens = own_ref.shape[1:]
    flip = place[2] == 1
    for j in range(n):
        cols = slice(j * tokens, (j + 1) * tokens)
        both_ref[:rows, cols] = jnp.where(flip, own_ref[j], other_ref[j])
        both_ref[rows:, cols] = jnp.where(flip, other_ref[j], own_ref[j])
    first = 0
    for part, far_ref in zip(parts, far_refs):
        blocks = [g_ref[:, start + first : start + first + part] for g_ref, start in zip(g_refs, starts)]
        total = dot_nn(both_ref[...], jnp.concatenate(blocks, axis=0))
        far_ref[...] = total[:rows].astype(BF16)
        kept_ref[:, first : first + part] = total[rows:]
        first += part


def weight_terms(place, own, other, half, parts, flops):
    n, rows, tokens = own.shape
    depth = sum(parts)
    return pl.pallas_call(
        functools.partial(weight_kernel, n, half[1], parts),
        in_specs=[SCALAR] + [VECTOR] * (2 + n),
        out_specs=[VECTOR] * (len(parts) + 1),
        out_shape=[jax.ShapeDtypeStruct((rows, part), BF16) for part in parts]
        + [jax.ShapeDtypeStruct((rows, depth), F32)],
        scratch_shapes=[pltpu.VMEM((2 * rows, n * tokens), BF16)],
        compiler_params=pltpu.CompilerParams(vmem_limit_bytes=16 << 20),
        cost_estimate=pl.CostEstimate(flops=flops, bytes_accessed=1000, transcendentals=0),
        name="weight_terms",
    )(place, own, other, *half[0])


def finish_kernel(n, scale, *refs):
    kept_refs, far_refs, out_ref = refs[:n], refs[n:-1], refs[-1]
    for group, cast in ((kept_refs, False), (far_refs, True)):
        first = 0
        for ref in group:
            last = first + ref.shape[1]
            if cast:
                out_ref[:, first:last] = (out_ref[:, first:last] + ref[...].astype(F32)) * scale
            else:
                out_ref[:, first:last] = ref[...]
            first = last


def finish(kept, far, scale):
    rows, depth = kept[0].shape[0], sum(a.shape[1] for a in kept)
    tile = rows // 4

    def block(a):
        return pl.BlockSpec((tile, a.shape[1]), lambda i: (i, 0))

    return pl.pallas_call(
        functools.partial(finish_kernel, len(kept), scale),
        grid=(rows // tile,),
        in_specs=[block(a) for a in (*kept, *far)],
        out_specs=pl.BlockSpec((tile, depth), lambda i: (i, 0)),
        out_shape=jax.ShapeDtypeStruct((rows, depth), F32),
        compiler_params=pltpu.CompilerParams(vmem_limit_bytes=16 << 20),
        cost_estimate=pl.CostEstimate(flops=1000, bytes_accessed=1000, transcendentals=0),
        name="finish",
    )(*kept, *far)


def xor(k):
    return [(j, j ^ k) for j in range(16)]


CORE, CROSS, PLANE = xor(1), xor(2), xor(4)
FAR = xor(12)
MIDDLE = [pair for pair in FAR if 4 <= pair[0] < 12]
ENDS = [pair for pair in FAR if not 4 <= pair[0] < 12]


def move(a, perm, name):
    with jax.named_scope(name):
        return lax.ppermute(a, "fsdp", perm)


def swap(a, name):
    with jax.named_scope(name):
        return lax.ppermute(a, "seq", [(0, 1), (1, 0)])


def local_grid(queries, keys, values, image_ids, q_gain, k_gain, w_out, grad_y):
    y = lax.axis_index("seq")
    f = lax.axis_index("fsdp")
    middle = (f >> 3) ^ ((f >> 2) & 1)
    place = jnp.stack([y, f & 7, (f >> 3) ^ y, middle]).astype(jnp.int32)
    dim = q_gain.shape[0]
    tokens = image_ids.shape[1]
    half = queries.shape[1] // 2
    row, col = image_ids, image_ids.reshape(tokens, 1)
    qg, kg = q_gain.reshape(1, dim), k_gain.reshape(1, dim)
    barrier = lax.optimization_barrier
    width = grad_y.shape[1]
    cut = 2 * width // 3

    width = grad_y.shape[1]
    cut = 2 * width // 3
    barrier = lax.optimization_barrier

    theirs = [lax.dynamic_slice_in_dim(a, (1 - y) * half, half, axis=1) for a in (queries, keys, values)]
    send, gy, w_own = barrier((jnp.stack(theirs[:2]), grad_y, w_out))
    came = swap(send, "qk_seq")
    came_v = swap(theirs[2], "v_seq")
    g2 = move(gy, CROSS, "gy_cross")
    g4 = move(gy, PLANE, "gy_plane")
    w_mid = move(w_own, MIDDLE, "w_middle")
    saved, low = attention_probabilities(place, queries, keys, came, row, col, qg, kg)
    even, odd, v_all = attention_attended(place, low, values, came_v, dim)
    saved.append(v_all)
    odd = move(odd, CORE, "att_core")
    even, odd, g2, g4, gy, w_own, w_mid = barrier((even, odd, g2, g4, gy, w_own, w_mid))
    own = [jnp.stack([even[j], odd[j]]) for j in range(4)]
    other = [swap(own[0], "att_seq")]
    own = [own[0]] + [move(own[j], xor(2 * j), "att_group") for j in (1, 2, 3)]
    g4a, g4b = g4[:, :cut], g4[:, cut:]
    g1 = move(gy, CORE, "gy_core")
    own, other, g4, g4a, g4b, g2, g1, gy = barrier((own, other, g4, g4a, g4b, g2, g1, gy))
    other.append(swap(jnp.concatenate(own[1:]), "att_seq"))
    g6a = move(g4a, CROSS, "gy_plane_cross_a")
    w_far = choose(place, w_mid, move(w_own, ENDS, "w_ends"))
    g3, g5 = (move(g, CORE, "gy_core") for g in (g2, g4))
    gy, w_held = hold(gy, w_out)
    other[1], gy, w_held = barrier((other[1], gy, w_held))
    own, other = jnp.concatenate(own), jnp.concatenate(other)
    other, g6a = barrier((other, g6a))
    g7a = move(g6a, CORE, "gy_core")
    blocks_a = [gy, g1, g2, g3, g4, g5, g6a, g7a]
    *sent, kept_a = weight_terms(place, own, other, (blocks_a, (0,) * 8), (cut // 2, cut // 2), 1000)
    own, other, g6a, g7a, g3, g5, g4b, w_far, sent, kept_a = barrier(
        (own, other, g6a, g7a, g3, g5, g4b, w_far, sent, kept_a)
    )
    g6b = move(g4b, CROSS, "gy_plane_cross_b")
    far = [move(sent[0], FAR, "grad_w_far")]
    weights = (w_held, w_far)
    near = (gy, g2, g1, g3)
    keep0, send0 = gradient_products(
        place, *weights, [(near, (start,) * 4, start, depth) for start, depth in ((0, cut), (cut, width - cut))]
    )
    came0 = swap(send0, "products_seq")
    g6b, far, sent, keep0, came0 = barrier((g6b, far, sent, keep0, came0))
    g7b = move(g6b, CORE, "gy_core")
    far.append(move(sent[1], FAR, "grad_w_far"))
    keep1, send1 = gradient_products(
        place,
        *weights,
        [((g4, g6a, g5, g7a), (0,) * 4, 0, cut), ((g4, g6b, g5, g7b), (cut, 0, cut, 0), cut, width - cut)],
    )
    came1 = swap(send1, "products_seq")
    came0, keep1, blocks_b = barrier((came0, keep1, [gy, g1, g2, g3, g4, g5, g6b, g7b]))
    summed0 = (keep0.astype(F32) + came0.astype(F32)).astype(BF16)
    odd = move(summed0[2:], CORE, "products_core")
    near = [jnp.stack([summed0[j], odd[j]]) for j in range(2)]
    near[1] = move(near[1], xor(2), "products_group")
    starts_b = (cut,) * 6 + (0,) * 2
    *sent, kept_b = weight_terms(place, own, other, (blocks_b, starts_b), ((width - cut) // 2,) * 2, 1000)
    far, near, keep1, came1, sent, kept_b = barrier((far, near, keep1, came1, sent, kept_b))
    summed1 = (keep1.astype(F32) + came1.astype(F32)).astype(BF16)
    odd = move(summed1[2:], CORE, "products_core")
    next_plane = [jnp.stack([summed1[j], odd[j]]) for j in range(2)]
    next_plane = [move(next_plane[j], xor(4 + 2 * j), "products_group") for j in range(2)]
    odd, sent = barrier((odd, sent))
    far += [move(part, FAR, "grad_w_far") for part in sent]
    grads = attention_backward(place, 0, 2, saved, jnp.stack(near), qg, kg)
    grads = attention_backward(place, 2, 2, saved, jnp.stack(next_plane), qg, kg, tuple(grads))

    grad_w = finish((kept_a, kept_b), far, tokens ** (-0.5))
    return (*(g.transpose(1, 0, 2) for g in grads), grad_w)


def solution(mesh):
    in_specs = (
        P(("fsdp", "seq"), None),
        P(("fsdp", "seq"), None),
        P(("fsdp", "seq"), None),
        P("fsdp", None),
        P(),
        P(),
        P("fsdp", "seq"),
        P("fsdp", "seq"),
    )
    out_specs = (
        P("fsdp", "seq", None),
        P("fsdp", "seq", None),
        P("fsdp", "seq", None),
        P("fsdp", "seq"),
    )
    grid = mesh.shape["fsdp"] == 16 and mesh.shape["seq"] == 2
    local = local_grid if grid else local_any
    return jax.shard_map(local, mesh=mesh, in_specs=in_specs, out_specs=out_specs, check_vma=False)
```

```python
import functools

import jax
import jax.numpy as jnp
from jax import lax
from jax.experimental import pallas as pl
from jax.experimental.pallas import tpu as pltpu
from jax.sharding import PartitionSpec as P

F32 = jnp.float32
BF16 = jnp.bfloat16


def norm_parts(source, gain):
    wide = source.astype(jnp.float32)
    centred = wide - jnp.mean(wide, axis=-1, keepdims=True)
    scale_inv = lax.rsqrt(jnp.mean(centred * centred, axis=-1, keepdims=True) + 1e-06)
    x_hat = centred * scale_inv
    return (x_hat, scale_inv, (x_hat * gain).astype(jnp.bfloat16))


def norm_back(grad_n, x_hat, scale_inv, gain):
    scaled = grad_n * gain
    return scale_inv * (
        scaled
        - jnp.mean(scaled, axis=-1, keepdims=True)
        - x_hat * jnp.mean(scaled * x_hat, axis=-1, keepdims=True)
    )


def probabilities(normalized_queries, normalized_keys, same_image, scale_factor):
    scores = (
        jnp.einsum(
            "krt,irt->rki", normalized_queries, normalized_keys, preferred_element_type=jnp.float32
        )
        * scale_factor
    )
    scores = jnp.where(same_image[None], scores, -1e30)
    row_top = jnp.max(scores, axis=-1, keepdims=True)
    exp_terms = jnp.exp(scores - row_top)
    return exp_terms / jnp.sum(exp_terms, axis=-1, keepdims=True)


def local_any(queries, keys, values, image_ids, q_gain, k_gain, w_out, grad_y):
    head_dim = q_gain.shape[0]
    tok_rows = queries.shape[0]
    heads_all = queries.shape[1] // head_dim
    scale_factor = head_dim ** (-0.5)
    q_patch = queries.reshape(tok_rows, heads_all, head_dim)
    k_patch = keys.reshape(tok_rows, heads_all, head_dim)
    v_patch = values.reshape(tok_rows, heads_all, head_dim)
    q_local, k_local, value_shard = (
        lax.all_to_all(q_patch, "seq", split_axis=1, concat_axis=0, tiled=True),
        lax.all_to_all(k_patch, "seq", split_axis=1, concat_axis=0, tiled=True),
        lax.all_to_all(v_patch, "seq", split_axis=1, concat_axis=0, tiled=True),
    )
    seq_length = q_local.shape[0]
    local_heads = q_local.shape[1]
    image_row = image_ids[0]
    same_image = image_row[:, None] == image_row[None, :]
    q_hat, q_inv, normalized_queries = norm_parts(q_local, q_gain)
    k_hat, k_inv, normalized_keys = norm_parts(k_local, k_gain)
    prob_rows = probabilities(normalized_queries, normalized_keys, same_image, scale_factor)
    probs_reduced_precision = prob_rows.astype(jnp.bfloat16)
    attended = jnp.einsum(
        "tgi,itp->gtp", probs_reduced_precision, value_shard, preferred_element_type=jnp.float32
    ).astype(jnp.bfloat16)
    attended_flat = attended.reshape(seq_length, local_heads * head_dim)
    partial_g = jnp.einsum(
        "ld,cd->lc",
        grad_y,
        lax.all_gather(w_out, "fsdp", axis=0, tiled=True),
        preferred_element_type=jnp.float32,
    )
    grad_sum = lax.psum_scatter(
        partial_g.astype(jnp.bfloat16), "seq", scatter_dimension=1, tiled=True
    )
    attention_gradient = grad_sum.reshape(seq_length, local_heads, head_dim)
    grad_values = jnp.einsum(
        "jpw,pjy->wjy",
        probs_reduced_precision,
        attention_gradient,
        preferred_element_type=jnp.float32,
    ).astype(jnp.bfloat16)
    probability_gradient = jnp.einsum(
        "krt,irt->rki", attention_gradient, value_shard, preferred_element_type=jnp.float32
    )
    row_delta = jnp.sum(prob_rows * probability_gradient, axis=-1, keepdims=True)
    score_gradient = (prob_rows * (probability_gradient - row_delta) * scale_factor).astype(
        jnp.bfloat16
    )
    normed_query_gradient = jnp.einsum(
        "tgi,itp->gtp", score_gradient, normalized_keys, preferred_element_type=jnp.float32
    )
    normed_key_gradient = jnp.einsum(
        "jpw,pjy->wjy", score_gradient, normalized_queries, preferred_element_type=jnp.float32
    )
    grad_queries = norm_back(normed_query_gradient, q_hat, q_inv, q_gain).astype(jnp.bfloat16)
    grad_keys = norm_back(normed_key_gradient, k_hat, k_inv, k_gain).astype(jnp.bfloat16)
    partial_w = jnp.einsum(
        "lc,ld->cd",
        lax.all_gather(attended_flat, "seq", axis=1, tiled=True),
        grad_y,
        preferred_element_type=jnp.float32,
    )
    summed = lax.psum_scatter(partial_w, "fsdp", scatter_dimension=0, tiled=True)
    grad_w = summed * seq_length ** (-0.5)
    return (grad_queries, grad_keys, grad_values, grad_w)


def dot_nt(a, b):
    return lax.dot_general(a, b, (((1,), (1,)), ((), ())), preferred_element_type=F32)


def dot_tn(a, b):
    return lax.dot_general(a, b, (((0,), (0,)), ((), ())), preferred_element_type=F32)


def dot_nn(a, b):
    return jnp.dot(a, b, preferred_element_type=F32)


def assemble(first, own, came):
    return jnp.concatenate([jnp.where(first, own, came), jnp.where(first, came, own)], axis=0)


def head_probs(q, k, qg, kg, same, scale):
    q_hat, q_inv, qn = norm_parts(q, qg)
    k_hat, k_inv, kn = norm_parts(k, kg)
    scores = jnp.where(same, dot_nt(qn, kn) * scale, -1e30)
    exp_terms = jnp.exp(scores - jnp.max(scores, axis=-1, keepdims=True))
    probs = exp_terms / jnp.sum(exp_terms, axis=-1, keepdims=True)
    return probs, q_hat, q_inv, qn, k_hat, k_inv, kn


def probabilities_kernel(per, dim, place, q_ref, k_ref, came_ref, row_ref, col_ref, qg_ref, kg_ref, p_ref, hat_ref, inv_ref, low_ref, p_low_ref):
    same = col_ref[...] == row_ref[...]
    first = place[0] == 0
    for h in range(per):
        cols = slice(h * dim, (h + 1) * dim)
        q, k = (assemble(first, ref[:, cols], came_ref[n, :, cols]) for n, ref in enumerate((q_ref, k_ref)))
        probs, *parts = head_probs(q, k, qg_ref[...], kg_ref[...], same, dim**-0.5)
        p_ref[h] = probs
        p_low_ref[h] = probs.astype(BF16)
        for n, (hat, inv, normed) in enumerate((parts[:3], parts[3:])):
            hat_ref[n, h] = hat
            inv_ref[n, h] = jnp.broadcast_to(inv, hat.shape)
            low_ref[n, h] = normed


def attended_kernel(per, dim, place, p_low_ref, v_ref, came_ref, even_ref, odd_ref, whole_ref):
    first = place[0] == 0
    done = []
    for h in range(per):
        cols = slice(h * dim, (h + 1) * dim)
        v = assemble(first, v_ref[:, cols], came_ref[:, cols])
        whole_ref[h] = v
        done.append(dot_nn(p_low_ref[h], v).T.astype(BF16))
    att = jnp.concatenate(done, axis=0)
    half = att.shape[0] // 2
    straight = (place[1] & 1) == 0
    low, high = att[:half], att[half:]
    even_ref[0] = jnp.where(straight, low, high)
    odd_ref[0] = jnp.where(straight, high, low)


def backward_kernel(per, dim, n_into, place, p_ref, hat_ref, inv_ref, low_ref, v_ref, d_ref, qg_ref, kg_ref, *rest):
    gq_ref, gk_ref, gv_ref = rest[n_into:]
    scale = dim**-0.5
    straight = (place[1] & 1) == 0
    one, two = d_ref[0, 0], d_ref[0, 1]
    grad = jnp.concatenate([jnp.where(straight, one, two), jnp.where(straight, two, one)], axis=0)
    qg, kg = qg_ref[...], kg_ref[...]
    for h in range(per):
        probs, qn, kn, v = p_ref[h], low_ref[0, h], low_ref[1, h], v_ref[h]
        d = grad[h * dim : (h + 1) * dim].T
        gp = dot_nt(d, v)
        gv_ref[h] = dot_tn(probs.astype(BF16), d).astype(BF16)
        delta = jnp.sum(probs * gp, axis=-1, keepdims=True)
        gs = (probs * (gp - delta) * scale).astype(BF16)
        gq_ref[h] = norm_back(dot_nn(gs, kn), hat_ref[0, h], inv_ref[0, h], qg).astype(BF16)
        gk_ref[h] = norm_back(dot_tn(gs, qn), hat_ref[1, h], inv_ref[1, h], kg).astype(BF16)


def whole(shape):
    return pl.BlockSpec(shape, lambda *_: (0,) * len(shape))


def pair_index(i, p):
    return i ^ (p[1] >> 1) ^ (p[2] << 1)


def own_heads(rows, wide):
    return pl.BlockSpec((rows, wide), lambda i, p: (0, p[0] * 4 + i))


def in_hbm(a):
    return pltpu.with_memory_space_constraint(a, pltpu.HBM)


def attention_probabilities(place, queries, keys, came, row, col, qg, kg):
    dim = qg.shape[1]
    half_tokens, heads = came.shape[1], came.shape[2] // dim
    tokens, per = 2 * half_tokens, heads // 4
    wide = per * dim

    def saved(n, dtype):
        spec = pl.BlockSpec((n, per, tokens, dim), lambda i, p: (0, i, 0, 0))
        return spec, pltpu.HBM((n, heads, tokens, dim), dtype)

    square, probs = pl.BlockSpec((per, tokens, tokens), lambda i, p: (i, 0, 0)), (heads, tokens, tokens)
    specs, shapes = zip(
        (square, pltpu.HBM(probs, F32)),
        saved(2, F32),
        saved(2, F32),
        saved(2, BF16),
        (square, jax.ShapeDtypeStruct(probs, BF16)),
    )
    *saved, low = pl.pallas_call(
        functools.partial(probabilities_kernel, per, dim),
        grid_spec=pltpu.PrefetchScalarGridSpec(
            num_scalar_prefetch=1,
            grid=(4,),
            in_specs=[own_heads(half_tokens, wide)] * 2
            + [pl.BlockSpec((2, half_tokens, wide), lambda i, p: (0, 0, i))]
            + [whole((1, tokens)), whole((tokens, 1)), whole((1, dim)), whole((1, dim))],
            out_specs=specs,
        ),
        out_shape=shapes,
        compiler_params=pltpu.CompilerParams(vmem_limit_bytes=16 << 20),
        cost_estimate=pl.CostEstimate(flops=1000, bytes_accessed=1000, transcendentals=0),
        name="attention_probabilities",
    )(place, in_hbm(queries), in_hbm(keys), came, row, col, qg, kg)
    return saved, low


def attention_attended(place, low, values, came, dim):
    half_tokens, heads = came.shape[0], low.shape[0]
    tokens, per = 2 * half_tokens, heads // 4
    rows, wide = per * dim // 2, per * dim
    out = pl.BlockSpec((1, rows, tokens), lambda i, p: (pair_index(i, p), 0, 0))
    return pl.pallas_call(
        functools.partial(attended_kernel, per, dim),
        grid_spec=pltpu.PrefetchScalarGridSpec(
            num_scalar_prefetch=1,
            grid=(4,),
            in_specs=[pl.BlockSpec((per, tokens, tokens), lambda i, p: (i, 0, 0))]
            + [own_heads(half_tokens, wide), pl.BlockSpec((half_tokens, wide), lambda i, p: (0, i))],
            out_specs=[out, out, pl.BlockSpec((per, tokens, dim), lambda i, p: (i, 0, 0))],
        ),
        out_shape=[jax.ShapeDtypeStruct((4, rows, tokens), BF16)] * 2 + [pltpu.HBM((heads, tokens, dim), BF16)],
        compiler_params=pltpu.CompilerParams(vmem_limit_bytes=16 << 20),
        cost_estimate=pl.CostEstimate(flops=1000, bytes_accessed=1000, transcendentals=0),
        name="attention_attended",
    )(place, low, in_hbm(values), came)


def attention_backward(place, first, pairs, saved, grads, qg, kg, into=()):
    heads, tokens = saved[0].shape[:2]
    dim, per, rows = qg.shape[1], heads // 4, grads.shape[2]

    def index(i, p):
        return pair_index(i + first, p)

    def block(n):
        return pl.BlockSpec((n, per, tokens, dim), lambda i, p: (0, index(i, p), 0, 0))

    return pl.pallas_call(
        functools.partial(backward_kernel, per, dim, len(into)),
        grid_spec=pltpu.PrefetchScalarGridSpec(
            num_scalar_prefetch=1,
            grid=(pairs,),
            in_specs=[pl.BlockSpec((per, tokens, tokens), lambda i, p: (index(i, p), 0, 0)), block(2), block(2), block(2)]
            + [pl.BlockSpec((per, tokens, dim), lambda i, p: (index(i, p), 0, 0))]
            + [pl.BlockSpec((1, 2, rows, tokens), lambda i, p: (i, 0, 0, 0))]
            + [whole((1, dim)), whole((1, dim))]
            + [pl.BlockSpec(memory_space=pl.ANY)] * len(into),
            out_specs=[pl.BlockSpec((per, tokens, dim), lambda i, p: (index(i, p), 0, 0))] * 3,
        ),
        out_shape=[pltpu.HBM((heads, tokens, dim), BF16)] * 3,
        input_output_aliases={9 + n: n for n in range(len(into))},
        compiler_params=pltpu.CompilerParams(vmem_limit_bytes=16 << 20),
        cost_estimate=pl.CostEstimate(flops=1000, bytes_accessed=1000, transcendentals=0),
        name="attention_backward",
    )(place, *saved, grads, qg, kg, *into)


VECTOR = pl.BlockSpec(memory_space=pltpu.VMEM)
SCALAR = pl.BlockSpec(memory_space=pltpu.SMEM)


def hold_kernel(*refs):
    n = len(refs) // 2
    for source, held in zip(refs[:n], refs[n:]):
        held[...] = source[...]


def hold(*arrays, steps=4):
    specs = [pl.BlockSpec((a.shape[0] // steps, a.shape[1]), lambda i: (i, 0)) for a in arrays]
    return pl.pallas_call(
        hold_kernel,
        grid=(steps,),
        in_specs=specs,
        out_specs=specs,
        out_shape=[pltpu.VMEM(a.shape, a.dtype) for a in arrays],
        compiler_params=pltpu.CompilerParams(vmem_limit_bytes=16 << 20),
        cost_estimate=pl.CostEstimate(flops=1000, bytes_accessed=1000, transcendentals=0),
        name="hold",
    )(*arrays)


def choose_kernel(place, mid_ref, end_ref, far_ref):
    far_ref[...] = jnp.where(place[3] == 1, mid_ref[...], end_ref[...])


def choose(place, mid, end):
    return pl.pallas_call(
        choose_kernel,
        in_specs=[SCALAR, VECTOR, VECTOR],
        out_specs=VECTOR,
        out_shape=pltpu.VMEM(mid.shape, mid.dtype),
        compiler_params=pltpu.CompilerParams(vmem_limit_bytes=4 << 20),
        cost_estimate=pl.CostEstimate(flops=10**10, bytes_accessed=1000, transcendentals=0),
        name="choose",
    )(place, mid, end)


def products_kernel(n, parts, place, w_ref, far_ref, *refs):
    g_refs, (keep_ref, send_ref, both_ref) = refs[:-3], refs[-3:]
    rows = w_ref.shape[0]
    flip = place[2] == 1
    for first, depth, _ in parts:
        cols = slice(first, first + depth)
        own, far = w_ref[:, cols], far_ref[:, cols]
        both_ref[:rows, cols] = jnp.where(flip, far, own)
        both_ref[rows:, cols] = jnp.where(flip, own, far)
    for j in range(n):
        total = None
        for c, (first, depth, starts) in enumerate(parts):
            start = starts[j]
            term = dot_nt(both_ref[:, first : first + depth], g_refs[c * n + j][:, start : start + depth])
            total = term if total is None else total + term
        keep_ref[j] = total[:rows].astype(BF16)
        send_ref[j] = total[rows:].astype(BF16)


def gradient_products(place, w, far, parts):
    rows, depth = w.shape
    n, tokens = len(parts[0][0]), parts[0][0][0].shape[0]
    blocks = [a for part in parts for a in part[0]]
    return pl.pallas_call(
        functools.partial(products_kernel, n, [(first, wide, starts) for _, starts, first, wide in parts]),
        in_specs=[SCALAR] + [VECTOR] * (2 + len(blocks)),
        out_specs=[VECTOR] * 2,
        out_shape=[jax.ShapeDtypeStruct((n, rows, tokens), BF16)] * 2,
        scratch_shapes=[pltpu.VMEM((2 * rows, depth), BF16)],
        compiler_params=pltpu.CompilerParams(vmem_limit_bytes=16 << 20),
        cost_estimate=pl.CostEstimate(flops=1000, bytes_accessed=1000, transcendentals=0),
        name="gradient_products",
    )(place, w, far, *blocks)


def weight_kernel(n, starts, parts, place, own_ref, other_ref, *refs):
    g_refs, far_refs, kept_ref, both_ref = refs[:n], refs[n:-2], refs[-2], refs[-1]
    rows, tokens = own_ref.shape[1:]
    flip = place[2] == 1
    for j in range(n):
        cols = slice(j * tokens, (j + 1) * tokens)
        both_ref[:rows, cols] = jnp.where(flip, own_ref[j], other_ref[j])
        both_ref[rows:, cols] = jnp.where(flip, other_ref[j], own_ref[j])
    first = 0
    for part, far_ref in zip(parts, far_refs):
        blocks = [g_ref[:, start + first : start + first + part] for g_ref, start in zip(g_refs, starts)]
        total = dot_nn(both_ref[...], jnp.concatenate(blocks, axis=0))
        far_ref[...] = total[:rows].astype(BF16)
        kept_ref[:, first : first + part] = total[rows:]
        first += part


def weight_terms(place, own, other, half, parts, flops):
    n, rows, tokens = own.shape
    depth = sum(parts)
    return pl.pallas_call(
        functools.partial(weight_kernel, n, half[1], parts),
        in_specs=[SCALAR] + [VECTOR] * (2 + n),
        out_specs=[VECTOR] * (len(parts) + 1),
        out_shape=[jax.ShapeDtypeStruct((rows, part), BF16) for part in parts]
        + [jax.ShapeDtypeStruct((rows, depth), F32)],
        scratch_shapes=[pltpu.VMEM((2 * rows, n * tokens), BF16)],
        compiler_params=pltpu.CompilerParams(vmem_limit_bytes=16 << 20),
        cost_estimate=pl.CostEstimate(flops=flops, bytes_accessed=1000, transcendentals=0),
        name="weight_terms",
    )(place, own, other, *half[0])


def finish_kernel(n, scale, *refs):
    kept_refs, far_refs, out_ref = refs[:n], refs[n:-1], refs[-1]
    for group, cast in ((kept_refs, False), (far_refs, True)):
        first = 0
        for ref in group:
            last = first + ref.shape[1]
            if cast:
                out_ref[:, first:last] = (out_ref[:, first:last] + ref[...].astype(F32)) * scale
            else:
                out_ref[:, first:last] = ref[...]
            first = last


def finish(kept, far, scale):
    rows, depth = kept[0].shape[0], sum(a.shape[1] for a in kept)
    tile = rows // 4

    def block(a):
        return pl.BlockSpec((tile, a.shape[1]), lambda i: (i, 0))

    return pl.pallas_call(
        functools.partial(finish_kernel, len(kept), scale),
        grid=(rows // tile,),
        in_specs=[block(a) for a in (*kept, *far)],
        out_specs=pl.BlockSpec((tile, depth), lambda i: (i, 0)),
        out_shape=jax.ShapeDtypeStruct((rows, depth), F32),
        compiler_params=pltpu.CompilerParams(vmem_limit_bytes=16 << 20),
        cost_estimate=pl.CostEstimate(flops=1000, bytes_accessed=1000, transcendentals=0),
        name="finish",
    )(*kept, *far)


def xor(k):
    return [(j, j ^ k) for j in range(16)]


CORE, CROSS, PLANE = xor(1), xor(2), xor(4)
FAR = xor(12)
MIDDLE = [pair for pair in FAR if 4 <= pair[0] < 12]
ENDS = [pair for pair in FAR if not 4 <= pair[0] < 12]


def move(a, perm, name):
    with jax.named_scope(name):
        return lax.ppermute(a, "fsdp", perm)


def swap(a, name):
    with jax.named_scope(name):
        return lax.ppermute(a, "seq", [(0, 1), (1, 0)])


def local_grid(queries, keys, values, image_ids, q_gain, k_gain, w_out, grad_y):
    y = lax.axis_index("seq")
    f = lax.axis_index("fsdp")
    middle = (f >> 3) ^ ((f >> 2) & 1)
    place = jnp.stack([y, f & 7, (f >> 3) ^ y, middle]).astype(jnp.int32)
    dim = q_gain.shape[0]
    tokens = image_ids.shape[1]
    half = queries.shape[1] // 2
    row, col = image_ids, image_ids.reshape(tokens, 1)
    qg, kg = q_gain.reshape(1, dim), k_gain.reshape(1, dim)
    barrier = lax.optimization_barrier
    width = grad_y.shape[1]
    cut = 2 * width // 3

    width = grad_y.shape[1]
    cut = 2 * width // 3
    barrier = lax.optimization_barrier

    theirs = [lax.dynamic_slice_in_dim(a, (1 - y) * half, half, axis=1) for a in (queries, keys, values)]
    send, gy, w_own = barrier((jnp.stack(theirs[:2]), grad_y, w_out))
    came = swap(send, "qk_seq")
    came_v = swap(theirs[2], "v_seq")
    g2 = move(gy, CROSS, "gy_cross")
    g4 = move(gy, PLANE, "gy_plane")
    w_mid = move(w_own, MIDDLE, "w_middle")
    saved, low = attention_probabilities(place, queries, keys, came, row, col, qg, kg)
    even, odd, v_all = attention_attended(place, low, values, came_v, dim)
    saved.append(v_all)
    odd = move(odd, CORE, "att_core")
    even, odd, g2, g4, gy, w_own, w_mid = barrier((even, odd, g2, g4, gy, w_own, w_mid))
    own = [jnp.stack([even[j], odd[j]]) for j in range(4)]
    other = [swap(own[0], "att_seq")]
    own = [own[0]] + [move(own[j], xor(2 * j), "att_group") for j in (1, 2, 3)]
    g4a, g4b = g4[:, :cut], g4[:, cut:]
    g1 = move(gy, CORE, "gy_core")
    own, other, g4, g4a, g4b, g2, g1, gy = barrier((own, other, g4, g4a, g4b, g2, g1, gy))
    other.append(swap(jnp.concatenate(own[1:]), "att_seq"))
    g6a = move(g4a, CROSS, "gy_plane_cross_a")
    w_far = choose(place, w_mid, move(w_own, ENDS, "w_ends"))
    g3, g5 = (move(g, CORE, "gy_core") for g in (g2, g4))
    gy, w_held = hold(gy, w_out)
    other[1], gy, w_held = barrier((other[1], gy, w_held))
    own, other = jnp.concatenate(own), jnp.concatenate(other)
    other, g6a = barrier((other, g6a))
    g7a = move(g6a, CORE, "gy_core")
    blocks_a = [gy, g1, g2, g3, g4, g5, g6a, g7a]
    *sent, kept_a = weight_terms(place, own, other, (blocks_a, (0,) * 8), (cut // 2, cut // 2), 1000)
    own, other, g6a, g7a, g3, g5, g4b, w_far, sent, kept_a = barrier(
        (own, other, g6a, g7a, g3, g5, g4b, w_far, sent, kept_a)
    )
    g6b = move(g4b, CROSS, "gy_plane_cross_b")
    far = [move(sent[0], FAR, "grad_w_far")]
    weights = (w_held, w_far)
    near = (gy, g2, g1, g3)
    keep0, send0 = gradient_products(
        place, *weights, [(near, (start,) * 4, start, depth) for start, depth in ((0, cut), (cut, width - cut))]
    )
    came0 = swap(send0, "products_seq")
    g6b, far, sent, keep0, came0 = barrier((g6b, far, sent, keep0, came0))
    g7b = move(g6b, CORE, "gy_core")
    far.append(move(sent[1], FAR, "grad_w_far"))
    keep1, send1 = gradient_products(
        place,
        *weights,
        [((g4, g6a, g5, g7a), (0,) * 4, 0, cut), ((g4, g6b, g5, g7b), (cut, 0, cut, 0), cut, width - cut)],
    )
    came1 = swap(send1, "products_seq")
    came0, keep1, blocks_b = barrier((came0, keep1, [gy, g1, g2, g3, g4, g5, g6b, g7b]))
    summed0 = (keep0.astype(F32) + came0.astype(F32)).astype(BF16)
    odd = move(summed0[2:], CORE, "products_core")
    near = [jnp.stack([summed0[j], odd[j]]) for j in range(2)]
    near[1] = move(near[1], xor(2), "products_group")
    starts_b = (cut,) * 6 + (0,) * 2
    *sent, kept_b = weight_terms(place, own, other, (blocks_b, starts_b), ((width - cut) // 2,) * 2, 1000)
    far, near, keep1, came1, sent, kept_b = barrier((far, near, keep1, came1, sent, kept_b))
    summed1 = (keep1.astype(F32) + came1.astype(F32)).astype(BF16)
    odd = move(summed1[2:], CORE, "products_core")
    next_plane = [jnp.stack([summed1[j], odd[j]]) for j in range(2)]
    next_plane = [move(next_plane[j], xor(4 + 2 * j), "products_group") for j in range(2)]
    far += [move(part, FAR, "grad_w_far") for part in sent]
    grads = attention_backward(place, 0, 2, saved, jnp.stack(near), qg, kg)
    grads = attention_backward(place, 2, 2, saved, jnp.stack(next_plane), qg, kg, tuple(grads))

    grad_w = finish((kept_a, kept_b), far, tokens ** (-0.5))
    return (*(g.transpose(1, 0, 2) for g in grads), grad_w)


def solution(mesh):
    in_specs = (
        P(("fsdp", "seq"), None),
        P(("fsdp", "seq"), None),
        P(("fsdp", "seq"), None),
        P("fsdp", None),
        P(),
        P(),
        P("fsdp", "seq"),
        P("fsdp", "seq"),
    )
    out_specs = (
        P("fsdp", "seq", None),
        P("fsdp", "seq", None),
        P("fsdp", "seq", None),
        P("fsdp", "seq"),
    )
    grid = mesh.shape["fsdp"] == 16 and mesh.shape["seq"] == 2
    local = local_grid if grid else local_any
    return jax.shard_map(local, mesh=mesh, in_specs=in_specs, out_specs=out_specs, check_vma=False)
```

```python
import functools

import jax
import jax.numpy as jnp
from jax import lax
from jax.experimental import pallas as pl
from jax.experimental.pallas import tpu as pltpu
from jax.sharding import PartitionSpec as P

F32 = jnp.float32
BF16 = jnp.bfloat16


def norm_parts(source, gain):
    wide = source.astype(jnp.float32)
    centred = wide - jnp.mean(wide, axis=-1, keepdims=True)
    scale_inv = lax.rsqrt(jnp.mean(centred * centred, axis=-1, keepdims=True) + 1e-06)
    x_hat = centred * scale_inv
    return (x_hat, scale_inv, (x_hat * gain).astype(jnp.bfloat16))


def norm_back(grad_n, x_hat, scale_inv, gain):
    scaled = grad_n * gain
    return scale_inv * (
        scaled
        - jnp.mean(scaled, axis=-1, keepdims=True)
        - x_hat * jnp.mean(scaled * x_hat, axis=-1, keepdims=True)
    )


def probabilities(normalized_queries, normalized_keys, same_image, scale_factor):
    scores = (
        jnp.einsum(
            "krt,irt->rki", normalized_queries, normalized_keys, preferred_element_type=jnp.float32
        )
        * scale_factor
    )
    scores = jnp.where(same_image[None], scores, -1e30)
    row_top = jnp.max(scores, axis=-1, keepdims=True)
    exp_terms = jnp.exp(scores - row_top)
    return exp_terms / jnp.sum(exp_terms, axis=-1, keepdims=True)


def local_any(queries, keys, values, image_ids, q_gain, k_gain, w_out, grad_y):
    head_dim = q_gain.shape[0]
    tok_rows = queries.shape[0]
    heads_all = queries.shape[1] // head_dim
    scale_factor = head_dim ** (-0.5)
    q_patch = queries.reshape(tok_rows, heads_all, head_dim)
    k_patch = keys.reshape(tok_rows, heads_all, head_dim)
    v_patch = values.reshape(tok_rows, heads_all, head_dim)
    q_local, k_local, value_shard = (
        lax.all_to_all(q_patch, "seq", split_axis=1, concat_axis=0, tiled=True),
        lax.all_to_all(k_patch, "seq", split_axis=1, concat_axis=0, tiled=True),
        lax.all_to_all(v_patch, "seq", split_axis=1, concat_axis=0, tiled=True),
    )
    seq_length = q_local.shape[0]
    local_heads = q_local.shape[1]
    image_row = image_ids[0]
    same_image = image_row[:, None] == image_row[None, :]
    q_hat, q_inv, normalized_queries = norm_parts(q_local, q_gain)
    k_hat, k_inv, normalized_keys = norm_parts(k_local, k_gain)
    prob_rows = probabilities(normalized_queries, normalized_keys, same_image, scale_factor)
    probs_reduced_precision = prob_rows.astype(jnp.bfloat16)
    attended = jnp.einsum(
        "tgi,itp->gtp", probs_reduced_precision, value_shard, preferred_element_type=jnp.float32
    ).astype(jnp.bfloat16)
    attended_flat = attended.reshape(seq_length, local_heads * head_dim)
    partial_g = jnp.einsum(
        "ld,cd->lc",
        grad_y,
        lax.all_gather(w_out, "fsdp", axis=0, tiled=True),
        preferred_element_type=jnp.float32,
    )
    grad_sum = lax.psum_scatter(
        partial_g.astype(jnp.bfloat16), "seq", scatter_dimension=1, tiled=True
    )
    attention_gradient = grad_sum.reshape(seq_length, local_heads, head_dim)
    grad_values = jnp.einsum(
        "jpw,pjy->wjy",
        probs_reduced_precision,
        attention_gradient,
        preferred_element_type=jnp.float32,
    ).astype(jnp.bfloat16)
    probability_gradient = jnp.einsum(
        "krt,irt->rki", attention_gradient, value_shard, preferred_element_type=jnp.float32
    )
    row_delta = jnp.sum(prob_rows * probability_gradient, axis=-1, keepdims=True)
    score_gradient = (prob_rows * (probability_gradient - row_delta) * scale_factor).astype(
        jnp.bfloat16
    )
    normed_query_gradient = jnp.einsum(
        "tgi,itp->gtp", score_gradient, normalized_keys, preferred_element_type=jnp.float32
    )
    normed_key_gradient = jnp.einsum(
        "jpw,pjy->wjy", score_gradient, normalized_queries, preferred_element_type=jnp.float32
    )
    grad_queries = norm_back(normed_query_gradient, q_hat, q_inv, q_gain).astype(jnp.bfloat16)
    grad_keys = norm_back(normed_key_gradient, k_hat, k_inv, k_gain).astype(jnp.bfloat16)
    partial_w = jnp.einsum(
        "lc,ld->cd",
        lax.all_gather(attended_flat, "seq", axis=1, tiled=True),
        grad_y,
        preferred_element_type=jnp.float32,
    )
    summed = lax.psum_scatter(partial_w, "fsdp", scatter_dimension=0, tiled=True)
    grad_w = summed * seq_length ** (-0.5)
    return (grad_queries, grad_keys, grad_values, grad_w)


def dot_nt(a, b):
    return lax.dot_general(a, b, (((1,), (1,)), ((), ())), preferred_element_type=F32)


def dot_tn(a, b):
    return lax.dot_general(a, b, (((0,), (0,)), ((), ())), preferred_element_type=F32)


def dot_nn(a, b):
    return jnp.dot(a, b, preferred_element_type=F32)


def assemble(first, own, came):
    return jnp.concatenate([jnp.where(first, own, came), jnp.where(first, came, own)], axis=0)


def head_probs(q, k, qg, kg, same, scale):
    q_hat, q_inv, qn = norm_parts(q, qg)
    k_hat, k_inv, kn = norm_parts(k, kg)
    scores = jnp.where(same, dot_nt(qn, kn) * scale, -1e30)
    exp_terms = jnp.exp(scores - jnp.max(scores, axis=-1, keepdims=True))
    probs = exp_terms / jnp.sum(exp_terms, axis=-1, keepdims=True)
    return probs, q_hat, q_inv, qn, k_hat, k_inv, kn


def probabilities_kernel(per, dim, place, q_ref, k_ref, came_ref, row_ref, col_ref, qg_ref, kg_ref, p_ref, hat_ref, inv_ref, low_ref, p_low_ref):
    same = col_ref[...] == row_ref[...]
    first = place[0] == 0
    for h in range(per):
        cols = slice(h * dim, (h + 1) * dim)
        q, k = (assemble(first, ref[:, cols], came_ref[n, :, cols]) for n, ref in enumerate((q_ref, k_ref)))
        probs, *parts = head_probs(q, k, qg_ref[...], kg_ref[...], same, dim**-0.5)
        p_ref[h] = probs
        p_low_ref[h] = probs.astype(BF16)
        for n, (hat, inv, normed) in enumerate((parts[:3], parts[3:])):
            hat_ref[n, h] = hat
            inv_ref[n, h] = jnp.broadcast_to(inv, hat.shape)
            low_ref[n, h] = normed


def attended_kernel(per, dim, place, p_low_ref, v_ref, came_ref, even_ref, odd_ref, whole_ref):
    first = place[0] == 0
    done = []
    for h in range(per):
        cols = slice(h * dim, (h + 1) * dim)
        v = assemble(first, v_ref[:, cols], came_ref[:, cols])
        whole_ref[h] = v
        done.append(dot_nn(p_low_ref[h], v).T.astype(BF16))
    att = jnp.concatenate(done, axis=0)
    half = att.shape[0] // 2
    straight = (place[1] & 1) == 0
    low, high = att[:half], att[half:]
    even_ref[0] = jnp.where(straight, low, high)
    odd_ref[0] = jnp.where(straight, high, low)


def backward_kernel(per, dim, n_into, place, p_ref, hat_ref, inv_ref, low_ref, v_ref, d_ref, qg_ref, kg_ref, *rest):
    gq_ref, gk_ref, gv_ref = rest[n_into:]
    scale = dim**-0.5
    straight = (place[1] & 1) == 0
    one, two = d_ref[0, 0], d_ref[0, 1]
    grad = jnp.concatenate([jnp.where(straight, one, two), jnp.where(straight, two, one)], axis=0)
    qg, kg = qg_ref[...], kg_ref[...]
    for h in range(per):
        probs, qn, kn, v = p_ref[h], low_ref[0, h], low_ref[1, h], v_ref[h]
        d = grad[h * dim : (h + 1) * dim].T
        gp = dot_nt(d, v)
        gv_ref[h] = dot_tn(probs.astype(BF16), d).astype(BF16)
        delta = jnp.sum(probs * gp, axis=-1, keepdims=True)
        gs = (probs * (gp - delta) * scale).astype(BF16)
        gq_ref[h] = norm_back(dot_nn(gs, kn), hat_ref[0, h], inv_ref[0, h], qg).astype(BF16)
        gk_ref[h] = norm_back(dot_tn(gs, qn), hat_ref[1, h], inv_ref[1, h], kg).astype(BF16)


def whole(shape):
    return pl.BlockSpec(shape, lambda *_: (0,) * len(shape))


def pair_index(i, p):
    return i ^ (p[1] >> 1) ^ (p[2] << 1)


def own_heads(rows, wide):
    return pl.BlockSpec((rows, wide), lambda i, p: (0, p[0] * 4 + i))


def in_hbm(a):
    return pltpu.with_memory_space_constraint(a, pltpu.HBM)


def attention_probabilities(place, queries, keys, came, row, col, qg, kg):
    dim = qg.shape[1]
    half_tokens, heads = came.shape[1], came.shape[2] // dim
    tokens, per = 2 * half_tokens, heads // 4
    wide = per * dim

    def saved(n, dtype):
        spec = pl.BlockSpec((n, per, tokens, dim), lambda i, p: (0, i, 0, 0))
        return spec, pltpu.HBM((n, heads, tokens, dim), dtype)

    square, probs = pl.BlockSpec((per, tokens, tokens), lambda i, p: (i, 0, 0)), (heads, tokens, tokens)
    specs, shapes = zip(
        (square, pltpu.HBM(probs, F32)),
        saved(2, F32),
        saved(2, F32),
        saved(2, BF16),
        (square, jax.ShapeDtypeStruct(probs, BF16)),
    )
    *saved, low = pl.pallas_call(
        functools.partial(probabilities_kernel, per, dim),
        grid_spec=pltpu.PrefetchScalarGridSpec(
            num_scalar_prefetch=1,
            grid=(4,),
            in_specs=[own_heads(half_tokens, wide)] * 2
            + [pl.BlockSpec((2, half_tokens, wide), lambda i, p: (0, 0, i))]
            + [whole((1, tokens)), whole((tokens, 1)), whole((1, dim)), whole((1, dim))],
            out_specs=specs,
        ),
        out_shape=shapes,
        compiler_params=pltpu.CompilerParams(vmem_limit_bytes=16 << 20),
        cost_estimate=pl.CostEstimate(flops=1000, bytes_accessed=1000, transcendentals=0),
        name="attention_probabilities",
    )(place, in_hbm(queries), in_hbm(keys), came, row, col, qg, kg)
    return saved, low


def attention_attended(place, low, values, came, dim):
    half_tokens, heads = came.shape[0], low.shape[0]
    tokens, per = 2 * half_tokens, heads // 4
    rows, wide = per * dim // 2, per * dim
    out = pl.BlockSpec((1, rows, tokens), lambda i, p: (pair_index(i, p), 0, 0))
    return pl.pallas_call(
        functools.partial(attended_kernel, per, dim),
        grid_spec=pltpu.PrefetchScalarGridSpec(
            num_scalar_prefetch=1,
            grid=(4,),
            in_specs=[pl.BlockSpec((per, tokens, tokens), lambda i, p: (i, 0, 0))]
            + [own_heads(half_tokens, wide), pl.BlockSpec((half_tokens, wide), lambda i, p: (0, i))],
            out_specs=[out, out, pl.BlockSpec((per, tokens, dim), lambda i, p: (i, 0, 0))],
        ),
        out_shape=[jax.ShapeDtypeStruct((4, rows, tokens), BF16)] * 2 + [pltpu.HBM((heads, tokens, dim), BF16)],
        compiler_params=pltpu.CompilerParams(vmem_limit_bytes=16 << 20),
        cost_estimate=pl.CostEstimate(flops=1000, bytes_accessed=1000, transcendentals=0),
        name="attention_attended",
    )(place, low, in_hbm(values), came)


def attention_backward(place, first, pairs, saved, grads, qg, kg, into=()):
    heads, tokens = saved[0].shape[:2]
    dim, per, rows = qg.shape[1], heads // 4, grads.shape[2]

    def index(i, p):
        return pair_index(i + first, p)

    def block(n):
        return pl.BlockSpec((n, per, tokens, dim), lambda i, p: (0, index(i, p), 0, 0))

    return pl.pallas_call(
        functools.partial(backward_kernel, per, dim, len(into)),
        grid_spec=pltpu.PrefetchScalarGridSpec(
            num_scalar_prefetch=1,
            grid=(pairs,),
            in_specs=[pl.BlockSpec((per, tokens, tokens), lambda i, p: (index(i, p), 0, 0)), block(2), block(2), block(2)]
            + [pl.BlockSpec((per, tokens, dim), lambda i, p: (index(i, p), 0, 0))]
            + [pl.BlockSpec((1, 2, rows, tokens), lambda i, p: (i, 0, 0, 0))]
            + [whole((1, dim)), whole((1, dim))]
            + [pl.BlockSpec(memory_space=pl.ANY)] * len(into),
            out_specs=[pl.BlockSpec((per, tokens, dim), lambda i, p: (index(i, p), 0, 0))] * 3,
        ),
        out_shape=[pltpu.HBM((heads, tokens, dim), BF16)] * 3,
        input_output_aliases={9 + n: n for n in range(len(into))},
        compiler_params=pltpu.CompilerParams(vmem_limit_bytes=16 << 20),
        cost_estimate=pl.CostEstimate(flops=1000, bytes_accessed=1000, transcendentals=0),
        name="attention_backward",
    )(place, *saved, grads, qg, kg, *into)


VECTOR = pl.BlockSpec(memory_space=pltpu.VMEM)
SCALAR = pl.BlockSpec(memory_space=pltpu.SMEM)


def hold_kernel(*refs):
    n = len(refs) // 2
    for source, held in zip(refs[:n], refs[n:]):
        held[...] = source[...]


def hold(*arrays, steps=4):
    specs = [pl.BlockSpec((a.shape[0] // steps, a.shape[1]), lambda i: (i, 0)) for a in arrays]
    return pl.pallas_call(
        hold_kernel,
        grid=(steps,),
        in_specs=specs,
        out_specs=specs,
        out_shape=[pltpu.VMEM(a.shape, a.dtype) for a in arrays],
        compiler_params=pltpu.CompilerParams(vmem_limit_bytes=16 << 20),
        cost_estimate=pl.CostEstimate(flops=1000, bytes_accessed=1000, transcendentals=0),
        name="hold",
    )(*arrays)


def choose_kernel(place, mid_ref, end_ref, far_ref):
    far_ref[...] = jnp.where(place[3] == 1, mid_ref[...], end_ref[...])


def choose(place, mid, end):
    return pl.pallas_call(
        choose_kernel,
        in_specs=[SCALAR, VECTOR, VECTOR],
        out_specs=VECTOR,
        out_shape=pltpu.VMEM(mid.shape, mid.dtype),
        compiler_params=pltpu.CompilerParams(vmem_limit_bytes=4 << 20),
        cost_estimate=pl.CostEstimate(flops=10**10, bytes_accessed=1000, transcendentals=0),
        name="choose",
    )(place, mid, end)


def products_kernel(n, parts, place, w_ref, far_ref, *refs):
    g_refs, (keep_ref, send_ref, both_ref) = refs[:-3], refs[-3:]
    rows = w_ref.shape[0]
    flip = place[2] == 1
    for first, depth, _ in parts:
        cols = slice(first, first + depth)
        own, far = w_ref[:, cols], far_ref[:, cols]
        both_ref[:rows, cols] = jnp.where(flip, far, own)
        both_ref[rows:, cols] = jnp.where(flip, own, far)
    for j in range(n):
        total = None
        for c, (first, depth, starts) in enumerate(parts):
            start = starts[j]
            term = dot_nt(both_ref[:, first : first + depth], g_refs[c * n + j][:, start : start + depth])
            total = term if total is None else total + term
        keep_ref[j] = total[:rows].astype(BF16)
        send_ref[j] = total[rows:].astype(BF16)


def gradient_products(place, w, far, parts):
    rows, depth = w.shape
    n, tokens = len(parts[0][0]), parts[0][0][0].shape[0]
    blocks = [a for part in parts for a in part[0]]
    return pl.pallas_call(
        functools.partial(products_kernel, n, [(first, wide, starts) for _, starts, first, wide in parts]),
        in_specs=[SCALAR] + [VECTOR] * (2 + len(blocks)),
        out_specs=[VECTOR] * 2,
        out_shape=[jax.ShapeDtypeStruct((n, rows, tokens), BF16)] * 2,
        scratch_shapes=[pltpu.VMEM((2 * rows, depth), BF16)],
        compiler_params=pltpu.CompilerParams(vmem_limit_bytes=16 << 20),
        cost_estimate=pl.CostEstimate(flops=1000, bytes_accessed=1000, transcendentals=0),
        name="gradient_products",
    )(place, w, far, *blocks)


def weight_kernel(n, starts, parts, place, own_ref, other_ref, *refs):
    g_refs, far_refs, kept_ref, both_ref = refs[:n], refs[n:-2], refs[-2], refs[-1]
    rows, tokens = own_ref.shape[1:]
    flip = place[2] == 1
    for j in range(n):
        cols = slice(j * tokens, (j + 1) * tokens)
        both_ref[:rows, cols] = jnp.where(flip, own_ref[j], other_ref[j])
        both_ref[rows:, cols] = jnp.where(flip, other_ref[j], own_ref[j])
    first = 0
    for part, far_ref in zip(parts, far_refs):
        blocks = [g_ref[:, start + first : start + first + part] for g_ref, start in zip(g_refs, starts)]
        total = dot_nn(both_ref[...], jnp.concatenate(blocks, axis=0))
        far_ref[...] = total[:rows].astype(BF16)
        kept_ref[:, first : first + part] = total[rows:]
        first += part


def weight_terms(place, own, other, half, parts, flops):
    n, rows, tokens = own.shape
    depth = sum(parts)
    return pl.pallas_call(
        functools.partial(weight_kernel, n, half[1], parts),
        in_specs=[SCALAR] + [VECTOR] * (2 + n),
        out_specs=[VECTOR] * (len(parts) + 1),
        out_shape=[jax.ShapeDtypeStruct((rows, part), BF16) for part in parts]
        + [jax.ShapeDtypeStruct((rows, depth), F32)],
        scratch_shapes=[pltpu.VMEM((2 * rows, n * tokens), BF16)],
        compiler_params=pltpu.CompilerParams(vmem_limit_bytes=16 << 20),
        cost_estimate=pl.CostEstimate(flops=flops, bytes_accessed=1000, transcendentals=0),
        name="weight_terms",
    )(place, own, other, *half[0])


def finish_kernel(n, scale, *refs):
    kept_refs, far_refs, out_ref = refs[:n], refs[n:-1], refs[-1]
    for group, cast in ((kept_refs, False), (far_refs, True)):
        first = 0
        for ref in group:
            last = first + ref.shape[1]
            if cast:
                out_ref[:, first:last] = (out_ref[:, first:last] + ref[...].astype(F32)) * scale
            else:
                out_ref[:, first:last] = ref[...]
            first = last


def finish(kept, far, scale):
    rows, depth = kept[0].shape[0], sum(a.shape[1] for a in kept)
    tile = rows // 4

    def block(a):
        return pl.BlockSpec((tile, a.shape[1]), lambda i: (i, 0))

    return pl.pallas_call(
        functools.partial(finish_kernel, len(kept), scale),
        grid=(rows // tile,),
        in_specs=[block(a) for a in (*kept, *far)],
        out_specs=pl.BlockSpec((tile, depth), lambda i: (i, 0)),
        out_shape=jax.ShapeDtypeStruct((rows, depth), F32),
        compiler_params=pltpu.CompilerParams(vmem_limit_bytes=16 << 20),
        cost_estimate=pl.CostEstimate(flops=1000, bytes_accessed=1000, transcendentals=0),
        name="finish",
    )(*kept, *far)


def xor(k):
    return [(j, j ^ k) for j in range(16)]


CORE, CROSS, PLANE = xor(1), xor(2), xor(4)
FAR = xor(12)
MIDDLE = [pair for pair in FAR if 4 <= pair[0] < 12]
ENDS = [pair for pair in FAR if not 4 <= pair[0] < 12]


def move(a, perm, name):
    with jax.named_scope(name):
        return lax.ppermute(a, "fsdp", perm)


def swap(a, name):
    with jax.named_scope(name):
        return lax.ppermute(a, "seq", [(0, 1), (1, 0)])


def local_grid(queries, keys, values, image_ids, q_gain, k_gain, w_out, grad_y):
    y = lax.axis_index("seq")
    f = lax.axis_index("fsdp")
    middle = (f >> 3) ^ ((f >> 2) & 1)
    place = jnp.stack([y, f & 7, (f >> 3) ^ y, middle]).astype(jnp.int32)
    dim = q_gain.shape[0]
    tokens = image_ids.shape[1]
    half = queries.shape[1] // 2
    row, col = image_ids, image_ids.reshape(tokens, 1)
    qg, kg = q_gain.reshape(1, dim), k_gain.reshape(1, dim)
    barrier = lax.optimization_barrier
    width = grad_y.shape[1]
    cut = 2 * width // 3

    width = grad_y.shape[1]
    cut = 2 * width // 3
    barrier = lax.optimization_barrier

    theirs = [lax.dynamic_slice_in_dim(a, (1 - y) * half, half, axis=1) for a in (queries, keys, values)]
    send, gy, w_own = barrier((jnp.stack(theirs[:2]), grad_y, w_out))
    came = swap(send, "qk_seq")
    came_v = swap(theirs[2], "v_seq")
    g2 = move(gy, CROSS, "gy_cross")
    g4 = move(gy, PLANE, "gy_plane")
    w_mid = move(w_own, MIDDLE, "w_middle")
    saved, low = attention_probabilities(place, queries, keys, came, row, col, qg, kg)
    even, odd, v_all = attention_attended(place, low, values, came_v, dim)
    saved.append(v_all)
    odd = move(odd, CORE, "att_core")
    even, odd, g2, g4, gy, w_own, w_mid = barrier((even, odd, g2, g4, gy, w_own, w_mid))
    own = [jnp.stack([even[j], odd[j]]) for j in range(4)]
    other = [swap(own[0], "att_seq")]
    own = [own[0]] + [move(own[j], xor(2 * j), "att_group") for j in (1, 2, 3)]
    g4a, g4b = g4[:, :cut], g4[:, cut:]
    g1 = move(gy, CORE, "gy_core")
    own, other, g4, g4a, g4b, g2, g1, gy = barrier((own, other, g4, g4a, g4b, g2, g1, gy))
    other.append(swap(jnp.concatenate(own[1:]), "att_seq"))
    g6a = move(g4a, CROSS, "gy_plane_cross_a")
    w_far = choose(place, w_mid, move(w_own, ENDS, "w_ends"))
    g3, g5 = (move(g, CORE, "gy_core") for g in (g2, g4))
    gy, w_held = hold(gy, w_out)
    other[1], gy, w_held = barrier((other[1], gy, w_held))
    own, other = jnp.concatenate(own), jnp.concatenate(other)
    other, g6a = barrier((other, g6a))
    g7a = move(g6a, CORE, "gy_core")
    blocks_a = [gy, g1, g2, g3, g4, g5, g6a, g7a]
    *sent, kept_a = weight_terms(place, own, other, (blocks_a, (0,) * 8), (cut // 2,), 1000)
    own, other, g6a, g7a, g3, g5, g4b, w_far, sent, kept_a = barrier(
        (own, other, g6a, g7a, g3, g5, g4b, w_far, sent, kept_a)
    )
    g6b = move(g4b, CROSS, "gy_plane_cross_b")
    far = [move(sent[0], FAR, "grad_w_far")]
    weights = (w_held, w_far)
    near = (gy, g2, g1, g3)
    keep0, send0 = gradient_products(
        place, *weights, [(near, (start,) * 4, start, depth) for start, depth in ((0, cut), (cut, width - cut))]
    )
    came0 = swap(send0, "products_seq")
    own_c, keep0 = barrier((own, keep0))
    *sent, kept_c = weight_terms(place, own_c, other, (blocks_a, (cut // 2,) * 8), (cut // 2,), 1000)
    g6b, far, sent, kept_c, keep0, came0 = barrier((g6b, far, sent, kept_c, keep0, came0))
    g7b = move(g6b, CORE, "gy_core")
    far.append(move(sent[0], FAR, "grad_w_far"))
    keep1, send1 = gradient_products(
        place,
        *weights,
        [((g4, g6a, g5, g7a), (0,) * 4, 0, cut), ((g4, g6b, g5, g7b), (cut, 0, cut, 0), cut, width - cut)],
    )
    came1 = swap(send1, "products_seq")
    came0, keep1, blocks_b = barrier((came0, keep1, [gy, g1, g2, g3, g4, g5, g6b, g7b]))
    summed0 = (keep0.astype(F32) + came0.astype(F32)).astype(BF16)
    odd = move(summed0[2:], CORE, "products_core")
    near = [jnp.stack([summed0[j], odd[j]]) for j in range(2)]
    near[1] = move(near[1], xor(2), "products_group")
    starts_b = (cut,) * 6 + (0,) * 2
    *sent, kept_b = weight_terms(place, own, other, (blocks_b, starts_b), ((width - cut) // 2,) * 2, 1000)
    far, near, keep1, came1, sent, kept_b = barrier((far, near, keep1, came1, sent, kept_b))
    summed1 = (keep1.astype(F32) + came1.astype(F32)).astype(BF16)
    odd = move(summed1[2:], CORE, "products_core")
    next_plane = [jnp.stack([summed1[j], odd[j]]) for j in range(2)]
    next_plane = [move(next_plane[j], xor(4 + 2 * j), "products_group") for j in range(2)]
    far += [move(part, FAR, "grad_w_far") for part in sent]
    grads = attention_backward(place, 0, 2, saved, jnp.stack(near), qg, kg)
    grads = attention_backward(place, 2, 2, saved, jnp.stack(next_plane), qg, kg, tuple(grads))

    grad_w = finish((kept_a, kept_c, kept_b), far, tokens ** (-0.5))
    return (*(g.transpose(1, 0, 2) for g in grads), grad_w)


def solution(mesh):
    in_specs = (
        P(("fsdp", "seq"), None),
        P(("fsdp", "seq"), None),
        P(("fsdp", "seq"), None),
        P("fsdp", None),
        P(),
        P(),
        P("fsdp", "seq"),
        P("fsdp", "seq"),
    )
    out_specs = (
        P("fsdp", "seq", None),
        P("fsdp", "seq", None),
        P("fsdp", "seq", None),
        P("fsdp", "seq"),
    )
    grid = mesh.shape["fsdp"] == 16 and mesh.shape["seq"] == 2
    local = local_grid if grid else local_any
    return jax.shard_map(local, mesh=mesh, in_specs=in_specs, out_specs=out_specs, check_vma=False)
```

```python
import functools

import jax
import jax.numpy as jnp
from jax import lax
from jax.experimental import pallas as pl
from jax.experimental.pallas import tpu as pltpu
from jax.sharding import PartitionSpec as P

F32 = jnp.float32
BF16 = jnp.bfloat16


def norm_parts(source, gain):
    wide = source.astype(jnp.float32)
    centred = wide - jnp.mean(wide, axis=-1, keepdims=True)
    scale_inv = lax.rsqrt(jnp.mean(centred * centred, axis=-1, keepdims=True) + 1e-06)
    x_hat = centred * scale_inv
    return (x_hat, scale_inv, (x_hat * gain).astype(jnp.bfloat16))


def norm_back(grad_n, x_hat, scale_inv, gain):
    scaled = grad_n * gain
    return scale_inv * (
        scaled
        - jnp.mean(scaled, axis=-1, keepdims=True)
        - x_hat * jnp.mean(scaled * x_hat, axis=-1, keepdims=True)
    )


def probabilities(normalized_queries, normalized_keys, same_image, scale_factor):
    scores = (
        jnp.einsum(
            "krt,irt->rki", normalized_queries, normalized_keys, preferred_element_type=jnp.float32
        )
        * scale_factor
    )
    scores = jnp.where(same_image[None], scores, -1e30)
    row_top = jnp.max(scores, axis=-1, keepdims=True)
    exp_terms = jnp.exp(scores - row_top)
    return exp_terms / jnp.sum(exp_terms, axis=-1, keepdims=True)


def local_any(queries, keys, values, image_ids, q_gain, k_gain, w_out, grad_y):
    head_dim = q_gain.shape[0]
    tok_rows = queries.shape[0]
    heads_all = queries.shape[1] // head_dim
    scale_factor = head_dim ** (-0.5)
    q_patch = queries.reshape(tok_rows, heads_all, head_dim)
    k_patch = keys.reshape(tok_rows, heads_all, head_dim)
    v_patch = values.reshape(tok_rows, heads_all, head_dim)
    q_local, k_local, value_shard = (
        lax.all_to_all(q_patch, "seq", split_axis=1, concat_axis=0, tiled=True),
        lax.all_to_all(k_patch, "seq", split_axis=1, concat_axis=0, tiled=True),
        lax.all_to_all(v_patch, "seq", split_axis=1, concat_axis=0, tiled=True),
    )
    seq_length = q_local.shape[0]
    local_heads = q_local.shape[1]
    image_row = image_ids[0]
    same_image = image_row[:, None] == image_row[None, :]
    q_hat, q_inv, normalized_queries = norm_parts(q_local, q_gain)
    k_hat, k_inv, normalized_keys = norm_parts(k_local, k_gain)
    prob_rows = probabilities(normalized_queries, normalized_keys, same_image, scale_factor)
    probs_reduced_precision = prob_rows.astype(jnp.bfloat16)
    attended = jnp.einsum(
        "tgi,itp->gtp", probs_reduced_precision, value_shard, preferred_element_type=jnp.float32
    ).astype(jnp.bfloat16)
    attended_flat = attended.reshape(seq_length, local_heads * head_dim)
    partial_g = jnp.einsum(
        "ld,cd->lc",
        grad_y,
        lax.all_gather(w_out, "fsdp", axis=0, tiled=True),
        preferred_element_type=jnp.float32,
    )
    grad_sum = lax.psum_scatter(
        partial_g.astype(jnp.bfloat16), "seq", scatter_dimension=1, tiled=True
    )
    attention_gradient = grad_sum.reshape(seq_length, local_heads, head_dim)
    grad_values = jnp.einsum(
        "jpw,pjy->wjy",
        probs_reduced_precision,
        attention_gradient,
        preferred_element_type=jnp.float32,
    ).astype(jnp.bfloat16)
    probability_gradient = jnp.einsum(
        "krt,irt->rki", attention_gradient, value_shard, preferred_element_type=jnp.float32
    )
    row_delta = jnp.sum(prob_rows * probability_gradient, axis=-1, keepdims=True)
    score_gradient = (prob_rows * (probability_gradient - row_delta) * scale_factor).astype(
        jnp.bfloat16
    )
    normed_query_gradient = jnp.einsum(
        "tgi,itp->gtp", score_gradient, normalized_keys, preferred_element_type=jnp.float32
    )
    normed_key_gradient = jnp.einsum(
        "jpw,pjy->wjy", score_gradient, normalized_queries, preferred_element_type=jnp.float32
    )
    grad_queries = norm_back(normed_query_gradient, q_hat, q_inv, q_gain).astype(jnp.bfloat16)
    grad_keys = norm_back(normed_key_gradient, k_hat, k_inv, k_gain).astype(jnp.bfloat16)
    partial_w = jnp.einsum(
        "lc,ld->cd",
        lax.all_gather(attended_flat, "seq", axis=1, tiled=True),
        grad_y,
        preferred_element_type=jnp.float32,
    )
    summed = lax.psum_scatter(partial_w, "fsdp", scatter_dimension=0, tiled=True)
    grad_w = summed * seq_length ** (-0.5)
    return (grad_queries, grad_keys, grad_values, grad_w)


def dot_nt(a, b):
    return lax.dot_general(a, b, (((1,), (1,)), ((), ())), preferred_element_type=F32)


def dot_tn(a, b):
    return lax.dot_general(a, b, (((0,), (0,)), ((), ())), preferred_element_type=F32)


def dot_nn(a, b):
    return jnp.dot(a, b, preferred_element_type=F32)


def assemble(first, own, came):
    return jnp.concatenate([jnp.where(first, own, came), jnp.where(first, came, own)], axis=0)


def head_probs(q, k, qg, kg, same, scale):
    q_hat, q_inv, qn = norm_parts(q, qg)
    k_hat, k_inv, kn = norm_parts(k, kg)
    scores = jnp.where(same, dot_nt(qn, kn) * scale, -1e30)
    exp_terms = jnp.exp(scores - jnp.max(scores, axis=-1, keepdims=True))
    probs = exp_terms / jnp.sum(exp_terms, axis=-1, keepdims=True)
    return probs, q_hat, q_inv, qn, k_hat, k_inv, kn


def probabilities_kernel(per, dim, place, q_ref, k_ref, came_ref, row_ref, col_ref, qg_ref, kg_ref, p_ref, hat_ref, inv_ref, low_ref, p_low_ref):
    same = col_ref[...] == row_ref[...]
    first = place[0] == 0
    for h in range(per):
        cols = slice(h * dim, (h + 1) * dim)
        q, k = (assemble(first, ref[:, cols], came_ref[n, :, cols]) for n, ref in enumerate((q_ref, k_ref)))
        probs, *parts = head_probs(q, k, qg_ref[...], kg_ref[...], same, dim**-0.5)
        p_ref[h] = probs
        p_low_ref[h] = probs.astype(BF16)
        for n, (hat, inv, normed) in enumerate((parts[:3], parts[3:])):
            hat_ref[n, h] = hat
            inv_ref[n, h] = jnp.broadcast_to(inv, hat.shape)
            low_ref[n, h] = normed


def attended_kernel(per, dim, place, p_low_ref, v_ref, came_ref, even_ref, odd_ref, whole_ref):
    first = place[0] == 0
    done = []
    for h in range(per):
        cols = slice(h * dim, (h + 1) * dim)
        v = assemble(first, v_ref[:, cols], came_ref[:, cols])
        whole_ref[h] = v
        done.append(dot_nn(p_low_ref[h], v).T.astype(BF16))
    att = jnp.concatenate(done, axis=0)
    half = att.shape[0] // 2
    straight = (place[1] & 1) == 0
    low, high = att[:half], att[half:]
    even_ref[0] = jnp.where(straight, low, high)
    odd_ref[0] = jnp.where(straight, high, low)


def backward_kernel(per, dim, n_into, place, p_ref, hat_ref, inv_ref, low_ref, v_ref, d_ref, qg_ref, kg_ref, *rest):
    gq_ref, gk_ref, gv_ref = rest[n_into:]
    scale = dim**-0.5
    straight = (place[1] & 1) == 0
    one, two = d_ref[0, 0], d_ref[0, 1]
    grad = jnp.concatenate([jnp.where(straight, one, two), jnp.where(straight, two, one)], axis=0)
    qg, kg = qg_ref[...], kg_ref[...]
    for h in range(per):
        probs, qn, kn, v = p_ref[h], low_ref[0, h], low_ref[1, h], v_ref[h]
        d = grad[h * dim : (h + 1) * dim].T
        gp = dot_nt(d, v)
        gv_ref[h] = dot_tn(probs.astype(BF16), d).astype(BF16)
        delta = jnp.sum(probs * gp, axis=-1, keepdims=True)
        gs = (probs * (gp - delta) * scale).astype(BF16)
        gq_ref[h] = norm_back(dot_nn(gs, kn), hat_ref[0, h], inv_ref[0, h], qg).astype(BF16)
        gk_ref[h] = norm_back(dot_tn(gs, qn), hat_ref[1, h], inv_ref[1, h], kg).astype(BF16)


def whole(shape):
    return pl.BlockSpec(shape, lambda *_: (0,) * len(shape))


def pair_index(i, p):
    return i ^ (p[1] >> 1) ^ (p[2] << 1)


def own_heads(rows, wide):
    return pl.BlockSpec((rows, wide), lambda i, p: (0, p[0] * 4 + i))


def in_hbm(a):
    return pltpu.with_memory_space_constraint(a, pltpu.HBM)


def attention_probabilities(place, queries, keys, came, row, col, qg, kg):
    dim = qg.shape[1]
    half_tokens, heads = came.shape[1], came.shape[2] // dim
    tokens, per = 2 * half_tokens, heads // 4
    wide = per * dim

    def saved(n, dtype):
        spec = pl.BlockSpec((n, per, tokens, dim), lambda i, p: (0, i, 0, 0))
        return spec, pltpu.HBM((n, heads, tokens, dim), dtype)

    square, probs = pl.BlockSpec((per, tokens, tokens), lambda i, p: (i, 0, 0)), (heads, tokens, tokens)
    specs, shapes = zip(
        (square, pltpu.HBM(probs, F32)),
        saved(2, F32),
        saved(2, F32),
        saved(2, BF16),
        (square, jax.ShapeDtypeStruct(probs, BF16)),
    )
    *saved, low = pl.pallas_call(
        functools.partial(probabilities_kernel, per, dim),
        grid_spec=pltpu.PrefetchScalarGridSpec(
            num_scalar_prefetch=1,
            grid=(4,),
            in_specs=[own_heads(half_tokens, wide)] * 2
            + [pl.BlockSpec((2, half_tokens, wide), lambda i, p: (0, 0, i))]
            + [whole((1, tokens)), whole((tokens, 1)), whole((1, dim)), whole((1, dim))],
            out_specs=specs,
        ),
        out_shape=shapes,
        compiler_params=pltpu.CompilerParams(vmem_limit_bytes=16 << 20),
        cost_estimate=pl.CostEstimate(flops=1000, bytes_accessed=1000, transcendentals=0),
        name="attention_probabilities",
    )(place, in_hbm(queries), in_hbm(keys), came, row, col, qg, kg)
    return saved, low


def attention_attended(place, low, values, came, dim):
    half_tokens, heads = came.shape[0], low.shape[0]
    tokens, per = 2 * half_tokens, heads // 4
    rows, wide = per * dim // 2, per * dim
    out = pl.BlockSpec((1, rows, tokens), lambda i, p: (pair_index(i, p), 0, 0))
    return pl.pallas_call(
        functools.partial(attended_kernel, per, dim),
        grid_spec=pltpu.PrefetchScalarGridSpec(
            num_scalar_prefetch=1,
            grid=(4,),
            in_specs=[pl.BlockSpec((per, tokens, tokens), lambda i, p: (i, 0, 0))]
            + [own_heads(half_tokens, wide), pl.BlockSpec((half_tokens, wide), lambda i, p: (0, i))],
            out_specs=[out, out, pl.BlockSpec((per, tokens, dim), lambda i, p: (i, 0, 0))],
        ),
        out_shape=[jax.ShapeDtypeStruct((4, rows, tokens), BF16)] * 2 + [pltpu.HBM((heads, tokens, dim), BF16)],
        compiler_params=pltpu.CompilerParams(vmem_limit_bytes=16 << 20),
        cost_estimate=pl.CostEstimate(flops=1000, bytes_accessed=1000, transcendentals=0),
        name="attention_attended",
    )(place, low, in_hbm(values), came)


def attention_backward(place, first, pairs, saved, grads, qg, kg, into=()):
    heads, tokens = saved[0].shape[:2]
    dim, per, rows = qg.shape[1], heads // 4, grads.shape[2]

    def index(i, p):
        return pair_index(i + first, p)

    def block(n):
        return pl.BlockSpec((n, per, tokens, dim), lambda i, p: (0, index(i, p), 0, 0))

    return pl.pallas_call(
        functools.partial(backward_kernel, per, dim, len(into)),
        grid_spec=pltpu.PrefetchScalarGridSpec(
            num_scalar_prefetch=1,
            grid=(pairs,),
            in_specs=[pl.BlockSpec((per, tokens, tokens), lambda i, p: (index(i, p), 0, 0)), block(2), block(2), block(2)]
            + [pl.BlockSpec((per, tokens, dim), lambda i, p: (index(i, p), 0, 0))]
            + [pl.BlockSpec((1, 2, rows, tokens), lambda i, p: (i, 0, 0, 0))]
            + [whole((1, dim)), whole((1, dim))]
            + [pl.BlockSpec(memory_space=pl.ANY)] * len(into),
            out_specs=[pl.BlockSpec((per, tokens, dim), lambda i, p: (index(i, p), 0, 0))] * 3,
        ),
        out_shape=[pltpu.HBM((heads, tokens, dim), BF16)] * 3,
        input_output_aliases={9 + n: n for n in range(len(into))},
        compiler_params=pltpu.CompilerParams(vmem_limit_bytes=16 << 20),
        cost_estimate=pl.CostEstimate(flops=1000, bytes_accessed=1000, transcendentals=0),
        name="attention_backward",
    )(place, *saved, grads, qg, kg, *into)


VECTOR = pl.BlockSpec(memory_space=pltpu.VMEM)
SCALAR = pl.BlockSpec(memory_space=pltpu.SMEM)


def hold_kernel(*refs):
    n = len(refs) // 2
    for source, held in zip(refs[:n], refs[n:]):
        held[...] = source[...]


def hold(*arrays, steps=4):
    specs = [pl.BlockSpec((a.shape[0] // steps, a.shape[1]), lambda i: (i, 0)) for a in arrays]
    return pl.pallas_call(
        hold_kernel,
        grid=(steps,),
        in_specs=specs,
        out_specs=specs,
        out_shape=[pltpu.VMEM(a.shape, a.dtype) for a in arrays],
        compiler_params=pltpu.CompilerParams(vmem_limit_bytes=16 << 20),
        cost_estimate=pl.CostEstimate(flops=1000, bytes_accessed=1000, transcendentals=0),
        name="hold",
    )(*arrays)


def choose_kernel(place, mid_ref, end_ref, far_ref):
    far_ref[...] = jnp.where(place[3] == 1, mid_ref[...], end_ref[...])


def choose(place, mid, end):
    return pl.pallas_call(
        choose_kernel,
        in_specs=[SCALAR, VECTOR, VECTOR],
        out_specs=VECTOR,
        out_shape=pltpu.VMEM(mid.shape, mid.dtype),
        compiler_params=pltpu.CompilerParams(vmem_limit_bytes=4 << 20),
        cost_estimate=pl.CostEstimate(flops=10**10, bytes_accessed=1000, transcendentals=0),
        name="choose",
    )(place, mid, end)


def products_kernel(n, parts, place, w_ref, far_ref, *refs):
    g_refs, (keep_ref, send_ref, both_ref) = refs[:-3], refs[-3:]
    rows = w_ref.shape[0]
    flip = place[2] == 1
    for first, depth, _ in parts:
        cols = slice(first, first + depth)
        own, far = w_ref[:, cols], far_ref[:, cols]
        both_ref[:rows, cols] = jnp.where(flip, far, own)
        both_ref[rows:, cols] = jnp.where(flip, own, far)
    for j in range(n):
        total = None
        for c, (first, depth, starts) in enumerate(parts):
            start = starts[j]
            term = dot_nt(both_ref[:, first : first + depth], g_refs[c * n + j][:, start : start + depth])
            total = term if total is None else total + term
        keep_ref[j] = total[:rows].astype(BF16)
        send_ref[j] = total[rows:].astype(BF16)


def gradient_products(place, w, far, parts):
    rows, depth = w.shape
    n, tokens = len(parts[0][0]), parts[0][0][0].shape[0]
    blocks = [a for part in parts for a in part[0]]
    return pl.pallas_call(
        functools.partial(products_kernel, n, [(first, wide, starts) for _, starts, first, wide in parts]),
        in_specs=[SCALAR] + [VECTOR] * (2 + len(blocks)),
        out_specs=[VECTOR] * 2,
        out_shape=[jax.ShapeDtypeStruct((n, rows, tokens), BF16)] * 2,
        scratch_shapes=[pltpu.VMEM((2 * rows, depth), BF16)],
        compiler_params=pltpu.CompilerParams(vmem_limit_bytes=16 << 20),
        cost_estimate=pl.CostEstimate(flops=1000, bytes_accessed=1000, transcendentals=0),
        name="gradient_products",
    )(place, w, far, *blocks)


def weight_kernel(n, starts, parts, place, own_ref, other_ref, *refs):
    g_refs, far_refs, kept_ref, both_ref = refs[:n], refs[n:-2], refs[-2], refs[-1]
    rows, tokens = own_ref.shape[1:]
    flip = place[2] == 1
    for j in range(n):
        cols = slice(j * tokens, (j + 1) * tokens)
        both_ref[:rows, cols] = jnp.where(flip, own_ref[j], other_ref[j])
        both_ref[rows:, cols] = jnp.where(flip, other_ref[j], own_ref[j])
    first = 0
    for part, far_ref in zip(parts, far_refs):
        blocks = [g_ref[:, start + first : start + first + part] for g_ref, start in zip(g_refs, starts)]
        total = dot_nn(both_ref[...], jnp.concatenate(blocks, axis=0))
        far_ref[...] = total[:rows].astype(BF16)
        kept_ref[:, first : first + part] = total[rows:]
        first += part


def weight_terms(place, own, other, half, parts, flops):
    n, rows, tokens = own.shape
    depth = sum(parts)
    return pl.pallas_call(
        functools.partial(weight_kernel, n, half[1], parts),
        in_specs=[SCALAR] + [VECTOR] * (2 + n),
        out_specs=[VECTOR] * (len(parts) + 1),
        out_shape=[jax.ShapeDtypeStruct((rows, part), BF16) for part in parts]
        + [jax.ShapeDtypeStruct((rows, depth), F32)],
        scratch_shapes=[pltpu.VMEM((2 * rows, n * tokens), BF16)],
        compiler_params=pltpu.CompilerParams(vmem_limit_bytes=16 << 20),
        cost_estimate=pl.CostEstimate(flops=flops, bytes_accessed=1000, transcendentals=0),
        name="weight_terms",
    )(place, own, other, *half[0])


def finish_kernel(scale, n_into, kept_ref, *refs):
    far_refs, out_ref = refs[: len(refs) - 1 - n_into], refs[-1]
    first = 0
    for ref in far_refs:
        cols = slice(first, first + ref.shape[1])
        out_ref[:, cols] = (kept_ref[:, cols] + ref[...].astype(F32)) * scale
        first = cols.stop


def finish(kept, far, scale, first, depth, flops, into=()):
    rows, wide = kept.shape
    tile, place = rows // 4, first // wide

    def block(a):
        return pl.BlockSpec((tile, a.shape[1]), lambda i: (i, 0))

    return pl.pallas_call(
        functools.partial(finish_kernel, scale, len(into)),
        grid=(rows // tile,),
        in_specs=[block(a) for a in (kept, *far)] + [pl.BlockSpec(memory_space=pl.ANY)] * len(into),
        out_specs=pl.BlockSpec((tile, wide), lambda i: (i, place)),
        out_shape=pltpu.HBM((rows, depth), F32),
        input_output_aliases={1 + len(far): 0} if into else {},
        compiler_params=pltpu.CompilerParams(vmem_limit_bytes=16 << 20),
        cost_estimate=pl.CostEstimate(flops=flops, bytes_accessed=1000, transcendentals=0),
        name="finish",
    )(kept, *far, *into)


def xor(k):
    return [(j, j ^ k) for j in range(16)]


CORE, CROSS, PLANE = xor(1), xor(2), xor(4)
FAR = xor(12)
MIDDLE = [pair for pair in FAR if 4 <= pair[0] < 12]
ENDS = [pair for pair in FAR if not 4 <= pair[0] < 12]


def move(a, perm, name):
    with jax.named_scope(name):
        return lax.ppermute(a, "fsdp", perm)


def swap(a, name):
    with jax.named_scope(name):
        return lax.ppermute(a, "seq", [(0, 1), (1, 0)])


def local_grid(queries, keys, values, image_ids, q_gain, k_gain, w_out, grad_y):
    y = lax.axis_index("seq")
    f = lax.axis_index("fsdp")
    middle = (f >> 3) ^ ((f >> 2) & 1)
    place = jnp.stack([y, f & 7, (f >> 3) ^ y, middle]).astype(jnp.int32)
    dim = q_gain.shape[0]
    tokens = image_ids.shape[1]
    half = queries.shape[1] // 2
    row, col = image_ids, image_ids.reshape(tokens, 1)
    qg, kg = q_gain.reshape(1, dim), k_gain.reshape(1, dim)
    barrier = lax.optimization_barrier
    width = grad_y.shape[1]
    cut = 2 * width // 3

    width = grad_y.shape[1]
    cut = 2 * width // 3
    barrier = lax.optimization_barrier

    theirs = [lax.dynamic_slice_in_dim(a, (1 - y) * half, half, axis=1) for a in (queries, keys, values)]
    send, gy, w_own = barrier((jnp.stack(theirs[:2]), grad_y, w_out))
    came = swap(send, "qk_seq")
    came_v = swap(theirs[2], "v_seq")
    g2 = move(gy, CROSS, "gy_cross")
    g4 = move(gy, PLANE, "gy_plane")
    w_mid = move(w_own, MIDDLE, "w_middle")
    saved, low = attention_probabilities(place, queries, keys, came, row, col, qg, kg)
    even, odd, v_all = attention_attended(place, low, values, came_v, dim)
    saved.append(v_all)
    odd = move(odd, CORE, "att_core")
    even, odd, g2, g4, gy, w_own, w_mid = barrier((even, odd, g2, g4, gy, w_own, w_mid))
    own = [jnp.stack([even[j], odd[j]]) for j in range(4)]
    other = [swap(own[0], "att_seq")]
    own = [own[0]] + [move(own[j], xor(2 * j), "att_group") for j in (1, 2, 3)]
    g4a, g4b = g4[:, :cut], g4[:, cut:]
    g1 = move(gy, CORE, "gy_core")
    own, other, g4, g4a, g4b, g2, g1, gy = barrier((own, other, g4, g4a, g4b, g2, g1, gy))
    other.append(swap(jnp.concatenate(own[1:]), "att_seq"))
    g6a = move(g4a, CROSS, "gy_plane_cross_a")
    w_far = choose(place, w_mid, move(w_own, ENDS, "w_ends"))
    g3, g5 = (move(g, CORE, "gy_core") for g in (g2, g4))
    gy, w_held = hold(gy, w_out)
    other[1], gy, w_held = barrier((other[1], gy, w_held))
    own, other = jnp.concatenate(own), jnp.concatenate(other)
    other, g6a = barrier((other, g6a))
    g7a = move(g6a, CORE, "gy_core")
    blocks_a = [gy, g1, g2, g3, g4, g5, g6a, g7a]
    *sent, kept_a = weight_terms(place, own, other, (blocks_a, (0,) * 8), (cut // 2,), 1000)
    own, other, g6a, g7a, g3, g5, g4b, w_far, sent, kept_a = barrier(
        (own, other, g6a, g7a, g3, g5, g4b, w_far, sent, kept_a)
    )
    g6b = move(g4b, CROSS, "gy_plane_cross_b")
    far = [move(sent[0], FAR, "grad_w_far")]
    weights = (w_held, w_far)
    near = (gy, g2, g1, g3)
    keep0, send0 = gradient_products(
        place, *weights, [(near, (start,) * 4, start, depth) for start, depth in ((0, cut), (cut, width - cut))]
    )
    came0 = swap(send0, "products_seq")
    own_c, keep0 = barrier((own, keep0))
    *sent, kept_c = weight_terms(place, own_c, other, (blocks_a, (cut // 2,) * 8), (cut // 2,), 1000)
    g6b, far, sent, kept_c, keep0, came0 = barrier((g6b, far, sent, kept_c, keep0, came0))
    g7b = move(g6b, CORE, "gy_core")
    far.append(move(sent[0], FAR, "grad_w_far"))
    keep1, send1 = gradient_products(
        place,
        *weights,
        [((g4, g6a, g5, g7a), (0,) * 4, 0, cut), ((g4, g6b, g5, g7b), (cut, 0, cut, 0), cut, width - cut)],
    )
    came1 = swap(send1, "products_seq")
    came0, keep1, blocks_b = barrier((came0, keep1, [gy, g1, g2, g3, g4, g5, g6b, g7b]))
    summed0 = (keep0.astype(F32) + came0.astype(F32)).astype(BF16)
    odd = move(summed0[2:], CORE, "products_core")
    near = [jnp.stack([summed0[j], odd[j]]) for j in range(2)]
    near[1] = move(near[1], xor(2), "products_group")
    starts_b = (cut,) * 6 + (0,) * 2
    *sent, kept_b = weight_terms(place, own, other, (blocks_b, starts_b), ((width - cut) // 2,) * 2, 1000)
    far, near, keep1, came1, sent, kept_b = barrier((far, near, keep1, came1, sent, kept_b))
    summed1 = (keep1.astype(F32) + came1.astype(F32)).astype(BF16)
    odd = move(summed1[2:], CORE, "products_core")
    next_plane = [jnp.stack([summed1[j], odd[j]]) for j in range(2)]
    next_plane = [move(next_plane[j], xor(4 + 2 * j), "products_group") for j in range(2)]
    last = [move(part, FAR, "grad_w_far") for part in sent]
    scale = tokens ** (-0.5)
    grad_w = finish(kept_a, far[:1], scale, 0, width, 1000)
    grad_w = finish(kept_c, far[1:], scale, cut // 2, width, 1000, (grad_w,))
    near, grad_w = barrier((near, grad_w))
    grads = attention_backward(place, 0, 2, saved, jnp.stack(near), qg, kg)
    grads = attention_backward(place, 2, 2, saved, jnp.stack(next_plane), qg, kg, tuple(grads))

    grad_w = finish(kept_b, last, scale, cut, width, 1000, (grad_w,))
    return (*(g.transpose(1, 0, 2) for g in grads), grad_w)


def solution(mesh):
    in_specs = (
        P(("fsdp", "seq"), None),
        P(("fsdp", "seq"), None),
        P(("fsdp", "seq"), None),
        P("fsdp", None),
        P(),
        P(),
        P("fsdp", "seq"),
        P("fsdp", "seq"),
    )
    out_specs = (
        P("fsdp", "seq", None),
        P("fsdp", "seq", None),
        P("fsdp", "seq", None),
        P("fsdp", "seq"),
    )
    grid = mesh.shape["fsdp"] == 16 and mesh.shape["seq"] == 2
    local = local_grid if grid else local_any
    return jax.shard_map(local, mesh=mesh, in_specs=in_specs, out_specs=out_specs, check_vma=False)
```

```python
import functools

import jax
import jax.numpy as jnp
from jax import lax
from jax.experimental import pallas as pl
from jax.experimental.pallas import tpu as pltpu
from jax.sharding import PartitionSpec as P

F32 = jnp.float32
BF16 = jnp.bfloat16


def norm_parts(source, gain):
    wide = source.astype(jnp.float32)
    centred = wide - jnp.mean(wide, axis=-1, keepdims=True)
    scale_inv = lax.rsqrt(jnp.mean(centred * centred, axis=-1, keepdims=True) + 1e-06)
    x_hat = centred * scale_inv
    return (x_hat, scale_inv, (x_hat * gain).astype(jnp.bfloat16))


def norm_back(grad_n, x_hat, scale_inv, gain):
    scaled = grad_n * gain
    return scale_inv * (
        scaled
        - jnp.mean(scaled, axis=-1, keepdims=True)
        - x_hat * jnp.mean(scaled * x_hat, axis=-1, keepdims=True)
    )


def probabilities(normalized_queries, normalized_keys, same_image, scale_factor):
    scores = (
        jnp.einsum(
            "krt,irt->rki", normalized_queries, normalized_keys, preferred_element_type=jnp.float32
        )
        * scale_factor
    )
    scores = jnp.where(same_image[None], scores, -1e30)
    row_top = jnp.max(scores, axis=-1, keepdims=True)
    exp_terms = jnp.exp(scores - row_top)
    return exp_terms / jnp.sum(exp_terms, axis=-1, keepdims=True)


def local_any(queries, keys, values, image_ids, q_gain, k_gain, w_out, grad_y):
    head_dim = q_gain.shape[0]
    tok_rows = queries.shape[0]
    heads_all = queries.shape[1] // head_dim
    scale_factor = head_dim ** (-0.5)
    q_patch = queries.reshape(tok_rows, heads_all, head_dim)
    k_patch = keys.reshape(tok_rows, heads_all, head_dim)
    v_patch = values.reshape(tok_rows, heads_all, head_dim)
    q_local, k_local, value_shard = (
        lax.all_to_all(q_patch, "seq", split_axis=1, concat_axis=0, tiled=True),
        lax.all_to_all(k_patch, "seq", split_axis=1, concat_axis=0, tiled=True),
        lax.all_to_all(v_patch, "seq", split_axis=1, concat_axis=0, tiled=True),
    )
    seq_length = q_local.shape[0]
    local_heads = q_local.shape[1]
    image_row = image_ids[0]
    same_image = image_row[:, None] == image_row[None, :]
    q_hat, q_inv, normalized_queries = norm_parts(q_local, q_gain)
    k_hat, k_inv, normalized_keys = norm_parts(k_local, k_gain)
    prob_rows = probabilities(normalized_queries, normalized_keys, same_image, scale_factor)
    probs_reduced_precision = prob_rows.astype(jnp.bfloat16)
    attended = jnp.einsum(
        "tgi,itp->gtp", probs_reduced_precision, value_shard, preferred_element_type=jnp.float32
    ).astype(jnp.bfloat16)
    attended_flat = attended.reshape(seq_length, local_heads * head_dim)
    partial_g = jnp.einsum(
        "ld,cd->lc",
        grad_y,
        lax.all_gather(w_out, "fsdp", axis=0, tiled=True),
        preferred_element_type=jnp.float32,
    )
    grad_sum = lax.psum_scatter(
        partial_g.astype(jnp.bfloat16), "seq", scatter_dimension=1, tiled=True
    )
    attention_gradient = grad_sum.reshape(seq_length, local_heads, head_dim)
    grad_values = jnp.einsum(
        "jpw,pjy->wjy",
        probs_reduced_precision,
        attention_gradient,
        preferred_element_type=jnp.float32,
    ).astype(jnp.bfloat16)
    probability_gradient = jnp.einsum(
        "krt,irt->rki", attention_gradient, value_shard, preferred_element_type=jnp.float32
    )
    row_delta = jnp.sum(prob_rows * probability_gradient, axis=-1, keepdims=True)
    score_gradient = (prob_rows * (probability_gradient - row_delta) * scale_factor).astype(
        jnp.bfloat16
    )
    normed_query_gradient = jnp.einsum(
        "tgi,itp->gtp", score_gradient, normalized_keys, preferred_element_type=jnp.float32
    )
    normed_key_gradient = jnp.einsum(
        "jpw,pjy->wjy", score_gradient, normalized_queries, preferred_element_type=jnp.float32
    )
    grad_queries = norm_back(normed_query_gradient, q_hat, q_inv, q_gain).astype(jnp.bfloat16)
    grad_keys = norm_back(normed_key_gradient, k_hat, k_inv, k_gain).astype(jnp.bfloat16)
    partial_w = jnp.einsum(
        "lc,ld->cd",
        lax.all_gather(attended_flat, "seq", axis=1, tiled=True),
        grad_y,
        preferred_element_type=jnp.float32,
    )
    summed = lax.psum_scatter(partial_w, "fsdp", scatter_dimension=0, tiled=True)
    grad_w = summed * seq_length ** (-0.5)
    return (grad_queries, grad_keys, grad_values, grad_w)


def dot_nt(a, b):
    return lax.dot_general(a, b, (((1,), (1,)), ((), ())), preferred_element_type=F32)


def dot_tn(a, b):
    return lax.dot_general(a, b, (((0,), (0,)), ((), ())), preferred_element_type=F32)


def dot_nn(a, b):
    return jnp.dot(a, b, preferred_element_type=F32)


def assemble(first, own, came):
    return jnp.concatenate([jnp.where(first, own, came), jnp.where(first, came, own)], axis=0)


def head_probs(q, k, qg, kg, same, scale):
    q_hat, q_inv, qn = norm_parts(q, qg)
    k_hat, k_inv, kn = norm_parts(k, kg)
    scores = jnp.where(same, dot_nt(qn, kn) * scale, -1e30)
    exp_terms = jnp.exp(scores - jnp.max(scores, axis=-1, keepdims=True))
    probs = exp_terms / jnp.sum(exp_terms, axis=-1, keepdims=True)
    return probs, q_hat, q_inv, qn, k_hat, k_inv, kn


def probabilities_kernel(per, dim, place, q_ref, k_ref, came_ref, row_ref, col_ref, qg_ref, kg_ref, p_ref, hat_ref, inv_ref, low_ref, p_low_ref):
    same = col_ref[...] == row_ref[...]
    first = place[0] == 0
    for h in range(per):
        cols = slice(h * dim, (h + 1) * dim)
        q, k = (assemble(first, ref[:, cols], came_ref[n, :, cols]) for n, ref in enumerate((q_ref, k_ref)))
        probs, *parts = head_probs(q, k, qg_ref[...], kg_ref[...], same, dim**-0.5)
        p_ref[h] = probs
        p_low_ref[h] = probs.astype(BF16)
        for n, (hat, inv, normed) in enumerate((parts[:3], parts[3:])):
            hat_ref[n, h] = hat
            inv_ref[n, h] = jnp.broadcast_to(inv, hat.shape)
            low_ref[n, h] = normed


def attended_kernel(per, dim, place, p_low_ref, v_ref, came_ref, even_ref, odd_ref, whole_ref):
    first = place[0] == 0
    done = []
    for h in range(per):
        cols = slice(h * dim, (h + 1) * dim)
        v = assemble(first, v_ref[:, cols], came_ref[:, cols])
        whole_ref[h] = v
        done.append(dot_nn(p_low_ref[h], v).T.astype(BF16))
    att = jnp.concatenate(done, axis=0)
    half = att.shape[0] // 2
    straight = (place[1] & 1) == 0
    low, high = att[:half], att[half:]
    even_ref[0] = jnp.where(straight, low, high)
    odd_ref[0] = jnp.where(straight, high, low)


def backward_kernel(per, dim, n_into, place, p_ref, hat_ref, inv_ref, low_ref, v_ref, d_ref, qg_ref, kg_ref, *rest):
    gq_ref, gk_ref, gv_ref = rest[n_into:]
    scale = dim**-0.5
    straight = (place[1] & 1) == 0
    one, two = d_ref[0, 0], d_ref[0, 1]
    grad = jnp.concatenate([jnp.where(straight, one, two), jnp.where(straight, two, one)], axis=0)
    qg, kg = qg_ref[...], kg_ref[...]
    for h in range(per):
        probs, qn, kn, v = p_ref[h], low_ref[0, h], low_ref[1, h], v_ref[h]
        d = grad[h * dim : (h + 1) * dim].T
        gp = dot_nt(d, v)
        gv_ref[h] = dot_tn(probs.astype(BF16), d).astype(BF16)
        delta = jnp.sum(probs * gp, axis=-1, keepdims=True)
        gs = (probs * (gp - delta) * scale).astype(BF16)
        gq_ref[h] = norm_back(dot_nn(gs, kn), hat_ref[0, h], inv_ref[0, h], qg).astype(BF16)
        gk_ref[h] = norm_back(dot_tn(gs, qn), hat_ref[1, h], inv_ref[1, h], kg).astype(BF16)


def whole(shape):
    return pl.BlockSpec(shape, lambda *_: (0,) * len(shape))


def pair_index(i, p):
    return i ^ (p[1] >> 1) ^ (p[2] << 1)


def own_heads(rows, wide):
    return pl.BlockSpec((rows, wide), lambda i, p: (0, p[0] * 4 + i))


def in_hbm(a):
    return pltpu.with_memory_space_constraint(a, pltpu.HBM)


def attention_probabilities(place, queries, keys, came, row, col, qg, kg):
    dim = qg.shape[1]
    half_tokens, heads = came.shape[1], came.shape[2] // dim
    tokens, per = 2 * half_tokens, heads // 4
    wide = per * dim

    def saved(n, dtype):
        spec = pl.BlockSpec((n, per, tokens, dim), lambda i, p: (0, i, 0, 0))
        return spec, pltpu.HBM((n, heads, tokens, dim), dtype)

    square, probs = pl.BlockSpec((per, tokens, tokens), lambda i, p: (i, 0, 0)), (heads, tokens, tokens)
    specs, shapes = zip(
        (square, pltpu.HBM(probs, F32)),
        saved(2, F32),
        saved(2, F32),
        saved(2, BF16),
        (square, jax.ShapeDtypeStruct(probs, BF16)),
    )
    *saved, low = pl.pallas_call(
        functools.partial(probabilities_kernel, per, dim),
        grid_spec=pltpu.PrefetchScalarGridSpec(
            num_scalar_prefetch=1,
            grid=(4,),
            in_specs=[own_heads(half_tokens, wide)] * 2
            + [pl.BlockSpec((2, half_tokens, wide), lambda i, p: (0, 0, i))]
            + [whole((1, tokens)), whole((tokens, 1)), whole((1, dim)), whole((1, dim))],
            out_specs=specs,
        ),
        out_shape=shapes,
        compiler_params=pltpu.CompilerParams(vmem_limit_bytes=16 << 20),
        cost_estimate=pl.CostEstimate(flops=1000, bytes_accessed=1000, transcendentals=0),
        name="attention_probabilities",
    )(place, in_hbm(queries), in_hbm(keys), came, row, col, qg, kg)
    return saved, low


def attention_attended(place, low, values, came, dim):
    half_tokens, heads = came.shape[0], low.shape[0]
    tokens, per = 2 * half_tokens, heads // 4
    rows, wide = per * dim // 2, per * dim
    out = pl.BlockSpec((1, rows, tokens), lambda i, p: (pair_index(i, p), 0, 0))
    return pl.pallas_call(
        functools.partial(attended_kernel, per, dim),
        grid_spec=pltpu.PrefetchScalarGridSpec(
            num_scalar_prefetch=1,
            grid=(4,),
            in_specs=[pl.BlockSpec((per, tokens, tokens), lambda i, p: (i, 0, 0))]
            + [own_heads(half_tokens, wide), pl.BlockSpec((half_tokens, wide), lambda i, p: (0, i))],
            out_specs=[out, out, pl.BlockSpec((per, tokens, dim), lambda i, p: (i, 0, 0))],
        ),
        out_shape=[jax.ShapeDtypeStruct((4, rows, tokens), BF16)] * 2 + [pltpu.HBM((heads, tokens, dim), BF16)],
        compiler_params=pltpu.CompilerParams(vmem_limit_bytes=16 << 20),
        cost_estimate=pl.CostEstimate(flops=1000, bytes_accessed=1000, transcendentals=0),
        name="attention_attended",
    )(place, low, in_hbm(values), came)


def attention_backward(place, first, pairs, saved, grads, qg, kg, into=()):
    heads, tokens = saved[0].shape[:2]
    dim, per, rows = qg.shape[1], heads // 4, grads.shape[2]

    def index(i, p):
        return pair_index(i + first, p)

    def block(n):
        return pl.BlockSpec((n, per, tokens, dim), lambda i, p: (0, index(i, p), 0, 0))

    return pl.pallas_call(
        functools.partial(backward_kernel, per, dim, len(into)),
        grid_spec=pltpu.PrefetchScalarGridSpec(
            num_scalar_prefetch=1,
            grid=(pairs,),
            in_specs=[pl.BlockSpec((per, tokens, tokens), lambda i, p: (index(i, p), 0, 0)), block(2), block(2), block(2)]
            + [pl.BlockSpec((per, tokens, dim), lambda i, p: (index(i, p), 0, 0))]
            + [pl.BlockSpec((1, 2, rows, tokens), lambda i, p: (i, 0, 0, 0))]
            + [whole((1, dim)), whole((1, dim))]
            + [pl.BlockSpec(memory_space=pl.ANY)] * len(into),
            out_specs=[pl.BlockSpec((per, tokens, dim), lambda i, p: (index(i, p), 0, 0))] * 3,
        ),
        out_shape=[pltpu.HBM((heads, tokens, dim), BF16)] * 3,
        input_output_aliases={9 + n: n for n in range(len(into))},
        compiler_params=pltpu.CompilerParams(vmem_limit_bytes=16 << 20),
        cost_estimate=pl.CostEstimate(flops=1000, bytes_accessed=1000, transcendentals=0),
        name="attention_backward",
    )(place, *saved, grads, qg, kg, *into)


VECTOR = pl.BlockSpec(memory_space=pltpu.VMEM)
SCALAR = pl.BlockSpec(memory_space=pltpu.SMEM)


def hold_kernel(*refs):
    n = len(refs) // 2
    for source, held in zip(refs[:n], refs[n:]):
        held[...] = source[...]


def hold(*arrays, steps=4):
    specs = [pl.BlockSpec((a.shape[0] // steps, a.shape[1]), lambda i: (i, 0)) for a in arrays]
    return pl.pallas_call(
        hold_kernel,
        grid=(steps,),
        in_specs=specs,
        out_specs=specs,
        out_shape=[pltpu.VMEM(a.shape, a.dtype) for a in arrays],
        compiler_params=pltpu.CompilerParams(vmem_limit_bytes=16 << 20),
        cost_estimate=pl.CostEstimate(flops=1000, bytes_accessed=1000, transcendentals=0),
        name="hold",
    )(*arrays)


def choose_kernel(place, mid_ref, end_ref, far_ref):
    far_ref[...] = jnp.where(place[3] == 1, mid_ref[...], end_ref[...])


def choose(place, mid, end):
    return pl.pallas_call(
        choose_kernel,
        in_specs=[SCALAR, VECTOR, VECTOR],
        out_specs=VECTOR,
        out_shape=pltpu.VMEM(mid.shape, mid.dtype),
        compiler_params=pltpu.CompilerParams(vmem_limit_bytes=4 << 20),
        cost_estimate=pl.CostEstimate(flops=10**10, bytes_accessed=1000, transcendentals=0),
        name="choose",
    )(place, mid, end)


def products_kernel(n, parts, place, w_ref, far_ref, *refs):
    g_refs, (keep_ref, send_ref, both_ref) = refs[:-3], refs[-3:]
    rows = w_ref.shape[0]
    flip = place[2] == 1
    for first, depth, _ in parts:
        cols = slice(first, first + depth)
        own, far = w_ref[:, cols], far_ref[:, cols]
        both_ref[:rows, cols] = jnp.where(flip, far, own)
        both_ref[rows:, cols] = jnp.where(flip, own, far)
    for j in range(n):
        total = None
        for c, (first, depth, starts) in enumerate(parts):
            start = starts[j]
            term = dot_nt(both_ref[:, first : first + depth], g_refs[c * n + j][:, start : start + depth])
            total = term if total is None else total + term
        keep_ref[j] = total[:rows].astype(BF16)
        send_ref[j] = total[rows:].astype(BF16)


def gradient_products(place, w, far, parts):
    rows, depth = w.shape
    n, tokens = len(parts[0][0]), parts[0][0][0].shape[0]
    blocks = [a for part in parts for a in part[0]]
    return pl.pallas_call(
        functools.partial(products_kernel, n, [(first, wide, starts) for _, starts, first, wide in parts]),
        in_specs=[SCALAR] + [VECTOR] * (2 + len(blocks)),
        out_specs=[VECTOR] * 2,
        out_shape=[jax.ShapeDtypeStruct((n, rows, tokens), BF16)] * 2,
        scratch_shapes=[pltpu.VMEM((2 * rows, depth), BF16)],
        compiler_params=pltpu.CompilerParams(vmem_limit_bytes=16 << 20),
        cost_estimate=pl.CostEstimate(flops=1000, bytes_accessed=1000, transcendentals=0),
        name="gradient_products",
    )(place, w, far, *blocks)


def weight_kernel(n, starts, parts, place, own_ref, other_ref, *refs):
    g_refs, far_refs, kept_ref, both_ref = refs[:n], refs[n:-2], refs[-2], refs[-1]
    rows, tokens = own_ref.shape[1:]
    flip = place[2] == 1
    for j in range(n):
        cols = slice(j * tokens, (j + 1) * tokens)
        both_ref[:rows, cols] = jnp.where(flip, own_ref[j], other_ref[j])
        both_ref[rows:, cols] = jnp.where(flip, other_ref[j], own_ref[j])
    first = 0
    for part, far_ref in zip(parts, far_refs):
        blocks = [g_ref[:, start + first : start + first + part] for g_ref, start in zip(g_refs, starts)]
        total = dot_nn(both_ref[...], jnp.concatenate(blocks, axis=0))
        far_ref[...] = total[:rows].astype(BF16)
        kept_ref[:, first : first + part] = total[rows:]
        first += part


def weight_terms(place, own, other, half, parts, flops):
    n, rows, tokens = own.shape
    depth = sum(parts)
    return pl.pallas_call(
        functools.partial(weight_kernel, n, half[1], parts),
        in_specs=[SCALAR] + [VECTOR] * (2 + n),
        out_specs=[VECTOR] * (len(parts) + 1),
        out_shape=[jax.ShapeDtypeStruct((rows, part), BF16) for part in parts]
        + [jax.ShapeDtypeStruct((rows, depth), F32)],
        scratch_shapes=[pltpu.VMEM((2 * rows, n * tokens), BF16)],
        compiler_params=pltpu.CompilerParams(vmem_limit_bytes=16 << 20),
        cost_estimate=pl.CostEstimate(flops=flops, bytes_accessed=1000, transcendentals=0),
        name="weight_terms",
    )(place, own, other, *half[0])


def finish_kernel(scale, n_into, kept_ref, *refs):
    far_refs, out_ref = refs[: len(refs) - 1 - n_into], refs[-1]
    first = 0
    for ref in far_refs:
        cols = slice(first, first + ref.shape[1])
        out_ref[:, cols] = (kept_ref[:, cols] + ref[...].astype(F32)) * scale
        first = cols.stop


def finish(kept, far, scale, first, depth, flops, into=()):
    rows, wide = kept.shape
    tile, place = rows // 2, first // wide

    def block(a):
        return pl.BlockSpec((tile, a.shape[1]), lambda i: (i, 0))

    return pl.pallas_call(
        functools.partial(finish_kernel, scale, len(into)),
        grid=(rows // tile,),
        in_specs=[block(a) for a in (kept, *far)] + [pl.BlockSpec(memory_space=pl.ANY)] * len(into),
        out_specs=pl.BlockSpec((tile, wide), lambda i: (i, place)),
        out_shape=pltpu.HBM((rows, depth), F32),
        input_output_aliases={1 + len(far): 0} if into else {},
        compiler_params=pltpu.CompilerParams(vmem_limit_bytes=16 << 20),
        cost_estimate=pl.CostEstimate(flops=flops, bytes_accessed=1000, transcendentals=0),
        name="finish",
    )(kept, *far, *into)


def xor(k):
    return [(j, j ^ k) for j in range(16)]


CORE, CROSS, PLANE = xor(1), xor(2), xor(4)
FAR = xor(12)
MIDDLE = [pair for pair in FAR if 4 <= pair[0] < 12]
ENDS = [pair for pair in FAR if not 4 <= pair[0] < 12]


def move(a, perm, name):
    with jax.named_scope(name):
        return lax.ppermute(a, "fsdp", perm)


def swap(a, name):
    with jax.named_scope(name):
        return lax.ppermute(a, "seq", [(0, 1), (1, 0)])


def local_grid(queries, keys, values, image_ids, q_gain, k_gain, w_out, grad_y):
    y = lax.axis_index("seq")
    f = lax.axis_index("fsdp")
    middle = (f >> 3) ^ ((f >> 2) & 1)
    place = jnp.stack([y, f & 7, (f >> 3) ^ y, middle]).astype(jnp.int32)
    dim = q_gain.shape[0]
    tokens = image_ids.shape[1]
    half = queries.shape[1] // 2
    row, col = image_ids, image_ids.reshape(tokens, 1)
    qg, kg = q_gain.reshape(1, dim), k_gain.reshape(1, dim)
    barrier = lax.optimization_barrier
    width = grad_y.shape[1]
    cut = 2 * width // 3

    width = grad_y.shape[1]
    cut = 2 * width // 3
    barrier = lax.optimization_barrier

    theirs = [lax.dynamic_slice_in_dim(a, (1 - y) * half, half, axis=1) for a in (queries, keys, values)]
    send, gy, w_own = barrier((jnp.stack(theirs[:2]), grad_y, w_out))
    came = swap(send, "qk_seq")
    came_v = swap(theirs[2], "v_seq")
    g2 = move(gy, CROSS, "gy_cross")
    g4 = move(gy, PLANE, "gy_plane")
    w_mid = move(w_own, MIDDLE, "w_middle")
    saved, low = attention_probabilities(place, queries, keys, came, row, col, qg, kg)
    even, odd, v_all = attention_attended(place, low, values, came_v, dim)
    saved.append(v_all)
    odd = move(odd, CORE, "att_core")
    even, odd, g2, g4, gy, w_own, w_mid = barrier((even, odd, g2, g4, gy, w_own, w_mid))
    own = [jnp.stack([even[j], odd[j]]) for j in range(4)]
    other = [swap(own[0], "att_seq")]
    own = [own[0]] + [move(own[j], xor(2 * j), "att_group") for j in (1, 2, 3)]
    g4a, g4b = g4[:, :cut], g4[:, cut:]
    g1 = move(gy, CORE, "gy_core")
    own, other, g4, g4a, g4b, g2, g1, gy = barrier((own, other, g4, g4a, g4b, g2, g1, gy))
    other.append(swap(jnp.concatenate(own[1:]), "att_seq"))
    g6a = move(g4a, CROSS, "gy_plane_cross_a")
    w_far = choose(place, w_mid, move(w_own, ENDS, "w_ends"))
    g3, g5 = (move(g, CORE, "gy_core") for g in (g2, g4))
    gy, w_held = hold(gy, w_out)
    other[1], gy, w_held = barrier((other[1], gy, w_held))
    own, other = jnp.concatenate(own), jnp.concatenate(other)
    other, g6a = barrier((other, g6a))
    g7a = move(g6a, CORE, "gy_core")
    blocks_a = [gy, g1, g2, g3, g4, g5, g6a, g7a]
    *sent, kept_a = weight_terms(place, own, other, (blocks_a, (0,) * 8), (cut // 2,), 1000)
    own, other, g6a, g7a, g3, g5, g4b, w_far, sent, kept_a = barrier(
        (own, other, g6a, g7a, g3, g5, g4b, w_far, sent, kept_a)
    )
    g6b = move(g4b, CROSS, "gy_plane_cross_b")
    far = [move(sent[0], FAR, "grad_w_far")]
    weights = (w_held, w_far)
    near = (gy, g2, g1, g3)
    keep0, send0 = gradient_products(
        place, *weights, [(near, (start,) * 4, start, depth) for start, depth in ((0, cut), (cut, width - cut))]
    )
    came0 = swap(send0, "products_seq")
    own_c, keep0 = barrier((own, keep0))
    *sent, kept_c = weight_terms(place, own_c, other, (blocks_a, (cut // 2,) * 8), (cut // 2,), 1000)
    g6b, far, sent, kept_c, keep0, came0 = barrier((g6b, far, sent, kept_c, keep0, came0))
    g7b = move(g6b, CORE, "gy_core")
    far.append(move(sent[0], FAR, "grad_w_far"))
    keep1, send1 = gradient_products(
        place,
        *weights,
        [((g4, g6a, g5, g7a), (0,) * 4, 0, cut), ((g4, g6b, g5, g7b), (cut, 0, cut, 0), cut, width - cut)],
    )
    came1 = swap(send1, "products_seq")
    came0, keep1, blocks_b = barrier((came0, keep1, [gy, g1, g2, g3, g4, g5, g6b, g7b]))
    summed0 = (keep0.astype(F32) + came0.astype(F32)).astype(BF16)
    odd = move(summed0[2:], CORE, "products_core")
    near = [jnp.stack([summed0[j], odd[j]]) for j in range(2)]
    near[1] = move(near[1], xor(2), "products_group")
    starts_b = (cut,) * 6 + (0,) * 2
    *sent, kept_b = weight_terms(place, own, other, (blocks_b, starts_b), ((width - cut) // 2,) * 2, 1000)
    far, near, keep1, came1, sent, kept_b = barrier((far, near, keep1, came1, sent, kept_b))
    summed1 = (keep1.astype(F32) + came1.astype(F32)).astype(BF16)
    odd = move(summed1[2:], CORE, "products_core")
    next_plane = [jnp.stack([summed1[j], odd[j]]) for j in range(2)]
    next_plane = [move(next_plane[j], xor(4 + 2 * j), "products_group") for j in range(2)]
    last = [move(part, FAR, "grad_w_far") for part in sent]
    scale = tokens ** (-0.5)
    grad_w = finish(kept_a, far[:1], scale, 0, width, 1000)
    grad_w = finish(kept_c, far[1:], scale, cut // 2, width, 1000, (grad_w,))
    near, grad_w = barrier((near, grad_w))
    grads = attention_backward(place, 0, 2, saved, jnp.stack(near), qg, kg)
    grads = attention_backward(place, 2, 2, saved, jnp.stack(next_plane), qg, kg, tuple(grads))

    grad_w = finish(kept_b, last, scale, cut, width, 1000, (grad_w,))
    return (*(g.transpose(1, 0, 2) for g in grads), grad_w)


def solution(mesh):
    in_specs = (
        P(("fsdp", "seq"), None),
        P(("fsdp", "seq"), None),
        P(("fsdp", "seq"), None),
        P("fsdp", None),
        P(),
        P(),
        P("fsdp", "seq"),
        P("fsdp", "seq"),
    )
    out_specs = (
        P("fsdp", "seq", None),
        P("fsdp", "seq", None),
        P("fsdp", "seq", None),
        P("fsdp", "seq"),
    )
    grid = mesh.shape["fsdp"] == 16 and mesh.shape["seq"] == 2
    local = local_grid if grid else local_any
    return jax.shard_map(local, mesh=mesh, in_specs=in_specs, out_specs=out_specs, check_vma=False)
```
